32 devices in a mesh: chan: 8 (over z, x), tile: 4 (over y, core).
Axes of the slice: x: 2, y: 2, z: 4, core: 2. Of those that a mesh axis runs over, the one named last changes fastest.
Arguments:
- voltage: float32 [2, 64, 512, 1024], P(None, 'tile', 'chan'), may hold values from -6 to 6
- fir_taps: float32 [4, 1024], replicated, may hold values from -3 to 3
- tile_slot: int32 [10], replicated, may hold values from 0 to 11, as said below
- tile_blocks: int32 [10, 2], replicated, may hold values from 0 to 3, as said below
Outputs:
- visibility: float32 [12, 1024, 2, 128, 128], P('tile', 'chan')
The draws below stay inside these ranges and needn't reach their ends.
Inputs may be any that keep to these rules, and one draw needn't show every extreme that they name: `tile_slot`: the values are distinct; slot g belongs to device g // 3 of the tile axis. Every device of the tile axis holds at least one tile and at most 3, some exactly 3, and a device's tiles fill its lowest slots. `tile_blocks`: the unordered pairs of the rows are the 10 pairs of blocks p <= q, each once; a row may name its pair in either order.
All inputs are finite; a program needn't handle non-finite values.
Results may differ from the reference program's by a relative error of at most 0.0001.
Values sent between devices are 32-bit elements; how exact they have to be, the bound alone decides.
No kernel may reach another device: no remote copies, remote signals or barrier semaphores. Data moves between devices by JAX's collectives and lax.ppermute only.
A program may use at most 256 MiB of HBM per device.

```python
import jax
import jax.numpy as jnp
import numpy as np
from jax import lax

CHANNELS = 1024
BLOCK = 128
NB = 4
TAPS = 4
SPECTRA = 64
INPUTS = 512
TRI = 10
SLOTS = 3
SLOTS_ALL = 12


def draw_tile_slot(key, part):
    devices = SLOTS_ALL // SLOTS
    order = jax.random.permutation(jax.random.fold_in(key, 11), devices)
    ranks = jnp.arange(TRI, dtype=jnp.int32)
    return (order[ranks % devices] * SLOTS + ranks // devices).astype(jnp.int32)


def draw_tile_blocks(key, part):
    row_block, col_block = np.triu_indices(NB)
    block_pairs = jnp.stack([jnp.asarray(row_block, jnp.int32), jnp.asarray(col_block, jnp.int32)], axis=1)
    chosen = block_pairs[jax.random.permutation(jax.random.fold_in(key, 23), TRI)]
    swapped = jax.random.randint(jax.random.fold_in(key, 37), (TRI, 1), 0, 2)
    return jnp.where(swapped == 1, chosen[:, ::-1], chosen).astype(jnp.int32)


def shard_levels(rng, shape, cuts, low, high):
    def one(position, blocks):
        heights = jax.random.uniform(jax.random.fold_in(jax.random.fold_in(rng, 6), position), (blocks,), jnp.float32, low / len(cuts), high / len(cuts))
        return jnp.repeat(jnp.exp(heights), shape[position] // blocks).reshape((-1,) + (1,) * (len(shape) - position - 1))

    level = one(*cuts[0])
    for cut in cuts[1:]:
        level = level * one(*cut)
    return level


def scatter_about(key, shape, spread, reach, split=(), kind=jnp.bfloat16):
    entries = spread * jax.random.normal(key, shape, jnp.float32)
    if split:
        entries = entries * shard_levels(key, shape, split, -0.22, 0.18)
    return jnp.clip(entries, -reach, reach).astype(kind)


def setup_inputs(seed: int = 0) -> dict:
    streams_of = jax.random.split(jax.random.key(seed), 5)
    voltage = scatter_about(streams_of[0], (2, SPECTRA, INPUTS, CHANNELS), 1.0, 6.0, ((1, 4), (2, 8)), jnp.float32)
    fir_taps = scatter_about(streams_of[1], (TAPS, CHANNELS), 0.5, 3.0, (), jnp.float32)
    tile_slot = draw_tile_slot(jax.random.fold_in(streams_of[4], 71), 0)
    tile_blocks = draw_tile_blocks(jax.random.fold_in(streams_of[4], 71), 0)
    return {"voltage": voltage, "fir_taps": fir_taps, "tile_slot": tile_slot, "tile_blocks": tile_blocks}


def product(left_rows, right_rows):
    return jnp.einsum("csi,csj->cij", left_rows, right_rows, precision=lax.Precision.HIGHEST)


def reference(voltage, fir_taps, tile_slot, tile_blocks):
    tap_count = fir_taps.shape[0]
    padded = jnp.concatenate([voltage, jnp.zeros((2, tap_count - 1, INPUTS, CHANNELS), jnp.float32)], axis=1)
    filtered = jnp.zeros((2, SPECTRA, INPUTS, CHANNELS), jnp.float32)
    for tap_index in range(tap_count):
        filtered = filtered + fir_taps[tap_index][None, None, None, :] * padded[:, tap_index:tap_index + SPECTRA]
    spectrum = jnp.fft.fft(filtered[0] + 1j * filtered[1], axis=-1, norm="ortho")
    real_rows = jnp.transpose(jnp.real(spectrum), (2, 0, 1))
    imag_rows = jnp.transpose(jnp.imag(spectrum), (2, 0, 1))

    def place_tile(tile_index, visibility):
        row_block = tile_blocks[tile_index, 0]
        col_block = tile_blocks[tile_index, 1]
        left_real = lax.dynamic_slice_in_dim(real_rows, row_block * BLOCK, BLOCK, 2)
        left_imag = lax.dynamic_slice_in_dim(imag_rows, row_block * BLOCK, BLOCK, 2)
        right_real = lax.dynamic_slice_in_dim(real_rows, col_block * BLOCK, BLOCK, 2)
        right_imag = lax.dynamic_slice_in_dim(imag_rows, col_block * BLOCK, BLOCK, 2)
        real_vis = product(left_real, right_real) + product(left_imag, right_imag)
        imag_vis = product(left_imag, right_real) - product(left_real, right_imag)
        update = (jnp.stack([real_vis, imag_vis], axis=1) / SPECTRA)[None]
        zero_index = jnp.zeros((), jnp.int32)
        return lax.dynamic_update_slice(visibility, update, (tile_slot[tile_index], zero_index, zero_index, zero_index, zero_index))

    initial = jnp.zeros((SLOTS_ALL, CHANNELS, 2, BLOCK, BLOCK), jnp.float32)
    return lax.fori_loop(0, TRI, place_tile, initial)
```

```python
import functools
import math

import jax
import jax.numpy as jnp
import numpy as np
from jax import lax
from jax.experimental import pallas as pl
from jax.experimental.pallas import tpu as pltpu
from jax.sharding import PartitionSpec as P

BLOCK = 128
PARTS = 2
VMEM_BYTES = 56 * 1024 * 1024
BF16 = jnp.bfloat16
F32 = jnp.float32


def shifted(value, axis, steps):
    count = lax.axis_size(axis)
    initial, last = (max(0, -steps), min(count, count - steps))
    return lax.ppermute(value, axis, [(source, source + steps) for source in range(initial, last)])


def swapped(value, axis, mask):
    count = lax.axis_size(axis)
    return lax.ppermute(value, axis, [(source, source ^ mask) for source in range(count)])


def params():
    return pltpu.CompilerParams(vmem_limit_bytes=VMEM_BYTES)


def split(value):
    high = value.astype(BF16)
    return high, (value - high.astype(F32)).astype(BF16)


def filter_frames(voltage, fir_taps):
    tap_count = fir_taps.shape[0]
    frames = voltage.shape[1]
    history = shifted(voltage[:, : tap_count - 1], "tile", -1)
    extended = jnp.concatenate([voltage, history], axis=1)
    filtered = jnp.zeros(voltage.shape, jnp.float32)
    for tap_index in range(tap_count):
        filtered = (
            filtered
            + fir_taps[tap_index][None, None, None, :] * extended[:, tap_index : tap_index + frames]
        )
    return filtered


def transform(filtered):
    channel_count = filtered.shape[3]
    row_count = filtered.shape[1] * filtered.shape[2]
    position = lax.broadcasted_iota(jnp.int32, (channel_count, channel_count), 0)
    frequency = lax.broadcasted_iota(jnp.int32, (channel_count, channel_count), 1)
    phase_angle = (position * frequency % channel_count).astype(jnp.float32) * (
        2.0 * math.pi / channel_count
    )
    factor = 1.0 / math.sqrt(channel_count)
    cosine = jnp.cos(phase_angle) * factor
    sine_table = jnp.sin(phase_angle) * factor
    samples = filtered.reshape(2 * row_count, channel_count)
    cos_part = jnp.dot(
        cosine, samples.T, precision=lax.Precision.HIGHEST, preferred_element_type=jnp.float32
    )
    sin_part = jnp.dot(
        sine_table, samples.T, precision=lax.Precision.HIGHEST, preferred_element_type=jnp.float32
    )
    real_part = cos_part[:, :row_count] + sin_part[:, row_count:]
    imag_part = cos_part[:, row_count:] - sin_part[:, :row_count]
    joined = jnp.concatenate([real_part, imag_part], axis=1)
    return joined.reshape(channel_count, 2, filtered.shape[1], filtered.shape[2])


def tile_product(gathered, row_block, col_block, block_width):
    left_block = lax.dynamic_slice_in_dim(gathered, row_block * block_width, block_width, 3)
    right_block = lax.dynamic_slice_in_dim(gathered, col_block * block_width, block_width, 3)
    channel_count = gathered.shape[0]
    depth = 2 * gathered.shape[2]
    left_real = left_block.reshape(channel_count, depth, block_width)
    left_imag = jnp.concatenate([left_block[:, 1], -left_block[:, 0]], axis=1)
    left_both = jnp.concatenate([left_real, left_imag], axis=2)
    right_both = right_block.reshape(channel_count, depth, block_width)
    return jnp.einsum(
        "cki,ckj->cij",
        left_both,
        right_both,
        precision=lax.Precision.HIGHEST,
        preferred_element_type=jnp.float32,
    )


def own_slots(tile_slot, tile_blocks, slot_count):
    first_slot = lax.axis_index("tile") * slot_count
    row_blocks = []
    col_blocks = []
    present = []
    for slot_index in range(slot_count):
        matches = (tile_slot == first_slot + slot_index).astype(jnp.int32)
        row_blocks.append(jnp.sum(matches * tile_blocks[:, 0]))
        col_blocks.append(jnp.sum(matches * tile_blocks[:, 1]))
        present.append(jnp.sum(matches))
    return row_blocks, col_blocks, present


def generic_body(voltage, fir_taps, tile_slot, tile_blocks):
    spectra = transform(filter_frames(voltage, fir_taps))
    tile_count = tile_blocks.shape[0]
    tile_size = lax.axis_size("tile")
    slot_count = (tile_count + tile_size - 1) // tile_size
    turned = lax.all_to_all(spectra, "chan", split_axis=0, concat_axis=3, tiled=True)
    spectra_total = turned.shape[2] * tile_size
    row_blocks, col_blocks, present = own_slots(tile_slot, tile_blocks, slot_count)
    portion = lax.all_gather(turned, "tile", axis=2, tiled=True)
    summed = jnp.stack(
        [
            tile_product(portion, row_blocks[slot_index], col_blocks[slot_index], BLOCK)
            for slot_index in range(slot_count)
        ]
    )
    weights = jnp.stack(present).astype(F32)[:, None, None, None] / spectra_total
    return (summed * weights).reshape(slot_count, turned.shape[0], 2, BLOCK, BLOCK)


def fourier_table(channel_count, owners, scale):
    phase = np.outer(np.arange(channel_count), np.arange(channel_count)) % channel_count
    angle = phase * (2.0 * math.pi / channel_count)
    cosine = np.cos(angle) * scale
    sine = np.sin(angle) * scale
    both = np.stack(
        [np.concatenate([cosine, sine], 1), np.concatenate([-sine, cosine], 1)], 0
    ).reshape(2, owners, channel_count // owners, 2 * channel_count)
    both = both.transpose(1, 0, 2, 3).reshape(owners, -1, 2 * channel_count)
    return both.astype(np.float32)


def filter_kernel(voltage_ref, next_ref, taps_ref, high_ref, low_ref):
    tap_count, length = taps_ref.shape
    frames = voltage_ref.shape[1]
    for part in range(2):
        for frame in range(frames):
            total = None
            for tap in range(tap_count):
                at = frame + tap
                source = voltage_ref[part, at] if at < frames else next_ref[part, at - frames]
                term = source * taps_ref[pl.ds(tap, 1), :]
                total = term if total is None else total + term
            high, low = split(total)
            high_ref[frame, :, part * length : (part + 1) * length] = high
            low_ref[frame, :, part * length : (part + 1) * length] = low


def filtered_samples(voltage, following, fir_taps):
    _, frames, inputs, length = voltage.shape
    extra = following.shape[1]
    width = 16
    out = jax.ShapeDtypeStruct((frames, inputs, 2 * length), BF16)
    out_spec = pl.BlockSpec((frames, width, 2 * length), lambda i: (0, i, 0))
    return pl.pallas_call(
        filter_kernel,
        grid=(inputs // width,),
        in_specs=[
            pl.BlockSpec((2, frames, width, length), lambda i: (0, 0, i, 0)),
            pl.BlockSpec((2, extra, width, length), lambda i: (0, 0, i, 0)),
            pl.BlockSpec(fir_taps.shape, lambda i: (0, 0)),
        ],
        out_specs=[out_spec, out_spec],
        out_shape=[out, out],
        compiler_params=params(),
        cost_estimate=pl.CostEstimate(
            flops=8 * voltage.size, bytes_accessed=8 * voltage.size, transcendentals=0
        ),
        name="filter",
    )(voltage, following, fir_taps)


def dot_rows(left, right):
    return lax.dot_general(left, right, (((1,), (1,)), ((), ())), preferred_element_type=F32)


def transform_kernel(owner_ref, table_ref, xh_ref, xl_ref, *refs):
    out_refs, (th_ref, tl_ref) = refs[:-2], refs[-2:]

    @pl.when(pl.program_id(0) == 0)
    def _():
        th_ref[...], tl_ref[...] = split(table_ref[0])

    high = xh_ref[...]
    result = dot_rows(th_ref[...], high) + dot_rows(th_ref[...], xl_ref[...])
    result = result + dot_rows(tl_ref[...], high)
    channels = result.shape[0] // 2
    piece = channels // len(out_refs)
    for part in range(2):
        for index, out_ref in enumerate(out_refs):
            first = part * channels + index * piece
            for column in range(result.shape[1] // BLOCK):
                out_ref[part, column] = result[
                    first : first + piece, column * BLOCK : (column + 1) * BLOCK
                ]


def transformed(owner, table, samples, parts):
    rows, depth = samples[0].shape
    channels = table.shape[1] // 2
    piece = channels // parts
    step = min(256, rows)
    out = jax.ShapeDtypeStruct((2, rows // BLOCK, piece, BLOCK), F32)
    table_spec = pl.BlockSpec((1, 2 * channels, depth), lambda i, owner: (owner[0], 0, 0))
    row_spec = pl.BlockSpec((step, depth), lambda i, owner: (i, 0))
    return pl.pallas_call(
        transform_kernel,
        grid_spec=pltpu.PrefetchScalarGridSpec(
            num_scalar_prefetch=1,
            grid=(rows // step,),
            in_specs=[table_spec, row_spec, row_spec],
            out_specs=[
                pl.BlockSpec((2, step // BLOCK, piece, BLOCK), lambda i, owner: (0, i, 0, 0))
            ]
            * parts,
            scratch_shapes=[pltpu.VMEM((2 * channels, depth), BF16)] * 2,
        ),
        out_shape=[out] * parts,
        compiler_params=params(),
        cost_estimate=pl.CostEstimate(
            flops=3 * 2 * 2 * channels * depth * rows,
            bytes_accessed=4 * depth * (rows + 2 * channels) + 8 * channels * rows,
            transcendentals=0,
        ),
        name="transform",
    )(owner, table, *samples)


def merge_kernel(groups, piece, side_ref, near_ref, far_ref, out_ref):
    odd = side_ref[0] == 1
    lower = lax.broadcasted_iota(jnp.int32, (groups, BLOCK), 1) < BLOCK // 2
    for channel in range(piece):
        for part in range(2):
            rows = pl.ds(part * groups * piece + channel, groups, stride=piece)
            near = near_ref[rows, :]
            far = far_ref[rows, :]
            first = jnp.where(odd, far, near)
            second = jnp.where(odd, near, far)
            at = part * 2 * groups
            out_ref[channel, at : at + groups] = jnp.where(
                lower, first, pltpu.roll(second, BLOCK // 2, 1)
            )
            out_ref[channel, at + groups : at + 2 * groups] = jnp.where(
                lower, pltpu.roll(first, BLOCK // 2, 1), second
            )


def merged(side, near, far):
    _, groups, piece, lanes = near.shape
    flat = (2 * groups * piece, lanes)
    return pl.pallas_call(
        functools.partial(merge_kernel, groups, piece),
        in_specs=[
            pl.BlockSpec(memory_space=pltpu.SMEM),
            pl.BlockSpec(memory_space=pltpu.VMEM),
            pl.BlockSpec(memory_space=pltpu.VMEM),
        ],
        out_specs=pl.BlockSpec(memory_space=pltpu.VMEM),
        out_shape=jax.ShapeDtypeStruct((piece, 4 * groups, lanes), F32),
        compiler_params=params(),
        cost_estimate=pl.CostEstimate(
            flops=4 * near.size, bytes_accessed=16 * near.size, transcendentals=0
        ),
        name="merge",
    )(side, near.reshape(flat), far.reshape(flat))


def dot_columns(left, right):
    return lax.dot_general(left, right, (((0,), (0,)), ((), ())), preferred_element_type=F32)


def correlate_kernel(blocks, tiles, slots, place_ref, *refs):
    unit_refs = refs[: blocks * tiles]
    out_ref, high_ref, low_ref = refs[-3:]
    width = out_ref.shape[1]
    rows = unit_refs[0].shape[1] // 2
    half = tiles * rows
    for channel in range(width):
        for mask in range(blocks):
            block = place_ref[mask]
            for part in range(2):
                joined = jnp.concatenate(
                    [
                        unit_refs[tile * blocks + mask][channel, part * rows : (part + 1) * rows]
                        for tile in range(tiles)
                    ],
                    axis=0,
                )
                high, low = split(joined)
                high_ref[channel, block, part * half : (part + 1) * half] = high
                low_ref[channel, block, part * half : (part + 1) * half] = low
        for slot in range(slots):
            row = place_ref[blocks + slot]
            col = place_ref[blocks + slots + slot]
            weight = place_ref[blocks + 2 * slots + slot].astype(F32)
            row_high = high_ref[channel, row]
            row_low = low_ref[channel, row]
            col_high = high_ref[channel, col]
            col_low = low_ref[channel, col]
            turned_high = jnp.concatenate([-col_high[half:], col_high[:half]], axis=0)
            turned_low = jnp.concatenate([-col_low[half:], col_low[:half]], axis=0)
            right_high = jnp.concatenate([col_high, turned_high], axis=1)
            right_low = jnp.concatenate([col_low, turned_low], axis=1)
            value = dot_columns(
                jnp.concatenate([row_high, row_low], axis=0),
                jnp.concatenate([right_high, right_high], axis=0),
            ) + dot_columns(row_high, right_low)
            value = value * weight
            out_ref[slot, channel, 0] = value[:, :BLOCK]
            out_ref[slot, channel, 1] = value[:, BLOCK:]


def correlated(place, units, visibility, part, parts, channels, slots):
    tiles = len(units)
    blocks = len(units[0])
    piece, depth, lanes = units[0][0].shape
    width = 4
    flat = [unit for group in units for unit in group]
    out = jax.ShapeDtypeStruct((slots, channels, 2, BLOCK, BLOCK), F32)
    first = part * piece // width
    operands = [place] + flat
    in_specs = [pl.BlockSpec((width, depth, lanes), lambda i, place: (i, 0, 0))] * len(flat)
    aliases = {}
    if visibility is not None:
        operands.append(visibility)
        in_specs.append(pl.BlockSpec(memory_space=pl.ANY))
        aliases = {len(operands) - 1: 0}
    return pl.pallas_call(
        functools.partial(correlate_kernel, blocks, tiles, slots),
        grid_spec=pltpu.PrefetchScalarGridSpec(
            num_scalar_prefetch=1,
            grid=(piece // width,),
            in_specs=in_specs,
            out_specs=pl.BlockSpec(
                (slots, width, 2, BLOCK, BLOCK), lambda i, place: (0, first + i, 0, 0, 0)
            ),
            scratch_shapes=[pltpu.VMEM((width, blocks, tiles * depth, lanes), BF16)] * 2,
        ),
        out_shape=out,
        input_output_aliases=aliases,
        compiler_params=params(),
        cost_estimate=pl.CostEstimate(
            flops=3 * 2 * slots * piece * tiles * depth * BLOCK * 2 * BLOCK,
            bytes_accessed=4 * piece * lanes * (tiles * blocks * depth + slots * 2 * BLOCK),
            transcendentals=0,
        ),
        name="correlate",
    )(*operands)


def body(voltage, fir_taps, tile_slot, tile_blocks):
    _, frames, inputs, length = voltage.shape
    tap_count = fir_taps.shape[0]
    owners = lax.axis_size("chan")
    tiles = lax.axis_size("tile")
    channels = length // owners
    blocks = owners // 2
    slots = -(-tile_blocks.shape[0] // tiles)
    scale = 1.0 / math.sqrt(length * frames * tiles)
    table = jnp.asarray(fourier_table(length, owners, scale))

    me = lax.axis_index("chan")
    side = (me % 2).astype(jnp.int32).reshape(1)
    row_blocks, col_blocks, present = own_slots(tile_slot, tile_blocks, slots)
    place = jnp.stack([(me // 2) ^ mask for mask in range(blocks)] + row_blocks + col_blocks + present)
    place = place.astype(jnp.int32)

    following = shifted(voltage[:, : tap_count - 1], "tile", -1)
    high, low = filtered_samples(voltage, following, fir_taps)
    samples = (high.reshape(frames * inputs, -1), low.reshape(frames * inputs, -1))

    order = [0, 1] + [2 * z + x for z in range(blocks - 1, 0, -1) for x in range(2)]
    pieces = {}
    for mask in order:
        owner = (me ^ mask).astype(jnp.int32).reshape(1)
        pieces[mask] = transformed(owner, table, samples, PARTS)

    visibility = None
    for part in range(PARTS):
        arrived = {}
        for mask in order:
            value = pieces[mask][part]
            arrived[mask] = swapped(value, "chan", mask) if mask else value
        units = [[None] * blocks for _ in range(tiles)]
        for mask in [m // 2 for m in order[::2]]:
            unit = merged(side, arrived[2 * mask], arrived[2 * mask + 1])
            units[0][mask] = unit
            units[2][mask] = swapped(unit, "tile", 2)
            units[1][mask] = swapped(unit, "tile", 1)
            units[3][mask] = swapped(units[2][mask], "tile", 1)
        visibility = correlated(place, units, visibility, part, PARTS, channels, slots)
    return visibility


def solution(mesh):
    in_specs = (P(None, "tile", "chan", None), P(), P(), P())
    out_specs = P("tile", "chan", None, None, None)
    owners, tiles = mesh.shape["chan"], mesh.shape["tile"]

    def run(voltage, fir_taps, tile_slot, tile_blocks):
        paired = 2 * voltage.shape[2] == BLOCK * owners and tiles == 4
        chosen = body if paired else generic_body
        return jax.shard_map(
            chosen, mesh=mesh, in_specs=in_specs, out_specs=out_specs, check_vma=False
        )(voltage, fir_taps, tile_slot, tile_blocks)

    return run
```

```python
import functools
import math

import jax
import jax.numpy as jnp
import numpy as np
from jax import lax
from jax.experimental import pallas as pl
from jax.experimental.pallas import tpu as pltpu
from jax.sharding import PartitionSpec as P

BLOCK = 128
RADIX = 4
VMEM_BYTES = 56 * 1024 * 1024
BF16 = jnp.bfloat16
F32 = jnp.float32


def shifted(value, axis, steps):
    count = lax.axis_size(axis)
    initial, last = (max(0, -steps), min(count, count - steps))
    return lax.ppermute(value, axis, [(source, source + steps) for source in range(initial, last)])


def swapped(value, axis, mask):
    count = lax.axis_size(axis)
    return lax.ppermute(value, axis, [(source, source ^ mask) for source in range(count)])


def params():
    return pltpu.CompilerParams(vmem_limit_bytes=VMEM_BYTES)


def split(value):
    high = value.astype(BF16)
    return high, (value - high.astype(F32)).astype(BF16)


def filter_frames(voltage, fir_taps):
    tap_count = fir_taps.shape[0]
    frames = voltage.shape[1]
    history = shifted(voltage[:, : tap_count - 1], "tile", -1)
    extended = jnp.concatenate([voltage, history], axis=1)
    filtered = jnp.zeros(voltage.shape, jnp.float32)
    for tap_index in range(tap_count):
        filtered = (
            filtered
            + fir_taps[tap_index][None, None, None, :] * extended[:, tap_index : tap_index + frames]
        )
    return filtered


def transform(filtered):
    channel_count = filtered.shape[3]
    row_count = filtered.shape[1] * filtered.shape[2]
    position = lax.broadcasted_iota(jnp.int32, (channel_count, channel_count), 0)
    frequency = lax.broadcasted_iota(jnp.int32, (channel_count, channel_count), 1)
    phase_angle = (position * frequency % channel_count).astype(jnp.float32) * (
        2.0 * math.pi / channel_count
    )
    factor = 1.0 / math.sqrt(channel_count)
    cosine = jnp.cos(phase_angle) * factor
    sine_table = jnp.sin(phase_angle) * factor
    samples = filtered.reshape(2 * row_count, channel_count)
    cos_part = jnp.dot(
        cosine, samples.T, precision=lax.Precision.HIGHEST, preferred_element_type=jnp.float32
    )
    sin_part = jnp.dot(
        sine_table, samples.T, precision=lax.Precision.HIGHEST, preferred_element_type=jnp.float32
    )
    real_part = cos_part[:, :row_count] + sin_part[:, row_count:]
    imag_part = cos_part[:, row_count:] - sin_part[:, :row_count]
    joined = jnp.concatenate([real_part, imag_part], axis=1)
    return joined.reshape(channel_count, 2, filtered.shape[1], filtered.shape[2])


def tile_product(gathered, row_block, col_block, block_width):
    left_block = lax.dynamic_slice_in_dim(gathered, row_block * block_width, block_width, 3)
    right_block = lax.dynamic_slice_in_dim(gathered, col_block * block_width, block_width, 3)
    channel_count = gathered.shape[0]
    depth = 2 * gathered.shape[2]
    left_real = left_block.reshape(channel_count, depth, block_width)
    left_imag = jnp.concatenate([left_block[:, 1], -left_block[:, 0]], axis=1)
    left_both = jnp.concatenate([left_real, left_imag], axis=2)
    right_both = right_block.reshape(channel_count, depth, block_width)
    return jnp.einsum(
        "cki,ckj->cij",
        left_both,
        right_both,
        precision=lax.Precision.HIGHEST,
        preferred_element_type=jnp.float32,
    )


def own_slots(tile_slot, tile_blocks, slot_count):
    first_slot = lax.axis_index("tile") * slot_count
    row_blocks = []
    col_blocks = []
    present = []
    for slot_index in range(slot_count):
        matches = (tile_slot == first_slot + slot_index).astype(jnp.int32)
        row_blocks.append(jnp.sum(matches * tile_blocks[:, 0]))
        col_blocks.append(jnp.sum(matches * tile_blocks[:, 1]))
        present.append(jnp.sum(matches))
    return row_blocks, col_blocks, present


def generic_body(voltage, fir_taps, tile_slot, tile_blocks):
    spectra = transform(filter_frames(voltage, fir_taps))
    tile_count = tile_blocks.shape[0]
    tile_size = lax.axis_size("tile")
    slot_count = (tile_count + tile_size - 1) // tile_size
    turned = lax.all_to_all(spectra, "chan", split_axis=0, concat_axis=3, tiled=True)
    spectra_total = turned.shape[2] * tile_size
    row_blocks, col_blocks, present = own_slots(tile_slot, tile_blocks, slot_count)
    portion = lax.all_gather(turned, "tile", axis=2, tiled=True)
    summed = jnp.stack(
        [
            tile_product(portion, row_blocks[slot_index], col_blocks[slot_index], BLOCK)
            for slot_index in range(slot_count)
        ]
    )
    weights = jnp.stack(present).astype(F32)[:, None, None, None] / spectra_total
    return (summed * weights).reshape(slot_count, turned.shape[0], 2, BLOCK, BLOCK)


def fourier_table(points, owners, scale):
    phase = np.outer(np.arange(points), np.arange(points)) % points
    angle = phase * (2.0 * math.pi / points)
    cosine = np.cos(angle) * scale
    sine = np.sin(angle) * scale
    both = np.stack([np.concatenate([cosine, sine], 1), np.concatenate([-sine, cosine], 1)], 0)
    both = both.reshape(2, owners, points // owners, 2 * points).transpose(1, 0, 2, 3)
    return both.reshape(owners, -1, 2 * points).astype(np.float32)


def twiddle_table(length):
    angle = np.outer(np.arange(1, RADIX), np.arange(length // RADIX)) * (2.0 * math.pi / length)
    return np.stack([np.cos(angle), np.sin(angle)], 1).reshape(-1, length // RADIX).astype(np.float32)


def filter_kernel(voltage_ref, next_ref, taps_ref, twiddle_ref, *out_refs):
    tap_count, length = taps_ref.shape
    frames = voltage_ref.shape[1]
    points = length // RADIX

    def quarter(part, frame, index):
        lanes = slice(index * points, (index + 1) * points)
        total = None
        for tap in range(tap_count):
            at = frame + tap
            source = voltage_ref[part, at, :, lanes] if at < frames else next_ref[part, at - frames, :, lanes]
            term = source * taps_ref[pl.ds(tap, 1), lanes]
            total = term if total is None else total + term
        return total

    for frame in range(frames):
        real = [quarter(0, frame, index) for index in range(RADIX)]
        imag = [quarter(1, frame, index) for index in range(RADIX)]
        even_real, odd_real = real[0] + real[2], real[1] + real[3]
        even_imag, odd_imag = imag[0] + imag[2], imag[1] + imag[3]
        left_real, right_real = real[0] - real[2], real[1] - real[3]
        left_imag, right_imag = imag[0] - imag[2], imag[1] - imag[3]
        residues = [
            (even_real + odd_real, even_imag + odd_imag),
            (left_real + right_imag, left_imag - right_real),
            (even_real - odd_real, even_imag - odd_imag),
            (left_real - right_imag, left_imag + right_real),
        ]
        for index, (re, im) in enumerate(residues):
            if index:
                cosine = twiddle_ref[pl.ds(2 * index - 2, 1), :]
                sine = twiddle_ref[pl.ds(2 * index - 1, 1), :]
                re, im = re * cosine + im * sine, im * cosine - re * sine
            for part, value in enumerate((re, im)):
                high, low = split(value)
                lanes = slice(part * points, (part + 1) * points)
                out_refs[2 * index][frame, :, lanes] = high
                out_refs[2 * index + 1][frame, :, lanes] = low


def filtered_samples(voltage, following, fir_taps):
    _, frames, inputs, length = voltage.shape
    extra = following.shape[1]
    width = 16
    depth = 2 * length // RADIX
    twiddles = jnp.asarray(twiddle_table(length))
    out = jax.ShapeDtypeStruct((frames, inputs, depth), BF16)
    out_spec = pl.BlockSpec((frames, width, depth), lambda i: (0, i, 0))
    results = pl.pallas_call(
        filter_kernel,
        grid=(inputs // width,),
        in_specs=[
            pl.BlockSpec((2, frames, width, length), lambda i: (0, 0, i, 0)),
            pl.BlockSpec((2, extra, width, length), lambda i: (0, 0, i, 0)),
            pl.BlockSpec(fir_taps.shape, lambda i: (0, 0)),
            pl.BlockSpec(twiddles.shape, lambda i: (0, 0)),
        ],
        out_specs=[out_spec] * (2 * RADIX),
        out_shape=[out] * (2 * RADIX),
        compiler_params=params(),
        cost_estimate=pl.CostEstimate(
            flops=16 * voltage.size, bytes_accessed=8 * voltage.size, transcendentals=0
        ),
        name="filter",
    )(voltage, following, fir_taps, twiddles)
    rows = [value.reshape(frames * inputs, depth) for value in results]
    return [(rows[2 * index], rows[2 * index + 1]) for index in range(RADIX)]


def dot_rows(left, right):
    return lax.dot_general(left, right, (((1,), (1,)), ((), ())), preferred_element_type=F32)


def transform_kernel(masks, table_ref, xh_ref, xl_ref, *refs):
    out_refs, (th_ref, tl_ref) = refs[-2 - len(masks) : -2], refs[-2:]
    height = table_ref.shape[1]

    @pl.when(pl.program_id(0) == 0)
    def _():
        me = lax.axis_index("chan")
        for index, mask in enumerate(masks):
            rows = slice(index * height, (index + 1) * height)
            th_ref[rows], tl_ref[rows] = split(table_ref[me ^ mask])

    high = xh_ref[...]
    result = dot_rows(th_ref[...], high) + dot_rows(th_ref[...], xl_ref[...])
    result = result + dot_rows(tl_ref[...], high)
    piece = height // 2
    for index, out_ref in enumerate(out_refs):
        for part in range(2):
            first = index * height + part * piece
            for column in range(result.shape[1] // BLOCK):
                out_ref[part, column] = result[
                    first : first + piece, column * BLOCK : (column + 1) * BLOCK
                ]


def transformed(masks, table, samples, after):
    rows, depth = samples[0].shape
    owners, height, _ = table.shape
    step = min(256, rows)
    out = jax.ShapeDtypeStruct((2, rows // BLOCK, height // 2, BLOCK), F32)
    row_spec = pl.BlockSpec((step, depth), lambda i: (i, 0))
    out_spec = pl.BlockSpec((2, step // BLOCK, height // 2, BLOCK), lambda i: (0, i, 0, 0))
    total = len(masks) * height
    results = pl.pallas_call(
        functools.partial(transform_kernel, masks),
        grid=(rows // step,),
        in_specs=[pl.BlockSpec(table.shape, lambda i: (0, 0, 0)), row_spec, row_spec]
        + [pl.BlockSpec(memory_space=pl.ANY)] * len(after),
        out_specs=[out_spec] * len(masks),
        out_shape=[out] * len(masks),
        scratch_shapes=[pltpu.VMEM((total, depth), BF16)] * 2,
        compiler_params=params(),
        cost_estimate=pl.CostEstimate(
            flops=3 * 2 * total * depth * rows,
            bytes_accessed=4 * depth * rows + 4 * table.size + 4 * total * rows,
            transcendentals=0,
        ),
        name="transform",
    )(table, *samples, *after)
    return dict(zip(masks, results))


def merge_kernel(groups, piece, near_ref, far_ref, out_ref):
    odd = lax.axis_index("chan") % 2 == 1
    lower = lax.broadcasted_iota(jnp.int32, (groups, BLOCK), 1) < BLOCK // 2
    for channel in range(piece):
        for part in range(2):
            rows = pl.ds(part * groups * piece + channel, groups, stride=piece)
            near = near_ref[rows, :]
            far = far_ref[rows, :]
            first = jnp.where(odd, far, near)
            second = jnp.where(odd, near, far)
            at = part * 2 * groups
            out_ref[channel, at : at + groups] = jnp.where(
                lower, first, pltpu.roll(second, BLOCK // 2, 1)
            )
            out_ref[channel, at + groups : at + 2 * groups] = jnp.where(
                lower, pltpu.roll(first, BLOCK // 2, 1), second
            )


def merged(near, far):
    _, groups, piece, lanes = near.shape
    flat = (2 * groups * piece, lanes)
    return pl.pallas_call(
        functools.partial(merge_kernel, groups, piece),
        in_specs=[pl.BlockSpec(memory_space=pltpu.VMEM)] * 2,
        out_specs=pl.BlockSpec(memory_space=pltpu.VMEM),
        out_shape=jax.ShapeDtypeStruct((piece, 4 * groups, lanes), F32),
        compiler_params=params(),
        cost_estimate=pl.CostEstimate(
            flops=4 * near.size, bytes_accessed=16 * near.size, transcendentals=0
        ),
        name="merge",
    )(near.reshape(flat), far.reshape(flat))


def dot_columns(left, right):
    return lax.dot_general(left, right, (((0,), (0,)), ((), ())), preferred_element_type=F32)


def correlate_kernel(slots, slot_ref, blocks_ref, *refs):
    out_ref, high_ref, low_ref, place_ref = refs[-4:]
    unit_refs = [ref for ref in refs[:-4] if len(ref.shape) == 4]
    blocks = len(unit_refs)
    width = out_ref.shape[1]
    tiles, _, depth, _ = unit_refs[0].shape
    rows = depth // 2
    half = tiles * rows

    @pl.when(pl.program_id(0) == 0)
    def _():
        first_slot = lax.axis_index("tile") * slots
        for slot in range(slots):
            row = jnp.int32(0)
            col = jnp.int32(0)
            present = jnp.int32(0)
            for tile in range(slot_ref.shape[0]):
                match = (slot_ref[tile] == first_slot + slot).astype(jnp.int32)
                row = row + match * blocks_ref[2 * tile]
                col = col + match * blocks_ref[2 * tile + 1]
                present = present + match
            place_ref[3 * slot] = row
            place_ref[3 * slot + 1] = col
            place_ref[3 * slot + 2] = present

    own = lax.axis_index("chan") // 2
    for channel in range(width):
        for mask in range(blocks):
            block = own ^ mask
            for part in range(2):
                joined = jnp.concatenate(
                    [
                        unit_refs[mask][tile, channel, part * rows : (part + 1) * rows]
                        for tile in range(tiles)
                    ],
                    axis=0,
                )
                high, low = split(joined)
                high_ref[channel, block, part * half : (part + 1) * half] = high
                low_ref[channel, block, part * half : (part + 1) * half] = low
        for slot in range(slots):
            row = place_ref[3 * slot]
            col = place_ref[3 * slot + 1]
            weight = place_ref[3 * slot + 2].astype(F32)
            row_high = high_ref[channel, row]
            row_low = low_ref[channel, row]
            col_high = high_ref[channel, col]
            col_low = low_ref[channel, col]
            turned_high = jnp.concatenate([-col_high[half:], col_high[:half]], axis=0)
            turned_low = jnp.concatenate([-col_low[half:], col_low[:half]], axis=0)
            right_high = jnp.concatenate([col_high, turned_high], axis=1)
            right_low = jnp.concatenate([col_low, turned_low], axis=1)
            value = dot_columns(
                jnp.concatenate([row_high, row_low], axis=0),
                jnp.concatenate([right_high, right_high], axis=0),
            ) + dot_columns(row_high, right_low)
            value = value * weight
            out_ref[slot, channel, 0] = value[:, :BLOCK]
            out_ref[slot, channel, 1] = value[:, BLOCK:]


def correlated(tile_slot, tile_blocks, units, visibility, residue, slots):
    tiles, piece, depth, lanes = units[0].shape
    blocks = len(units)
    width = 4
    out = jax.ShapeDtypeStruct((slots, piece, RADIX, 2, BLOCK, BLOCK), F32)
    operands = [tile_slot, tile_blocks.reshape(-1)] + units
    in_specs = [pl.BlockSpec((tiles, width, depth, lanes), lambda i, *_: (0, i, 0, 0))] * blocks
    aliases = {}
    if visibility is not None:
        operands.append(visibility)
        in_specs.append(pl.BlockSpec(memory_space=pl.ANY))
        aliases = {len(operands) - 1: 0}
    return pl.pallas_call(
        functools.partial(correlate_kernel, slots),
        grid_spec=pltpu.PrefetchScalarGridSpec(
            num_scalar_prefetch=2,
            grid=(piece // width,),
            in_specs=in_specs,
            out_specs=pl.BlockSpec(
                (slots, width, None, 2, BLOCK, BLOCK), lambda i, *_: (0, i, residue, 0, 0, 0)
            ),
            scratch_shapes=[pltpu.VMEM((width, blocks, tiles * depth, lanes), BF16)] * 2
            + [pltpu.SMEM((3 * slots,), jnp.int32)],
        ),
        out_shape=out,
        input_output_aliases=aliases,
        compiler_params=params(),
        cost_estimate=pl.CostEstimate(
            flops=3 * 2 * slots * piece * tiles * depth * BLOCK * 2 * BLOCK,
            bytes_accessed=4 * piece * lanes * (tiles * blocks * depth + slots * 2 * BLOCK),
            transcendentals=0,
        ),
        name="correlate",
    )(*operands)


def body(voltage, fir_taps, tile_slot, tile_blocks):
    _, frames, inputs, length = voltage.shape
    tap_count = fir_taps.shape[0]
    owners = lax.axis_size("chan")
    tiles = lax.axis_size("tile")
    channels = length // owners
    blocks = owners // 2
    slots = -(-tile_blocks.shape[0] // tiles)
    scale = 1.0 / math.sqrt(length * frames * tiles)
    table = jnp.asarray(fourier_table(length // RADIX, owners, scale))

    following = shifted(voltage[:, : tap_count - 1], "tile", -1)
    samples = filtered_samples(voltage, following, fir_taps)

    own = (0, 1)
    far = [mask for block in list(range(2, blocks)) + [1] for mask in (2 * block, 2 * block + 1)]
    arrived = [{} for _ in range(RADIX)]
    units = [[None] * blocks for _ in range(RADIX)]

    def send(residue, masks, after):
        for mask, value in transformed(masks, table, samples[residue], after).items():
            arrived[residue][mask] = swapped(value, "chan", mask) if mask else value

    def join(residue, block):
        unit = merged(arrived[residue][2 * block], arrived[residue][2 * block + 1])
        units[residue][block] = lax.all_gather(unit, "tile")
        return unit

    send(0, far, [])
    after = []
    for residue in range(RADIX):
        send(residue, own, after)
        after = [join(residue, 0)]
    visibility = None
    for residue in range(RADIX):
        first = True
        for block in list(range(2, blocks)) + [1]:
            unit = join(residue, block)
            if first and residue + 1 < RADIX:
                send(residue + 1, far, [unit])
            first = False
        visibility = correlated(tile_slot, tile_blocks, units[residue], visibility, residue, slots)
    return visibility.reshape(slots, channels, 2, BLOCK, BLOCK)


def solution(mesh):
    in_specs = (P(None, "tile", "chan", None), P(), P(), P())
    out_specs = P("tile", "chan", None, None, None)
    owners, tiles = mesh.shape["chan"], mesh.shape["tile"]

    def run(voltage, fir_taps, tile_slot, tile_blocks):
        paired = 2 * voltage.shape[2] == BLOCK * owners and tiles == 4
        chosen = body if paired else generic_body
        return jax.shard_map(
            chosen, mesh=mesh, in_specs=in_specs, out_specs=out_specs, check_vma=False
        )(voltage, fir_taps, tile_slot, tile_blocks)

    return run
```

```python
import functools
import math

import jax
import jax.numpy as jnp
import numpy as np
from jax import lax
from jax.experimental import pallas as pl
from jax.experimental.pallas import tpu as pltpu
from jax.sharding import PartitionSpec as P

BLOCK = 128
RADIX = 4
VMEM_BYTES = 56 * 1024 * 1024
BF16 = jnp.bfloat16
F32 = jnp.float32


def shifted(value, axis, steps):
    count = lax.axis_size(axis)
    initial, last = (max(0, -steps), min(count, count - steps))
    return lax.ppermute(value, axis, [(source, source + steps) for source in range(initial, last)])


def swapped(value, axis, mask):
    count = lax.axis_size(axis)
    return lax.ppermute(value, axis, [(source, source ^ mask) for source in range(count)])


def params():
    return pltpu.CompilerParams(vmem_limit_bytes=VMEM_BYTES)


def split(value):
    high = value.astype(BF16)
    return high, (value - high.astype(F32)).astype(BF16)


def filter_frames(voltage, fir_taps):
    tap_count = fir_taps.shape[0]
    frames = voltage.shape[1]
    history = shifted(voltage[:, : tap_count - 1], "tile", -1)
    extended = jnp.concatenate([voltage, history], axis=1)
    filtered = jnp.zeros(voltage.shape, jnp.float32)
    for tap_index in range(tap_count):
        filtered = (
            filtered
            + fir_taps[tap_index][None, None, None, :] * extended[:, tap_index : tap_index + frames]
        )
    return filtered


def transform(filtered):
    channel_count = filtered.shape[3]
    row_count = filtered.shape[1] * filtered.shape[2]
    position = lax.broadcasted_iota(jnp.int32, (channel_count, channel_count), 0)
    frequency = lax.broadcasted_iota(jnp.int32, (channel_count, channel_count), 1)
    phase_angle = (position * frequency % channel_count).astype(jnp.float32) * (
        2.0 * math.pi / channel_count
    )
    factor = 1.0 / math.sqrt(channel_count)
    cosine = jnp.cos(phase_angle) * factor
    sine_table = jnp.sin(phase_angle) * factor
    samples = filtered.reshape(2 * row_count, channel_count)
    cos_part = jnp.dot(
        cosine, samples.T, precision=lax.Precision.HIGHEST, preferred_element_type=jnp.float32
    )
    sin_part = jnp.dot(
        sine_table, samples.T, precision=lax.Precision.HIGHEST, preferred_element_type=jnp.float32
    )
    real_part = cos_part[:, :row_count] + sin_part[:, row_count:]
    imag_part = cos_part[:, row_count:] - sin_part[:, :row_count]
    joined = jnp.concatenate([real_part, imag_part], axis=1)
    return joined.reshape(channel_count, 2, filtered.shape[1], filtered.shape[2])


def tile_product(gathered, row_block, col_block, block_width):
    left_block = lax.dynamic_slice_in_dim(gathered, row_block * block_width, block_width, 3)
    right_block = lax.dynamic_slice_in_dim(gathered, col_block * block_width, block_width, 3)
    channel_count = gathered.shape[0]
    depth = 2 * gathered.shape[2]
    left_real = left_block.reshape(channel_count, depth, block_width)
    left_imag = jnp.concatenate([left_block[:, 1], -left_block[:, 0]], axis=1)
    left_both = jnp.concatenate([left_real, left_imag], axis=2)
    right_both = right_block.reshape(channel_count, depth, block_width)
    return jnp.einsum(
        "cki,ckj->cij",
        left_both,
        right_both,
        precision=lax.Precision.HIGHEST,
        preferred_element_type=jnp.float32,
    )


def own_slots(tile_slot, tile_blocks, slot_count):
    first_slot = lax.axis_index("tile") * slot_count
    row_blocks = []
    col_blocks = []
    present = []
    for slot_index in range(slot_count):
        matches = (tile_slot == first_slot + slot_index).astype(jnp.int32)
        row_blocks.append(jnp.sum(matches * tile_blocks[:, 0]))
        col_blocks.append(jnp.sum(matches * tile_blocks[:, 1]))
        present.append(jnp.sum(matches))
    return row_blocks, col_blocks, present


def generic_body(voltage, fir_taps, tile_slot, tile_blocks):
    spectra = transform(filter_frames(voltage, fir_taps))
    tile_count = tile_blocks.shape[0]
    tile_size = lax.axis_size("tile")
    slot_count = (tile_count + tile_size - 1) // tile_size
    turned = lax.all_to_all(spectra, "chan", split_axis=0, concat_axis=3, tiled=True)
    spectra_total = turned.shape[2] * tile_size
    row_blocks, col_blocks, present = own_slots(tile_slot, tile_blocks, slot_count)
    portion = lax.all_gather(turned, "tile", axis=2, tiled=True)
    summed = jnp.stack(
        [
            tile_product(portion, row_blocks[slot_index], col_blocks[slot_index], BLOCK)
            for slot_index in range(slot_count)
        ]
    )
    weights = jnp.stack(present).astype(F32)[:, None, None, None] / spectra_total
    return (summed * weights).reshape(slot_count, turned.shape[0], 2, BLOCK, BLOCK)


def fourier_table(points, owners, scale):
    phase = np.outer(np.arange(points), np.arange(points)) % points
    angle = phase * (2.0 * math.pi / points)
    cosine = np.cos(angle) * scale
    sine = np.sin(angle) * scale
    both = np.stack([np.concatenate([cosine, sine], 1), np.concatenate([-sine, cosine], 1)], 0)
    both = both.reshape(2, owners, points // owners, 2 * points).transpose(1, 0, 2, 3)
    return both.reshape(owners, -1, 2 * points).astype(np.float32)


def twiddle_table(length):
    angle = np.outer(np.arange(1, RADIX), np.arange(length // RADIX)) * (2.0 * math.pi / length)
    return np.stack([np.cos(angle), np.sin(angle)], 1).reshape(-1, length // RADIX).astype(np.float32)


def filter_kernel(voltage_ref, next_ref, taps_ref, twiddle_ref, *out_refs):
    tap_count, length = taps_ref.shape
    frames = voltage_ref.shape[1]
    points = length // RADIX

    def quarter(part, frame, index):
        lanes = slice(index * points, (index + 1) * points)
        total = None
        for tap in range(tap_count):
            at = frame + tap
            source = voltage_ref[part, at, :, lanes] if at < frames else next_ref[part, at - frames, :, lanes]
            term = source * taps_ref[pl.ds(tap, 1), lanes]
            total = term if total is None else total + term
        return total

    for frame in range(frames):
        real = [quarter(0, frame, index) for index in range(RADIX)]
        imag = [quarter(1, frame, index) for index in range(RADIX)]
        even_real, odd_real = real[0] + real[2], real[1] + real[3]
        even_imag, odd_imag = imag[0] + imag[2], imag[1] + imag[3]
        left_real, right_real = real[0] - real[2], real[1] - real[3]
        left_imag, right_imag = imag[0] - imag[2], imag[1] - imag[3]
        residues = [
            (even_real + odd_real, even_imag + odd_imag),
            (left_real + right_imag, left_imag - right_real),
            (even_real - odd_real, even_imag - odd_imag),
            (left_real - right_imag, left_imag + right_real),
        ]
        for index, (re, im) in enumerate(residues):
            if index:
                cosine = twiddle_ref[pl.ds(2 * index - 2, 1), :]
                sine = twiddle_ref[pl.ds(2 * index - 1, 1), :]
                re, im = re * cosine + im * sine, im * cosine - re * sine
            for part, value in enumerate((re, im)):
                high, low = split(value)
                lanes = slice(part * points, (part + 1) * points)
                out_refs[2 * index][frame, :, lanes] = high
                out_refs[2 * index + 1][frame, :, lanes] = low


def filtered_samples(voltage, following, fir_taps):
    _, frames, inputs, length = voltage.shape
    extra = following.shape[1]
    width = 16
    depth = 2 * length // RADIX
    twiddles = jnp.asarray(twiddle_table(length))
    out = jax.ShapeDtypeStruct((frames, inputs, depth), BF16)
    out_spec = pl.BlockSpec((frames, width, depth), lambda i: (0, i, 0))
    results = pl.pallas_call(
        filter_kernel,
        grid=(inputs // width,),
        in_specs=[
            pl.BlockSpec((2, frames, width, length), lambda i: (0, 0, i, 0)),
            pl.BlockSpec((2, extra, width, length), lambda i: (0, 0, i, 0)),
            pl.BlockSpec(fir_taps.shape, lambda i: (0, 0)),
            pl.BlockSpec(twiddles.shape, lambda i: (0, 0)),
        ],
        out_specs=[out_spec] * (2 * RADIX),
        out_shape=[out] * (2 * RADIX),
        compiler_params=params(),
        cost_estimate=pl.CostEstimate(
            flops=16 * voltage.size, bytes_accessed=8 * voltage.size, transcendentals=0
        ),
        name="filter",
    )(voltage, following, fir_taps, twiddles)
    rows = [value.reshape(frames * inputs, depth) for value in results]
    return [(rows[2 * index], rows[2 * index + 1]) for index in range(RADIX)]


def dot_rows(left, right):
    return lax.dot_general(left, right, (((1,), (1,)), ((), ())), preferred_element_type=F32)


def transform_kernel(groups, pieces, table_ref, xh_ref, xl_ref, *refs):
    out_refs, (th_ref, tl_ref) = refs[-2 - len(groups) * pieces : -2], refs[-2:]
    height = table_ref.shape[1]
    masks = [mask for group in groups for mask in group]

    @pl.when(pl.program_id(0) == 0)
    def _():
        me = lax.axis_index("chan")
        for index, mask in enumerate(masks):
            rows = slice(index * height, (index + 1) * height)
            th_ref[rows], tl_ref[rows] = split(table_ref[me ^ mask])

    high = xh_ref[...]
    result = dot_rows(th_ref[...], high) + dot_rows(th_ref[...], xl_ref[...])
    result = result + dot_rows(tl_ref[...], high)
    count = height // 2
    size = count // pieces
    places = [(which, at) for which, group in enumerate(groups) for at in range(len(group))]
    for index, (which, at) in enumerate(places):
        for part in range(2):
            for piece in range(pieces):
                first = index * height + part * count + piece * size
                for column in range(result.shape[1] // BLOCK):
                    out_refs[which * pieces + piece][at, part, column] = result[
                        first : first + size, column * BLOCK : (column + 1) * BLOCK
                    ]


def transformed(groups, pieces, table, samples):
    rows, depth = samples[0].shape
    owners, height, _ = table.shape
    size = height // 2 // pieces
    step = min(256, rows)
    row_spec = pl.BlockSpec((step, depth), lambda i: (i, 0))
    total = sum(map(len, groups)) * height
    counts = [len(group) for group in groups for _ in range(pieces)]
    return pl.pallas_call(
        functools.partial(transform_kernel, groups, pieces),
        grid=(rows // step,),
        in_specs=[pl.BlockSpec(table.shape, lambda i: (0, 0, 0)), row_spec, row_spec],
        out_specs=[
            pl.BlockSpec((count, 2, step // BLOCK, size, BLOCK), lambda i: (0, 0, i, 0, 0))
            for count in counts
        ],
        out_shape=[
            jax.ShapeDtypeStruct((count, 2, rows // BLOCK, size, BLOCK), F32) for count in counts
        ],
        scratch_shapes=[pltpu.VMEM((total, depth), BF16)] * 2,
        compiler_params=params(),
        cost_estimate=pl.CostEstimate(
            flops=3 * 2 * total * depth * rows,
            bytes_accessed=4 * depth * rows + 4 * table.size + 4 * total * rows,
            transcendentals=0,
        ),
        name="transform",
    )(table, *samples)


def merge_kernel(count, groups, piece, near_ref, far_ref, *out_refs):
    odd = lax.axis_index("chan") % 2 == 1
    lower = lax.broadcasted_iota(jnp.int32, (groups, BLOCK), 1) < BLOCK // 2
    for unit, out_ref in enumerate(out_refs):
        for channel in range(piece):
            for part in range(2):
                rows = pl.ds((unit * 2 + part) * groups * piece + channel, groups, stride=piece)
                near = near_ref[rows, :]
                far = far_ref[rows, :]
                first = jnp.where(odd, far, near)
                second = jnp.where(odd, near, far)
                at = part * 2 * groups
                out_ref[channel, at : at + groups] = jnp.where(
                    lower, first, pltpu.roll(second, BLOCK // 2, 1)
                )
                out_ref[channel, at + groups : at + 2 * groups] = jnp.where(
                    lower, pltpu.roll(first, BLOCK // 2, 1), second
                )


def merged(near, far):
    count, _, groups, piece, lanes = near.shape
    flat = (count * 2 * groups * piece, lanes)
    return pl.pallas_call(
        functools.partial(merge_kernel, count, groups, piece),
        in_specs=[pl.BlockSpec(memory_space=pltpu.VMEM)] * 2,
        out_specs=[pl.BlockSpec(memory_space=pltpu.VMEM)] * count,
        out_shape=[jax.ShapeDtypeStruct((piece, 4 * groups, lanes), F32)] * count,
        compiler_params=params(),
        cost_estimate=pl.CostEstimate(
            flops=4 * near.size, bytes_accessed=16 * near.size, transcendentals=0
        ),
        name="merge",
    )(near.reshape(flat), far.reshape(flat))


def pack_kernel(count, *refs):
    out_ref = refs[-1]
    for index, ref in enumerate(refs[:count]):
        out_ref[index] = ref[...]


def packed(values, after):
    shape = values[0].shape
    lead = shape[:-3]
    piece, depth, lanes = shape[-3:]
    width = min(8, piece)
    count = len(values)
    none = (0,) * len(lead)
    return pl.pallas_call(
        functools.partial(pack_kernel, count),
        grid=(piece // width,),
        in_specs=[pl.BlockSpec(lead + (width, depth, lanes), lambda i: none + (i, 0, 0))] * count
        + [pl.BlockSpec(memory_space=pl.ANY)] * len(after),
        out_specs=pl.BlockSpec((count,) + lead + (width, depth, lanes), lambda i: (0,) + none + (i, 0, 0)),
        out_shape=jax.ShapeDtypeStruct((count,) + shape, F32),
        compiler_params=params(),
        cost_estimate=pl.CostEstimate(
            flops=0, bytes_accessed=8 * count * values[0].size, transcendentals=0
        ),
        name="pack",
    )(*values, *after)


def dot_columns(left, right):
    return lax.dot_general(left, right, (((0,), (0,)), ((), ())), preferred_element_type=F32)


def correlate_kernel(slots, tiles, order, slot_ref, blocks_ref, *refs):
    unit_refs = []
    for ref in refs[:-5]:
        if len(ref.shape) == 4:
            unit_refs.append(ref)
        elif len(ref.shape) == 5 and len(unit_refs) < tiles:
            unit_refs += [ref.at[0], ref.at[1]]
    out_ref, done_ref, high_ref, low_ref, place_ref = refs[-5:]
    done_ref[...] = jnp.zeros(done_ref.shape, F32)
    blocks, width, depth, _ = unit_refs[0].shape
    rows = depth // 2
    half = tiles * rows

    @pl.when(pl.program_id(0) == 0)
    def _():
        first_slot = lax.axis_index("tile") * slots
        for slot in range(slots):
            row = jnp.int32(0)
            col = jnp.int32(0)
            present = jnp.int32(0)
            for tile in range(slot_ref.shape[0]):
                match = (slot_ref[tile] == first_slot + slot).astype(jnp.int32)
                row = row + match * blocks_ref[2 * tile]
                col = col + match * blocks_ref[2 * tile + 1]
                present = present + match
            place_ref[3 * slot] = row
            place_ref[3 * slot + 1] = col
            place_ref[3 * slot + 2] = present

    own = lax.axis_index("chan") // 2
    for channel in range(width):
        for mask in range(blocks):
            block = own ^ order[mask]
            for part in range(2):
                joined = jnp.concatenate(
                    [
                        unit_ref[mask, channel, part * rows : (part + 1) * rows]
                        for unit_ref in unit_refs
                    ],
                    axis=0,
                )
                high, low = split(joined)
                high_ref[channel, block, part * half : (part + 1) * half] = high
                low_ref[channel, block, part * half : (part + 1) * half] = low
        for slot in range(slots):
            row = place_ref[3 * slot]
            col = place_ref[3 * slot + 1]
            weight = place_ref[3 * slot + 2].astype(F32)
            row_high = high_ref[channel, row]
            row_low = low_ref[channel, row]
            col_high = high_ref[channel, col]
            col_low = low_ref[channel, col]
            turned_high = jnp.concatenate([-col_high[half:], col_high[:half]], axis=0)
            turned_low = jnp.concatenate([-col_low[half:], col_low[:half]], axis=0)
            right_high = jnp.concatenate([col_high, turned_high], axis=1)
            right_low = jnp.concatenate([col_low, turned_low], axis=1)
            value = dot_columns(
                jnp.concatenate([row_high, row_low], axis=0),
                jnp.concatenate([right_high, right_high], axis=0),
            ) + dot_columns(row_high, right_low)
            value = value * weight
            out_ref[slot, channel, 0] = value[:, :BLOCK]
            out_ref[slot, channel, 1] = value[:, BLOCK:]


def correlated(order, tile_slot, tile_blocks, units, visibility, residue, first, total, slots):
    tiles = sum(1 if unit.ndim == 4 else unit.shape[0] for unit in units)
    blocks, piece, depth, lanes = units[0].shape
    width = 4
    out = jax.ShapeDtypeStruct((slots, total, RADIX, 2, BLOCK, BLOCK), F32)
    operands = [tile_slot, tile_blocks.reshape(-1)] + units
    in_specs = [
        pl.BlockSpec((blocks, width, depth, lanes), lambda i, *_: (0, i, 0, 0))
        if unit.ndim == 4
        else pl.BlockSpec(unit.shape[:2] + (width, depth, lanes), lambda i, *_: (0, 0, i, 0, 0))
        for unit in units
    ]
    aliases = {}
    if visibility is not None:
        operands.append(visibility)
        in_specs.append(pl.BlockSpec(memory_space=pl.ANY))
        aliases = {len(operands) - 1: 0}
    return pl.pallas_call(
        functools.partial(correlate_kernel, slots, tiles, order),
        grid_spec=pltpu.PrefetchScalarGridSpec(
            num_scalar_prefetch=2,
            grid=(piece // width,),
            in_specs=in_specs,
            out_specs=[
                pl.BlockSpec(
                    (slots, width, None, 2, BLOCK, BLOCK), lambda i, *_: (0, first // width + i, residue, 0, 0, 0)
                ),
                pl.BlockSpec((8, BLOCK), lambda i, *_: (0, 0)),
            ],
            scratch_shapes=[pltpu.VMEM((width, blocks, tiles * depth, lanes), BF16)] * 2
            + [pltpu.SMEM((3 * slots,), jnp.int32)],
        ),
        out_shape=[out, jax.ShapeDtypeStruct((8, BLOCK), F32)],
        input_output_aliases=aliases,
        compiler_params=params(),
        cost_estimate=pl.CostEstimate(
            flops=3 * 2 * slots * piece * tiles * depth * BLOCK * 2 * BLOCK,
            bytes_accessed=4 * piece * lanes * (tiles * blocks * depth + slots * 2 * BLOCK),
            transcendentals=0,
        ),
        name="correlate",
    )(*operands)


def body(voltage, fir_taps, tile_slot, tile_blocks):
    _, frames, inputs, length = voltage.shape
    tap_count = fir_taps.shape[0]
    owners = lax.axis_size("chan")
    tiles = lax.axis_size("tile")
    channels = length // owners
    blocks = owners // 2
    slots = -(-tile_blocks.shape[0] // tiles)
    scale = 1.0 / math.sqrt(length * frames * tiles)
    table = jnp.asarray(fourier_table(length // RADIX, owners, scale))

    following = shifted(voltage[:, : tap_count - 1], "tile", -1)
    samples = filtered_samples(voltage, following, fir_taps)

    order = list(range(2, blocks)) + [1, 0]
    groups = [tuple(2 * block + x for block in order) for x in range(2)]
    halves = 2
    size = channels // RADIX // halves
    near, away = [], []
    for residue in range(RADIX):
        values = transformed(groups, halves, table, samples[residue])
        near += values[:halves]
        away += [swapped(value, "chan", 1) for value in values[halves:]]
    count = len(near)
    units = [merged(near[piece], away[piece]) for piece in range(count)]

    def along(piece):
        return [
            swapped(unit, "chan", 2 * block) if block else unit
            for block, unit in zip(order, units[piece])
        ]

    visibility = None
    finished = []
    turned = along(0)
    own, across, ready = [], [], []
    for piece in range(count + 2):
        if piece < count:
            after = [across[piece - 1]] if piece else []
            after += [unit[0] for unit in units[2 * piece + 1 : 2 * piece + 3]]
            after += finished[piece - 2 : piece - 1] if piece >= 2 else []
            own.append(packed(turned, after))
            if piece + 1 < count:
                turned = along(piece + 1)
            across.append(swapped(own[piece], "tile", 2))
        if 0 <= piece - 1 < count:
            pair = [own[piece - 1], across[piece - 1]]
            if piece < count:
                ready.append(pair + [swapped(packed(pair, [own[piece]]), "tile", 1)])
            else:
                ready.append(pair + [swapped(value, "tile", 1) for value in pair])
        if 0 <= piece - 1 < count:
            at = piece - 1
            visibility, token = correlated(
                order, tile_slot, tile_blocks, ready[at], visibility,
                at // halves, at % halves * size, channels // RADIX, slots,
            )
            finished.append(token)
    return visibility.reshape(slots, channels, 2, BLOCK, BLOCK)


def solution(mesh):
    in_specs = (P(None, "tile", "chan", None), P(), P(), P())
    out_specs = P("tile", "chan", None, None, None)
    owners, tiles = mesh.shape["chan"], mesh.shape["tile"]

    def run(voltage, fir_taps, tile_slot, tile_blocks):
        paired = 2 * voltage.shape[2] == BLOCK * owners and tiles == 4
        chosen = body if paired else generic_body
        return jax.shard_map(
            chosen, mesh=mesh, in_specs=in_specs, out_specs=out_specs, check_vma=False
        )(voltage, fir_taps, tile_slot, tile_blocks)

    return run
```

```python
import functools
import math

import jax
import jax.numpy as jnp
import numpy as np
from jax import lax
from jax.experimental import pallas as pl
from jax.experimental.pallas import tpu as pltpu
from jax.sharding import PartitionSpec as P

BLOCK = 128
RADIX = 4
VMEM_BYTES = 20 * 1024 * 1024
BF16 = jnp.bfloat16
F32 = jnp.float32


def shifted(value, axis, steps):
    count = lax.axis_size(axis)
    initial, last = (max(0, -steps), min(count, count - steps))
    return lax.ppermute(value, axis, [(source, source + steps) for source in range(initial, last)])


def swapped(value, axis, mask):
    count = lax.axis_size(axis)
    return lax.ppermute(value, axis, [(source, source ^ mask) for source in range(count)])


def params():
    return pltpu.CompilerParams(vmem_limit_bytes=VMEM_BYTES)


def split(value):
    high = value.astype(BF16)
    return high, (value - high.astype(F32)).astype(BF16)


def filter_frames(voltage, fir_taps):
    tap_count = fir_taps.shape[0]
    frames = voltage.shape[1]
    history = shifted(voltage[:, : tap_count - 1], "tile", -1)
    extended = jnp.concatenate([voltage, history], axis=1)
    filtered = jnp.zeros(voltage.shape, jnp.float32)
    for tap_index in range(tap_count):
        filtered = (
            filtered
            + fir_taps[tap_index][None, None, None, :] * extended[:, tap_index : tap_index + frames]
        )
    return filtered


def transform(filtered):
    channel_count = filtered.shape[3]
    row_count = filtered.shape[1] * filtered.shape[2]
    position = lax.broadcasted_iota(jnp.int32, (channel_count, channel_count), 0)
    frequency = lax.broadcasted_iota(jnp.int32, (channel_count, channel_count), 1)
    phase_angle = (position * frequency % channel_count).astype(jnp.float32) * (
        2.0 * math.pi / channel_count
    )
    factor = 1.0 / math.sqrt(channel_count)
    cosine = jnp.cos(phase_angle) * factor
    sine_table = jnp.sin(phase_angle) * factor
    samples = filtered.reshape(2 * row_count, channel_count)
    cos_part = jnp.dot(
        cosine, samples.T, precision=lax.Precision.HIGHEST, preferred_element_type=jnp.float32
    )
    sin_part = jnp.dot(
        sine_table, samples.T, precision=lax.Precision.HIGHEST, preferred_element_type=jnp.float32
    )
    real_part = cos_part[:, :row_count] + sin_part[:, row_count:]
    imag_part = cos_part[:, row_count:] - sin_part[:, :row_count]
    joined = jnp.concatenate([real_part, imag_part], axis=1)
    return joined.reshape(channel_count, 2, filtered.shape[1], filtered.shape[2])


def tile_product(gathered, row_block, col_block, block_width):
    left_block = lax.dynamic_slice_in_dim(gathered, row_block * block_width, block_width, 3)
    right_block = lax.dynamic_slice_in_dim(gathered, col_block * block_width, block_width, 3)
    channel_count = gathered.shape[0]
    depth = 2 * gathered.shape[2]
    left_real = left_block.reshape(channel_count, depth, block_width)
    left_imag = jnp.concatenate([left_block[:, 1], -left_block[:, 0]], axis=1)
    left_both = jnp.concatenate([left_real, left_imag], axis=2)
    right_both = right_block.reshape(channel_count, depth, block_width)
    return jnp.einsum(
        "cki,ckj->cij",
        left_both,
        right_both,
        precision=lax.Precision.HIGHEST,
        preferred_element_type=jnp.float32,
    )


def own_slots(tile_slot, tile_blocks, slot_count):
    first_slot = lax.axis_index("tile") * slot_count
    row_blocks = []
    col_blocks = []
    present = []
    for slot_index in range(slot_count):
        matches = (tile_slot == first_slot + slot_index).astype(jnp.int32)
        row_blocks.append(jnp.sum(matches * tile_blocks[:, 0]))
        col_blocks.append(jnp.sum(matches * tile_blocks[:, 1]))
        present.append(jnp.sum(matches))
    return row_blocks, col_blocks, present


def generic_body(voltage, fir_taps, tile_slot, tile_blocks):
    spectra = transform(filter_frames(voltage, fir_taps))
    tile_count = tile_blocks.shape[0]
    tile_size = lax.axis_size("tile")
    slot_count = (tile_count + tile_size - 1) // tile_size
    turned = lax.all_to_all(spectra, "chan", split_axis=0, concat_axis=3, tiled=True)
    spectra_total = turned.shape[2] * tile_size
    row_blocks, col_blocks, present = own_slots(tile_slot, tile_blocks, slot_count)
    portion = lax.all_gather(turned, "tile", axis=2, tiled=True)
    summed = jnp.stack(
        [
            tile_product(portion, row_blocks[slot_index], col_blocks[slot_index], BLOCK)
            for slot_index in range(slot_count)
        ]
    )
    weights = jnp.stack(present).astype(F32)[:, None, None, None] / spectra_total
    return (summed * weights).reshape(slot_count, turned.shape[0], 2, BLOCK, BLOCK)


def fourier_table(points, owners, scale):
    phase = np.outer(np.arange(points), np.arange(points)) % points
    angle = phase * (2.0 * math.pi / points)
    cosine = np.cos(angle) * scale
    sine = np.sin(angle) * scale
    both = np.stack([np.concatenate([cosine, sine], 1), np.concatenate([-sine, cosine], 1)], 0)
    both = both.reshape(2, owners, points // owners, 2 * points).transpose(1, 0, 2, 3)
    return both.reshape(owners, -1, 2 * points).astype(np.float32)


def twiddle_table(length):
    angle = np.outer(np.arange(1, RADIX), np.arange(length // RADIX)) * (2.0 * math.pi / length)
    return np.stack([np.cos(angle), np.sin(angle)], 1).reshape(-1, length // RADIX).astype(np.float32)


def filter_kernel(voltage_ref, next_ref, taps_ref, twiddle_ref, *out_refs):
    tap_count, length = taps_ref.shape
    frames = voltage_ref.shape[1]
    points = length // RADIX

    def quarter(part, frame, index):
        lanes = slice(index * points, (index + 1) * points)
        total = None
        for tap in range(tap_count):
            at = frame + tap
            source = voltage_ref[part, at, :, lanes] if at < frames else next_ref[part, at - frames, :, lanes]
            term = source * taps_ref[pl.ds(tap, 1), lanes]
            total = term if total is None else total + term
        return total

    for frame in range(frames):
        real = [quarter(0, frame, index) for index in range(RADIX)]
        imag = [quarter(1, frame, index) for index in range(RADIX)]
        even_real, odd_real = real[0] + real[2], real[1] + real[3]
        even_imag, odd_imag = imag[0] + imag[2], imag[1] + imag[3]
        left_real, right_real = real[0] - real[2], real[1] - real[3]
        left_imag, right_imag = imag[0] - imag[2], imag[1] - imag[3]
        residues = [
            (even_real + odd_real, even_imag + odd_imag),
            (left_real + right_imag, left_imag - right_real),
            (even_real - odd_real, even_imag - odd_imag),
            (left_real - right_imag, left_imag + right_real),
        ]
        for index, (re, im) in enumerate(residues):
            if index:
                cosine = twiddle_ref[pl.ds(2 * index - 2, 1), :]
                sine = twiddle_ref[pl.ds(2 * index - 1, 1), :]
                re, im = re * cosine + im * sine, im * cosine - re * sine
            for part, value in enumerate((re, im)):
                high, low = split(value)
                lanes = slice(part * points, (part + 1) * points)
                out_refs[2 * index][frame, :, lanes] = high
                out_refs[2 * index + 1][frame, :, lanes] = low


def filtered_samples(voltage, following, fir_taps):
    _, frames, inputs, length = voltage.shape
    extra = following.shape[1]
    width = 16
    depth = 2 * length // RADIX
    twiddles = jnp.asarray(twiddle_table(length))
    out = jax.ShapeDtypeStruct((frames, inputs, depth), BF16)
    out_spec = pl.BlockSpec((frames, width, depth), lambda i: (0, i, 0))
    results = pl.pallas_call(
        filter_kernel,
        grid=(inputs // width,),
        in_specs=[
            pl.BlockSpec((2, frames, width, length), lambda i: (0, 0, i, 0)),
            pl.BlockSpec((2, extra, width, length), lambda i: (0, 0, i, 0)),
            pl.BlockSpec(fir_taps.shape, lambda i: (0, 0)),
            pl.BlockSpec(twiddles.shape, lambda i: (0, 0)),
        ],
        out_specs=[out_spec] * (2 * RADIX),
        out_shape=[out] * (2 * RADIX),
        compiler_params=params(),
        cost_estimate=pl.CostEstimate(
            flops=16 * voltage.size, bytes_accessed=8 * voltage.size, transcendentals=0
        ),
        name="filter",
    )(voltage, following, fir_taps, twiddles)
    rows = [value.reshape(frames * inputs, depth) for value in results]
    return [(rows[2 * index], rows[2 * index + 1]) for index in range(RADIX)]


def dot_rows(left, right):
    return lax.dot_general(left, right, (((1,), (1,)), ((), ())), preferred_element_type=F32)


def transform_kernel(groups, pieces, table_ref, xh_ref, xl_ref, *refs):
    out_refs, (th_ref, tl_ref) = refs[-2 - len(groups) * pieces : -2], refs[-2:]
    height = table_ref.shape[1]
    masks = [mask for group in groups for mask in group]

    @pl.when(pl.program_id(0) == 0)
    def _():
        me = lax.axis_index("chan")
        for index, mask in enumerate(masks):
            rows = slice(index * height, (index + 1) * height)
            th_ref[rows], tl_ref[rows] = split(table_ref[me ^ mask])

    high = xh_ref[...]
    result = dot_rows(th_ref[...], high) + dot_rows(th_ref[...], xl_ref[...])
    result = result + dot_rows(tl_ref[...], high)
    count = height // 2
    size = count // pieces
    places = [(which, at) for which, group in enumerate(groups) for at in range(len(group))]
    for index, (which, at) in enumerate(places):
        for part in range(2):
            for piece in range(pieces):
                first = index * height + part * count + piece * size
                for column in range(result.shape[1] // BLOCK):
                    out_refs[which * pieces + piece][at, part, column] = result[
                        first : first + size, column * BLOCK : (column + 1) * BLOCK
                    ]


def transformed(groups, pieces, table, samples, after):
    rows, depth = samples[0].shape
    owners, height, _ = table.shape
    size = height // 2 // pieces
    step = min(256, rows)
    row_spec = pl.BlockSpec((step, depth), lambda i: (i, 0))
    total = sum(map(len, groups)) * height
    counts = [len(group) for group in groups for _ in range(pieces)]
    return pl.pallas_call(
        functools.partial(transform_kernel, groups, pieces),
        grid=(rows // step,),
        in_specs=[pl.BlockSpec(table.shape, lambda i: (0, 0, 0)), row_spec, row_spec]
        + [pl.BlockSpec(memory_space=pl.ANY)] * len(after),
        out_specs=[
            pl.BlockSpec((count, 2, step // BLOCK, size, BLOCK), lambda i: (0, 0, i, 0, 0))
            for count in counts
        ],
        out_shape=[
            jax.ShapeDtypeStruct((count, 2, rows // BLOCK, size, BLOCK), F32) for count in counts
        ],
        scratch_shapes=[pltpu.VMEM((total, depth), BF16)] * 2,
        compiler_params=params(),
        cost_estimate=pl.CostEstimate(
            flops=3 * 2 * total * depth * rows,
            bytes_accessed=4 * depth * rows + 4 * table.size + 4 * total * rows,
            transcendentals=0,
        ),
        name="transform",
    )(table, *samples, *after)


def merge_kernel(count, groups, piece, near_ref, far_ref, *refs):
    out_refs = refs[-count:]
    odd = lax.axis_index("chan") % 2 == 1
    lower = lax.broadcasted_iota(jnp.int32, (groups, BLOCK), 1) < BLOCK // 2
    for unit, out_ref in enumerate(out_refs):
        for channel in range(piece):
            for part in range(2):
                rows = pl.ds((unit * 2 + part) * groups * piece + channel, groups, stride=piece)
                near = near_ref[rows, :]
                far = far_ref[rows, :]
                first = jnp.where(odd, far, near)
                second = jnp.where(odd, near, far)
                at = part * 2 * groups
                out_ref[channel, at : at + groups] = jnp.where(
                    lower, first, pltpu.roll(second, BLOCK // 2, 1)
                )
                out_ref[channel, at + groups : at + 2 * groups] = jnp.where(
                    lower, pltpu.roll(first, BLOCK // 2, 1), second
                )


def merged(near, far, after):
    count, _, groups, piece, lanes = near.shape
    flat = (count * 2 * groups * piece, lanes)
    return pl.pallas_call(
        functools.partial(merge_kernel, count, groups, piece),
        in_specs=[pl.BlockSpec(memory_space=pltpu.VMEM)] * 2
        + [pl.BlockSpec(memory_space=pl.ANY)] * len(after),
        out_specs=[pl.BlockSpec(memory_space=pltpu.VMEM)] * count,
        out_shape=[jax.ShapeDtypeStruct((piece, 4 * groups, lanes), F32)] * count,
        compiler_params=params(),
        cost_estimate=pl.CostEstimate(
            flops=4 * near.size, bytes_accessed=16 * near.size, transcendentals=0
        ),
        name="merge",
    )(near.reshape(flat), far.reshape(flat), *after)


def pack_kernel(counts, *refs):
    sources = iter(refs)
    for count, out_ref in zip(counts, refs[-len(counts) :]):
        for index in range(count):
            out_ref[index] = next(sources)[...]


def packed(batches, after):
    counts = [len(batch) for batch in batches]
    values = [value for batch in batches for value in batch]
    width = 8

    def spec(shape):
        lead = shape[:-3]
        return pl.BlockSpec(
            lead + (min(width, shape[-3]),) + shape[-2:], lambda i: (0,) * len(lead) + (i, 0, 0)
        )

    shapes = [(len(batch),) + batch[0].shape for batch in batches]
    return pl.pallas_call(
        functools.partial(pack_kernel, counts),
        grid=(values[0].shape[-3] // min(width, values[0].shape[-3]),),
        in_specs=[spec(value.shape) for value in values]
        + [pl.BlockSpec(memory_space=pl.ANY)] * len(after),
        out_specs=[spec(shape) for shape in shapes],
        out_shape=[jax.ShapeDtypeStruct(shape, F32) for shape in shapes],
        compiler_params=params(),
        cost_estimate=pl.CostEstimate(
            flops=0, bytes_accessed=8 * sum(value.size for value in values), transcendentals=0
        ),
        name="pack",
    )(*values, *after)


def dot_columns(left, right):
    return lax.dot_general(left, right, (((0,), (0,)), ((), ())), preferred_element_type=F32)


def correlate_kernel(slots, tiles, order, slot_ref, blocks_ref, *refs):
    unit_refs = []
    for ref in refs[:-5]:
        if len(ref.shape) == 4:
            unit_refs.append(ref)
        elif len(ref.shape) == 5 and len(unit_refs) < tiles:
            unit_refs += [ref.at[0], ref.at[1]]
    out_ref, done_ref, high_ref, low_ref, place_ref = refs[-5:]
    done_ref[...] = jnp.zeros(done_ref.shape, F32)
    blocks, width, depth, _ = unit_refs[0].shape
    rows = depth // 2
    half = tiles * rows

    @pl.when(pl.program_id(0) == 0)
    def _():
        first_slot = lax.axis_index("tile") * slots
        for slot in range(slots):
            row = jnp.int32(0)
            col = jnp.int32(0)
            present = jnp.int32(0)
            for tile in range(slot_ref.shape[0]):
                match = (slot_ref[tile] == first_slot + slot).astype(jnp.int32)
                row = row + match * blocks_ref[2 * tile]
                col = col + match * blocks_ref[2 * tile + 1]
                present = present + match
            place_ref[3 * slot] = row
            place_ref[3 * slot + 1] = col
            place_ref[3 * slot + 2] = present

    own = lax.axis_index("chan") // 2
    for channel in range(width):
        for mask in range(blocks):
            block = own ^ order[mask]
            for part in range(2):
                joined = jnp.concatenate(
                    [
                        unit_ref[mask, channel, part * rows : (part + 1) * rows]
                        for unit_ref in unit_refs
                    ],
                    axis=0,
                )
                high, low = split(joined)
                high_ref[channel, block, part * half : (part + 1) * half] = high
                low_ref[channel, block, part * half : (part + 1) * half] = low
        for slot in range(slots):
            row = place_ref[3 * slot]
            col = place_ref[3 * slot + 1]
            weight = place_ref[3 * slot + 2].astype(F32)
            row_high = high_ref[channel, row]
            row_low = low_ref[channel, row]
            col_high = high_ref[channel, col]
            col_low = low_ref[channel, col]
            turned_high = jnp.concatenate([-col_high[half:], col_high[:half]], axis=0)
            turned_low = jnp.concatenate([-col_low[half:], col_low[:half]], axis=0)
            right_high = jnp.concatenate([col_high, turned_high], axis=1)
            right_low = jnp.concatenate([col_low, turned_low], axis=1)
            value = dot_columns(
                jnp.concatenate([row_high, row_low], axis=0),
                jnp.concatenate([right_high, right_high], axis=0),
            ) + dot_columns(row_high, right_low)
            value = value * weight
            out_ref[slot, channel, 0] = value[:, :BLOCK]
            out_ref[slot, channel, 1] = value[:, BLOCK:]


def correlated(order, tile_slot, tile_blocks, units, visibility, residue, first, total, slots):
    tiles = sum(1 if unit.ndim == 4 else unit.shape[0] for unit in units)
    blocks, piece, depth, lanes = units[0].shape
    width = 4
    out = jax.ShapeDtypeStruct((slots, total, RADIX, 2, BLOCK, BLOCK), F32)
    operands = [tile_slot, tile_blocks.reshape(-1)] + units
    in_specs = [
        pl.BlockSpec((blocks, width, depth, lanes), lambda i, *_: (0, i, 0, 0))
        if unit.ndim == 4
        else pl.BlockSpec(unit.shape[:2] + (width, depth, lanes), lambda i, *_: (0, 0, i, 0, 0))
        for unit in units
    ]
    aliases = {}
    if visibility is not None:
        operands.append(visibility)
        in_specs.append(pl.BlockSpec(memory_space=pl.ANY))
        aliases = {len(operands) - 1: 0}
    return pl.pallas_call(
        functools.partial(correlate_kernel, slots, tiles, order),
        grid_spec=pltpu.PrefetchScalarGridSpec(
            num_scalar_prefetch=2,
            grid=(piece // width,),
            in_specs=in_specs,
            out_specs=[
                pl.BlockSpec(
                    (slots, width, None, 2, BLOCK, BLOCK), lambda i, *_: (0, first // width + i, residue, 0, 0, 0)
                ),
                pl.BlockSpec((8, BLOCK), lambda i, *_: (0, 0)),
            ],
            scratch_shapes=[pltpu.VMEM((width, blocks, tiles * depth, lanes), BF16)] * 2
            + [pltpu.SMEM((3 * slots,), jnp.int32)],
        ),
        out_shape=[out, jax.ShapeDtypeStruct((8, BLOCK), F32)],
        input_output_aliases=aliases,
        compiler_params=params(),
        cost_estimate=pl.CostEstimate(
            flops=3 * 2 * slots * piece * tiles * depth * BLOCK * 2 * BLOCK,
            bytes_accessed=4 * piece * lanes * (tiles * blocks * depth + slots * 2 * BLOCK),
            transcendentals=0,
        ),
        name="correlate",
    )(*operands)


def body(voltage, fir_taps, tile_slot, tile_blocks):
    _, frames, inputs, length = voltage.shape
    tap_count = fir_taps.shape[0]
    owners = lax.axis_size("chan")
    tiles = lax.axis_size("tile")
    channels = length // owners
    blocks = owners // 2
    slots = -(-tile_blocks.shape[0] // tiles)
    scale = 1.0 / math.sqrt(length * frames * tiles)
    table = jnp.asarray(fourier_table(length // RADIX, owners, scale))

    following = shifted(voltage[:, : tap_count - 1], "tile", -1)
    samples = filtered_samples(voltage, following, fir_taps)

    order = list(range(2, blocks)) + [1, 0]
    groups = [tuple(2 * block + x for block in order) for x in range(2)]
    halves = 2
    size = channels // RADIX // halves
    count = RADIX * halves
    near, away, units = [None] * count, [None] * count, [None] * count

    def spectra(residue, after):
        values = transformed(groups, halves, table, samples[residue], after)
        for half in range(halves):
            piece = residue * halves + half
            near[piece] = values[half]
            away[piece] = swapped(values[halves + half], "chan", 1)

    def merge(piece, after):
        units[piece] = merged(near[piece], away[piece], after)

    def along(piece):
        return [
            swapped(unit, "chan", 2 * block) if block else unit
            for block, unit in zip(order, units[piece])
        ]

    spectra(0, [])
    for residue in range(2, RADIX):
        spectra(residue, [])
    merge(0, near[2 * halves :: halves])
    turned = along(0)
    spectra(1, turned[-2:-1])
    for piece in range(1, count):
        merge(piece, [])

    def products(piece, arrays, visibility):
        return correlated(
            order, tile_slot, tile_blocks, arrays, visibility,
            piece // halves, piece % halves * size, channels // RADIX, slots,
        )

    visibility = None
    finished = []
    pair = None
    for piece in range(count):
        after = [unit[0] for unit in units[piece + 1 : piece + 3 if piece else 2]]
        after += [] if piece else near[halves : halves + 1]
        after += finished[piece - 2 : piece - 1] if piece >= 2 else []
        own, *both = packed([turned] + ([pair] if pair else []), after)
        if piece + 1 < count:
            turned = along(piece + 1)
        across = swapped(own, "tile", 2)
        if pair:
            arrays = pair + [swapped(both[0], "tile", 1)]
            visibility, token = products(piece - 1, arrays, visibility)
            finished.append(token)
        pair = [own, across]
    (last,) = packed([[across]], finished[-1:])
    arrays = pair + [swapped(own, "tile", 1), swapped(last[0], "tile", 1)]
    visibility, _ = products(count - 1, arrays, visibility)
    return visibility.reshape(slots, channels, 2, BLOCK, BLOCK)


def solution(mesh):
    in_specs = (P(None, "tile", "chan", None), P(), P(), P())
    out_specs = P("tile", "chan", None, None, None)
    owners, tiles = mesh.shape["chan"], mesh.shape["tile"]

    def run(voltage, fir_taps, tile_slot, tile_blocks):
        paired = 2 * voltage.shape[2] == BLOCK * owners and tiles == 4
        chosen = body if paired else generic_body
        return jax.shard_map(
            chosen, mesh=mesh, in_specs=in_specs, out_specs=out_specs, check_vma=False
        )(voltage, fir_taps, tile_slot, tile_blocks)

    return run
```

```python
import functools
import math

import jax
import jax.numpy as jnp
import numpy as np
from jax import lax
from jax.experimental import pallas as pl
from jax.experimental.pallas import tpu as pltpu
from jax.sharding import PartitionSpec as P

BLOCK = 128
RADIX = 4
STEP = 256
VMEM_BYTES = 20 * 1024 * 1024
BF16 = jnp.bfloat16
F32 = jnp.float32


def shifted(value, axis, steps):
    count = lax.axis_size(axis)
    initial, last = (max(0, -steps), min(count, count - steps))
    return lax.ppermute(value, axis, [(source, source + steps) for source in range(initial, last)])


def swapped(value, axis, mask):
    count = lax.axis_size(axis)
    return lax.ppermute(value, axis, [(source, source ^ mask) for source in range(count)])


def params():
    return pltpu.CompilerParams(vmem_limit_bytes=VMEM_BYTES)


def split(value):
    high = value.astype(BF16)
    return high, (value - high.astype(F32)).astype(BF16)


def filter_frames(voltage, fir_taps):
    tap_count = fir_taps.shape[0]
    frames = voltage.shape[1]
    history = shifted(voltage[:, : tap_count - 1], "tile", -1)
    extended = jnp.concatenate([voltage, history], axis=1)
    filtered = jnp.zeros(voltage.shape, jnp.float32)
    for tap_index in range(tap_count):
        filtered = (
            filtered
            + fir_taps[tap_index][None, None, None, :] * extended[:, tap_index : tap_index + frames]
        )
    return filtered


def transform(filtered):
    channel_count = filtered.shape[3]
    row_count = filtered.shape[1] * filtered.shape[2]
    position = lax.broadcasted_iota(jnp.int32, (channel_count, channel_count), 0)
    frequency = lax.broadcasted_iota(jnp.int32, (channel_count, channel_count), 1)
    phase_angle = (position * frequency % channel_count).astype(jnp.float32) * (
        2.0 * math.pi / channel_count
    )
    factor = 1.0 / math.sqrt(channel_count)
    cosine = jnp.cos(phase_angle) * factor
    sine_table = jnp.sin(phase_angle) * factor
    samples = filtered.reshape(2 * row_count, channel_count)
    cos_part = jnp.dot(
        cosine, samples.T, precision=lax.Precision.HIGHEST, preferred_element_type=jnp.float32
    )
    sin_part = jnp.dot(
        sine_table, samples.T, precision=lax.Precision.HIGHEST, preferred_element_type=jnp.float32
    )
    real_part = cos_part[:, :row_count] + sin_part[:, row_count:]
    imag_part = cos_part[:, row_count:] - sin_part[:, :row_count]
    joined = jnp.concatenate([real_part, imag_part], axis=1)
    return joined.reshape(channel_count, 2, filtered.shape[1], filtered.shape[2])


def tile_product(gathered, row_block, col_block, block_width):
    left_block = lax.dynamic_slice_in_dim(gathered, row_block * block_width, block_width, 3)
    right_block = lax.dynamic_slice_in_dim(gathered, col_block * block_width, block_width, 3)
    channel_count = gathered.shape[0]
    depth = 2 * gathered.shape[2]
    left_real = left_block.reshape(channel_count, depth, block_width)
    left_imag = jnp.concatenate([left_block[:, 1], -left_block[:, 0]], axis=1)
    left_both = jnp.concatenate([left_real, left_imag], axis=2)
    right_both = right_block.reshape(channel_count, depth, block_width)
    return jnp.einsum(
        "cki,ckj->cij",
        left_both,
        right_both,
        precision=lax.Precision.HIGHEST,
        preferred_element_type=jnp.float32,
    )


def own_slots(tile_slot, tile_blocks, slot_count):
    first_slot = lax.axis_index("tile") * slot_count
    row_blocks = []
    col_blocks = []
    present = []
    for slot_index in range(slot_count):
        matches = (tile_slot == first_slot + slot_index).astype(jnp.int32)
        row_blocks.append(jnp.sum(matches * tile_blocks[:, 0]))
        col_blocks.append(jnp.sum(matches * tile_blocks[:, 1]))
        present.append(jnp.sum(matches))
    return row_blocks, col_blocks, present


def generic_body(voltage, fir_taps, tile_slot, tile_blocks):
    spectra = transform(filter_frames(voltage, fir_taps))
    tile_count = tile_blocks.shape[0]
    tile_size = lax.axis_size("tile")
    slot_count = (tile_count + tile_size - 1) // tile_size
    turned = lax.all_to_all(spectra, "chan", split_axis=0, concat_axis=3, tiled=True)
    spectra_total = turned.shape[2] * tile_size
    row_blocks, col_blocks, present = own_slots(tile_slot, tile_blocks, slot_count)
    portion = lax.all_gather(turned, "tile", axis=2, tiled=True)
    summed = jnp.stack(
        [
            tile_product(portion, row_blocks[slot_index], col_blocks[slot_index], BLOCK)
            for slot_index in range(slot_count)
        ]
    )
    weights = jnp.stack(present).astype(F32)[:, None, None, None] / spectra_total
    return (summed * weights).reshape(slot_count, turned.shape[0], 2, BLOCK, BLOCK)


def fourier_table(points, owners, scale):
    phase = np.outer(np.arange(points), np.arange(points)) % points
    angle = phase * (2.0 * math.pi / points)
    cosine = np.cos(angle) * scale
    sine = np.sin(angle) * scale
    both = np.stack([np.concatenate([cosine, sine], 1), np.concatenate([-sine, cosine], 1)], 0)
    both = both.reshape(2, owners, points // owners, 2 * points).transpose(1, 0, 2, 3)
    return both.reshape(owners, -1, 2 * points).astype(np.float32)


def twiddle_table(length):
    angle = np.outer(np.arange(1, RADIX), np.arange(length // RADIX)) * (2.0 * math.pi / length)
    return np.stack([np.cos(angle), np.sin(angle)], 1).reshape(-1, length // RADIX).astype(np.float32)


def filter_kernel(frames, voltage_ref, next_ref, taps_ref, twiddle_ref, *refs):
    out_refs = refs[-2 * RADIX :]
    tap_count, length = taps_ref.shape
    held = voltage_ref.shape[1]
    points = length // RADIX

    def quarter(part, frame, index):
        lanes = slice(index * points, (index + 1) * points)
        total = None
        for tap in range(tap_count):
            at = frame + tap
            source = voltage_ref[part, at, :, lanes] if at < held else next_ref[part, at - held, :, lanes]
            term = source * taps_ref[pl.ds(tap, 1), lanes]
            total = term if total is None else total + term
        return total

    for frame in range(frames):
        real = [quarter(0, frame, index) for index in range(RADIX)]
        imag = [quarter(1, frame, index) for index in range(RADIX)]
        even_real, odd_real = real[0] + real[2], real[1] + real[3]
        even_imag, odd_imag = imag[0] + imag[2], imag[1] + imag[3]
        left_real, right_real = real[0] - real[2], real[1] - real[3]
        left_imag, right_imag = imag[0] - imag[2], imag[1] - imag[3]
        residues = [
            (even_real + odd_real, even_imag + odd_imag),
            (left_real + right_imag, left_imag - right_real),
            (even_real - odd_real, even_imag - odd_imag),
            (left_real - right_imag, left_imag + right_real),
        ]
        for index, (re, im) in enumerate(residues):
            if index:
                cosine = twiddle_ref[pl.ds(2 * index - 2, 1), :]
                sine = twiddle_ref[pl.ds(2 * index - 1, 1), :]
                re, im = re * cosine + im * sine, im * cosine - re * sine
            for part, value in enumerate((re, im)):
                high, low = split(value)
                lanes = slice(part * points, (part + 1) * points)
                out_refs[2 * index][frame, :, lanes] = high
                out_refs[2 * index + 1][frame, :, lanes] = low


def filtered_samples(voltage, following, fir_taps, late, earlier, after):
    _, frames, inputs, length = voltage.shape
    width = 16
    depth = 2 * length // RADIX
    twiddles = jnp.asarray(twiddle_table(length))
    out = jax.ShapeDtypeStruct((frames, inputs, depth), BF16)
    if earlier:
        count, held, place = late, late, frames // late - 1
    else:
        count, held, place = frames - late, frames, 0
    others = list(earlier) + list(after)
    return pl.pallas_call(
        functools.partial(filter_kernel, count),
        grid=(inputs // width,),
        in_specs=[
            pl.BlockSpec((2, held, width, length), lambda i: (0, place, i, 0)),
            pl.BlockSpec((2, following.shape[1], width, length), lambda i: (0, 0, i, 0)),
            pl.BlockSpec(fir_taps.shape, lambda i: (0, 0)),
            pl.BlockSpec(twiddles.shape, lambda i: (0, 0)),
        ]
        + [pl.BlockSpec(memory_space=pl.ANY)] * len(others),
        out_specs=[pl.BlockSpec((count, width, depth), lambda i: (place, i, 0))] * (2 * RADIX),
        out_shape=[out] * (2 * RADIX),
        input_output_aliases={4 + index: index for index in range(len(earlier))},
        compiler_params=params(),
        cost_estimate=pl.CostEstimate(
            flops=16 * voltage.size * count // frames,
            bytes_accessed=8 * voltage.size * count // frames,
            transcendentals=0,
        ),
        name="filter",
    )(voltage, following, fir_taps, twiddles, *others)


def dot_rows(left, right):
    return lax.dot_general(left, right, (((1,), (1,)), ((), ())), preferred_element_type=F32)


def transform_kernel(groups, pieces, table_ref, xh_ref, xl_ref, *refs):
    out_refs, (th_ref, tl_ref) = refs[-2 - len(groups) * pieces : -2], refs[-2:]
    height = table_ref.shape[1]
    masks = [mask for group in groups for mask in group]

    @pl.when(pl.program_id(0) == 0)
    def _():
        me = lax.axis_index("chan")
        for index, mask in enumerate(masks):
            rows = slice(index * height, (index + 1) * height)
            th_ref[rows], tl_ref[rows] = split(table_ref[me ^ mask])

    high = xh_ref[...]
    result = dot_rows(th_ref[...], high) + dot_rows(th_ref[...], xl_ref[...])
    result = result + dot_rows(tl_ref[...], high)
    count = height // 2
    size = count // pieces
    places = [(which, at) for which, group in enumerate(groups) for at in range(len(group))]
    for index, (which, at) in enumerate(places):
        for part in range(2):
            for piece in range(pieces):
                first = index * height + part * count + piece * size
                for column in range(result.shape[1] // BLOCK):
                    out_refs[which * pieces + piece][at, part, column] = result[
                        first : first + size, column * BLOCK : (column + 1) * BLOCK
                    ]


def transformed(groups, pieces, table, samples, after, first, last):
    depth = samples[0].shape[1]
    owners, height, _ = table.shape
    size = height // 2 // pieces
    step = STEP
    rows = (last - first) * step
    row_spec = pl.BlockSpec((step, depth), lambda i: (first + i, 0))
    total = sum(map(len, groups)) * height
    counts = [len(group) for group in groups for _ in range(pieces)]
    return pl.pallas_call(
        functools.partial(transform_kernel, groups, pieces),
        grid=(rows // step,),
        in_specs=[pl.BlockSpec(table.shape, lambda i: (0, 0, 0)), row_spec, row_spec]
        + [pl.BlockSpec(memory_space=pl.ANY)] * len(after),
        out_specs=[
            pl.BlockSpec((count, 2, step // BLOCK, size, BLOCK), lambda i: (0, 0, i, 0, 0))
            for count in counts
        ],
        out_shape=[
            jax.ShapeDtypeStruct((count, 2, rows // BLOCK, size, BLOCK), F32) for count in counts
        ],
        scratch_shapes=[pltpu.VMEM((total, depth), BF16)] * 2,
        compiler_params=params(),
        cost_estimate=pl.CostEstimate(
            flops=3 * 2 * total * depth * rows,
            bytes_accessed=4 * depth * rows + 4 * table.size + 4 * total * rows,
            transcendentals=0,
        ),
        name="transform",
    )(table, *samples, *after)


def merge_kernel(count, groups, piece, *refs):
    near_refs, far_refs, out_refs = refs[: len(groups)], refs[len(groups) : 2 * len(groups)], refs[-count:]
    total = sum(groups)
    odd = lax.axis_index("chan") % 2 == 1
    lower = lax.broadcasted_iota(jnp.int32, (total, BLOCK), 1) < BLOCK // 2
    for unit, out_ref in enumerate(out_refs):
        for channel in range(piece):
            for part in range(2):

                def rows_of(segment_refs):
                    rows = [
                        ref[pl.ds((unit * 2 + part) * held * piece + channel, held, stride=piece), :]
                        for ref, held in zip(segment_refs, groups)
                    ]
                    return rows[0] if len(rows) == 1 else jnp.concatenate(rows, axis=0)

                near, far = rows_of(near_refs), rows_of(far_refs)
                first = jnp.where(odd, far, near)
                second = jnp.where(odd, near, far)
                at = part * 2 * total
                out_ref[channel, at : at + total] = jnp.where(
                    lower, first, pltpu.roll(second, BLOCK // 2, 1)
                )
                out_ref[channel, at + total : at + 2 * total] = jnp.where(
                    lower, pltpu.roll(first, BLOCK // 2, 1), second
                )


def merged(near, far, after):
    count, _, _, piece, lanes = near[0].shape
    groups = [value.shape[2] for value in near]
    size = sum(value.size for value in near)
    return pl.pallas_call(
        functools.partial(merge_kernel, count, groups, piece),
        in_specs=[pl.BlockSpec(memory_space=pltpu.VMEM)] * (2 * len(near))
        + [pl.BlockSpec(memory_space=pl.ANY)] * len(after),
        out_specs=[pl.BlockSpec(memory_space=pltpu.VMEM)] * count,
        out_shape=[jax.ShapeDtypeStruct((piece, 4 * sum(groups), lanes), F32)] * count,
        compiler_params=params(),
        cost_estimate=pl.CostEstimate(flops=4 * size, bytes_accessed=16 * size, transcendentals=0),
        name="merge",
    )(*[value.reshape(-1, lanes) for value in list(near) + list(far)], *after)


def pack_kernel(counts, *refs):
    sources = iter(refs)
    for count, out_ref in zip(counts, refs[-len(counts) :]):
        for index in range(count):
            out_ref[index] = next(sources)[...]


def packed(batches, after):
    counts = [len(batch) for batch in batches]
    values = [value for batch in batches for value in batch]
    width = 8

    def spec(shape):
        lead = shape[:-3]
        return pl.BlockSpec(
            lead + (min(width, shape[-3]),) + shape[-2:], lambda i: (0,) * len(lead) + (i, 0, 0)
        )

    shapes = [(len(batch),) + batch[0].shape for batch in batches]
    return pl.pallas_call(
        functools.partial(pack_kernel, counts),
        grid=(values[0].shape[-3] // min(width, values[0].shape[-3]),),
        in_specs=[spec(value.shape) for value in values]
        + [pl.BlockSpec(memory_space=pl.ANY)] * len(after),
        out_specs=[spec(shape) for shape in shapes],
        out_shape=[jax.ShapeDtypeStruct(shape, F32) for shape in shapes],
        compiler_params=params(),
        cost_estimate=pl.CostEstimate(
            flops=0, bytes_accessed=8 * sum(value.size for value in values), transcendentals=0
        ),
        name="pack",
    )(*values, *after)


def dot_columns(left, right):
    return lax.dot_general(left, right, (((0,), (0,)), ((), ())), preferred_element_type=F32)


def correlate_kernel(slots, tiles, order, slot_ref, blocks_ref, *refs):
    unit_refs = []
    for ref in refs[:-5]:
        if len(ref.shape) == 4:
            unit_refs.append(ref)
        elif len(ref.shape) == 5 and len(unit_refs) < tiles:
            unit_refs += [ref.at[0], ref.at[1]]
    out_ref, done_ref, high_ref, low_ref, place_ref = refs[-5:]
    done_ref[...] = jnp.zeros(done_ref.shape, F32)
    blocks, width, depth, _ = unit_refs[0].shape
    rows = depth // 2
    half = tiles * rows

    @pl.when(pl.program_id(0) == 0)
    def _():
        first_slot = lax.axis_index("tile") * slots
        for slot in range(slots):
            row = jnp.int32(0)
            col = jnp.int32(0)
            present = jnp.int32(0)
            for tile in range(slot_ref.shape[0]):
                match = (slot_ref[tile] == first_slot + slot).astype(jnp.int32)
                row = row + match * blocks_ref[2 * tile]
                col = col + match * blocks_ref[2 * tile + 1]
                present = present + match
            place_ref[3 * slot] = row
            place_ref[3 * slot + 1] = col
            place_ref[3 * slot + 2] = present

    own = lax.axis_index("chan") // 2
    for channel in range(width):
        for mask in range(blocks):
            block = own ^ order[mask]
            for part in range(2):
                joined = jnp.concatenate(
                    [
                        unit_ref[mask, channel, part * rows : (part + 1) * rows]
                        for unit_ref in unit_refs
                    ],
                    axis=0,
                )
                high, low = split(joined)
                high_ref[channel, block, part * half : (part + 1) * half] = high
                low_ref[channel, block, part * half : (part + 1) * half] = low
        for slot in range(slots):
            row = place_ref[3 * slot]
            col = place_ref[3 * slot + 1]
            weight = place_ref[3 * slot + 2].astype(F32)
            row_high = high_ref[channel, row]
            row_low = low_ref[channel, row]
            col_high = high_ref[channel, col]
            col_low = low_ref[channel, col]
            turned_high = jnp.concatenate([-col_high[half:], col_high[:half]], axis=0)
            turned_low = jnp.concatenate([-col_low[half:], col_low[:half]], axis=0)
            right_high = jnp.concatenate([col_high, turned_high], axis=1)
            right_low = jnp.concatenate([col_low, turned_low], axis=1)
            value = dot_columns(
                jnp.concatenate([row_high, row_low], axis=0),
                jnp.concatenate([right_high, right_high], axis=0),
            ) + dot_columns(row_high, right_low)
            value = value * weight
            out_ref[slot, channel, 0] = value[:, :BLOCK]
            out_ref[slot, channel, 1] = value[:, BLOCK:]


def correlated(order, tile_slot, tile_blocks, units, visibility, residue, first, total, slots):
    tiles = sum(1 if unit.ndim == 4 else unit.shape[0] for unit in units)
    blocks, piece, depth, lanes = units[0].shape
    width = 4
    out = jax.ShapeDtypeStruct((slots, total, RADIX, 2, BLOCK, BLOCK), F32)
    operands = [tile_slot, tile_blocks.reshape(-1)] + units
    in_specs = [
        pl.BlockSpec((blocks, width, depth, lanes), lambda i, *_: (0, i, 0, 0))
        if unit.ndim == 4
        else pl.BlockSpec(unit.shape[:2] + (width, depth, lanes), lambda i, *_: (0, 0, i, 0, 0))
        for unit in units
    ]
    aliases = {}
    if visibility is not None:
        operands.append(visibility)
        in_specs.append(pl.BlockSpec(memory_space=pl.ANY))
        aliases = {len(operands) - 1: 0}
    return pl.pallas_call(
        functools.partial(correlate_kernel, slots, tiles, order),
        grid_spec=pltpu.PrefetchScalarGridSpec(
            num_scalar_prefetch=2,
            grid=(piece // width,),
            in_specs=in_specs,
            out_specs=[
                pl.BlockSpec(
                    (slots, width, None, 2, BLOCK, BLOCK), lambda i, *_: (0, first // width + i, residue, 0, 0, 0)
                ),
                pl.BlockSpec((8, BLOCK), lambda i, *_: (0, 0)),
            ],
            scratch_shapes=[pltpu.VMEM((width, blocks, tiles * depth, lanes), BF16)] * 2
            + [pltpu.SMEM((3 * slots,), jnp.int32)],
        ),
        out_shape=[out, jax.ShapeDtypeStruct((8, BLOCK), F32)],
        input_output_aliases=aliases,
        compiler_params=params(),
        cost_estimate=pl.CostEstimate(
            flops=3 * 2 * slots * piece * tiles * depth * BLOCK * 2 * BLOCK,
            bytes_accessed=4 * piece * lanes * (tiles * blocks * depth + slots * 2 * BLOCK),
            transcendentals=0,
        ),
        name="correlate",
    )(*operands)


def body(voltage, fir_taps, tile_slot, tile_blocks):
    _, frames, inputs, length = voltage.shape
    tap_count = fir_taps.shape[0]
    owners = lax.axis_size("chan")
    tiles = lax.axis_size("tile")
    channels = length // owners
    blocks = owners // 2
    slots = -(-tile_blocks.shape[0] // tiles)
    scale = 1.0 / math.sqrt(length * frames * tiles)
    table = jnp.asarray(fourier_table(length // RADIX, owners, scale))

    order = list(range(2, blocks)) + [1, 0]
    groups = [tuple(2 * block + x for block in order) for x in range(2)]
    halves = 2
    size = channels // RADIX // halves
    count = RADIX * halves
    near = [[] for _ in range(count)]
    share = [[] for _ in range(count)]
    away = [None] * count
    units = [None] * count
    paired = [None] * count

    steps = frames * inputs // STEP
    late = STEP // inputs
    following = shifted(voltage[:, : tap_count - 1], "tile", -1)
    early = filtered_samples(voltage, voltage[:, : tap_count - 1], fir_taps, late, [], [])

    def spectra(samples, residue, after, first, last):
        rows = [value.reshape(frames * inputs, -1) for value in samples[2 * residue : 2 * residue + 2]]
        values = transformed(groups, halves, table, rows, after, first, last)
        for half in range(halves):
            near[residue * halves + half].append(values[half])
            share[residue * halves + half].append(values[halves + half])

    spectra(early, 0, [], 0, steps - 1)
    samples = filtered_samples(voltage, following, fir_taps, late, early, [near[0][0]])
    spectra(samples, 0, [], steps - 1, steps)
    spectra(samples, 1, [], 0, steps)

    def leave(piece):
        values = share[piece]
        if 0 < piece < 4:
            after = [away[piece - 1][-1]]
            values = [packed([[value]], after)[0].reshape(value.shape) for value in values]
        away[piece] = [swapped(value, "chan", 1) for value in values]

    def merge(piece, after):
        units[piece] = merged(near[piece], away[piece], after)

    def along(piece):
        return [
            swapped(unit, "chan", 2 * block) if block else unit
            for block, unit in zip(order, units[piece])
        ]

    leave(0)
    merge(0, near[halves][:1])
    turned = along(0)
    for residue in range(2, RADIX):
        spectra(samples, residue, turned[-2:-1], 0, steps)
    leave(1)
    merge(1, [])
    leave(2)

    def products(piece, arrays, visibility):
        return correlated(
            order, tile_slot, tile_blocks, arrays, visibility,
            piece // halves, piece % halves * size, channels // RADIX, slots,
        )

    visibility = None
    finished = []
    pair = None
    for piece in range(count):
        if piece:
            after = [pair[1]]
            for later in range(piece + 1, min(piece + 3, count)):
                if units[later] is None:
                    merge(later, [])
                after.append(units[later][0])
        else:
            after = [units[1][0]] + [near[residue * halves][0] for residue in range(2, RADIX)]
        after += finished[piece - 2 : piece - 1] if piece >= 2 else []
        (own,) = packed([turned], after)
        if piece + 1 < count:
            turned = along(piece + 1)
        across = swapped(own, "tile", 2)
        if piece + 3 < count:
            leave(piece + 3)
        if pair:
            (both,) = packed([pair], [own] + (away[piece + 3][-1:] if piece + 3 < count else []))
            paired[piece - 1] = swapped(both, "tile", 1)
            visibility, token = products(piece - 1, pair + [paired[piece - 1]], visibility)
            finished.append(token)
        pair = [own, across]
    (last,) = packed([[across]], finished[-1:])
    arrays = pair + [swapped(own, "tile", 1), swapped(last[0], "tile", 1)]
    visibility, _ = products(count - 1, arrays, visibility)
    return visibility.reshape(slots, channels, 2, BLOCK, BLOCK)


def solution(mesh):
    in_specs = (P(None, "tile", "chan", None), P(), P(), P())
    out_specs = P("tile", "chan", None, None, None)
    owners, tiles = mesh.shape["chan"], mesh.shape["tile"]

    def run(voltage, fir_taps, tile_slot, tile_blocks):
        paired = 2 * voltage.shape[2] == BLOCK * owners and tiles == 4
        chosen = body if paired else generic_body
        return jax.shard_map(
            chosen, mesh=mesh, in_specs=in_specs, out_specs=out_specs, check_vma=False
        )(voltage, fir_taps, tile_slot, tile_blocks)

    return run
```

```python
import functools
import math

import jax
import jax.numpy as jnp
import numpy as np
from jax import lax
from jax.experimental import pallas as pl
from jax.experimental.pallas import tpu as pltpu
from jax.sharding import PartitionSpec as P

BLOCK = 128
RADIX = 4
STEP = 256
HALF = 2
LONG = 2_000_000_000_000
VMEM_BYTES = 20 * 1024 * 1024
BF16 = jnp.bfloat16
F32 = jnp.float32


def shifted(value, axis, steps):
    count = lax.axis_size(axis)
    initial, last = (max(0, -steps), min(count, count - steps))
    return lax.ppermute(value, axis, [(source, source + steps) for source in range(initial, last)])


def swapped(value, axis, mask):
    count = lax.axis_size(axis)
    return lax.ppermute(value, axis, [(source, source ^ mask) for source in range(count)])


def params():
    return pltpu.CompilerParams(vmem_limit_bytes=VMEM_BYTES)


def split(value):
    high = value.astype(BF16)
    return high, (value - high.astype(F32)).astype(BF16)


def filter_frames(voltage, fir_taps):
    tap_count = fir_taps.shape[0]
    frames = voltage.shape[1]
    history = shifted(voltage[:, : tap_count - 1], "tile", -1)
    extended = jnp.concatenate([voltage, history], axis=1)
    filtered = jnp.zeros(voltage.shape, jnp.float32)
    for tap_index in range(tap_count):
        filtered = (
            filtered
            + fir_taps[tap_index][None, None, None, :] * extended[:, tap_index : tap_index + frames]
        )
    return filtered


def transform(filtered):
    channel_count = filtered.shape[3]
    row_count = filtered.shape[1] * filtered.shape[2]
    position = lax.broadcasted_iota(jnp.int32, (channel_count, channel_count), 0)
    frequency = lax.broadcasted_iota(jnp.int32, (channel_count, channel_count), 1)
    phase_angle = (position * frequency % channel_count).astype(jnp.float32) * (
        2.0 * math.pi / channel_count
    )
    factor = 1.0 / math.sqrt(channel_count)
    cosine = jnp.cos(phase_angle) * factor
    sine_table = jnp.sin(phase_angle) * factor
    samples = filtered.reshape(2 * row_count, channel_count)
    cos_part = jnp.dot(
        cosine, samples.T, precision=lax.Precision.HIGHEST, preferred_element_type=jnp.float32
    )
    sin_part = jnp.dot(
        sine_table, samples.T, precision=lax.Precision.HIGHEST, preferred_element_type=jnp.float32
    )
    real_part = cos_part[:, :row_count] + sin_part[:, row_count:]
    imag_part = cos_part[:, row_count:] - sin_part[:, :row_count]
    joined = jnp.concatenate([real_part, imag_part], axis=1)
    return joined.reshape(channel_count, 2, filtered.shape[1], filtered.shape[2])


def tile_product(gathered, row_block, col_block, block_width):
    left_block = lax.dynamic_slice_in_dim(gathered, row_block * block_width, block_width, 3)
    right_block = lax.dynamic_slice_in_dim(gathered, col_block * block_width, block_width, 3)
    channel_count = gathered.shape[0]
    depth = 2 * gathered.shape[2]
    left_real = left_block.reshape(channel_count, depth, block_width)
    left_imag = jnp.concatenate([left_block[:, 1], -left_block[:, 0]], axis=1)
    left_both = jnp.concatenate([left_real, left_imag], axis=2)
    right_both = right_block.reshape(channel_count, depth, block_width)
    return jnp.einsum(
        "cki,ckj->cij",
        left_both,
        right_both,
        precision=lax.Precision.HIGHEST,
        preferred_element_type=jnp.float32,
    )


def own_slots(tile_slot, tile_blocks, slot_count):
    first_slot = lax.axis_index("tile") * slot_count
    row_blocks = []
    col_blocks = []
    present = []
    for slot_index in range(slot_count):
        matches = (tile_slot == first_slot + slot_index).astype(jnp.int32)
        row_blocks.append(jnp.sum(matches * tile_blocks[:, 0]))
        col_blocks.append(jnp.sum(matches * tile_blocks[:, 1]))
        present.append(jnp.sum(matches))
    return row_blocks, col_blocks, present


def generic_body(voltage, fir_taps, tile_slot, tile_blocks):
    spectra = transform(filter_frames(voltage, fir_taps))
    tile_count = tile_blocks.shape[0]
    tile_size = lax.axis_size("tile")
    slot_count = (tile_count + tile_size - 1) // tile_size
    turned = lax.all_to_all(spectra, "chan", split_axis=0, concat_axis=3, tiled=True)
    spectra_total = turned.shape[2] * tile_size
    row_blocks, col_blocks, present = own_slots(tile_slot, tile_blocks, slot_count)
    portion = lax.all_gather(turned, "tile", axis=2, tiled=True)
    summed = jnp.stack(
        [
            tile_product(portion, row_blocks[slot_index], col_blocks[slot_index], BLOCK)
            for slot_index in range(slot_count)
        ]
    )
    weights = jnp.stack(present).astype(F32)[:, None, None, None] / spectra_total
    return (summed * weights).reshape(slot_count, turned.shape[0], 2, BLOCK, BLOCK)


def fourier_table(points, owners, scale):
    phase = np.outer(np.arange(points), np.arange(points)) % points
    angle = phase * (2.0 * math.pi / points)
    cosine = np.cos(angle) * scale
    sine = np.sin(angle) * scale
    both = np.stack([np.concatenate([cosine, sine], 1), np.concatenate([-sine, cosine], 1)], 0)
    both = both.reshape(2, owners, points // owners, 2 * points).transpose(1, 0, 2, 3)
    return both.reshape(owners, -1, 2 * points).astype(np.float32)


def twiddle_table(length):
    angle = np.outer(np.arange(1, RADIX), np.arange(length // RADIX)) * (2.0 * math.pi / length)
    return np.stack([np.cos(angle), np.sin(angle)], 1).reshape(-1, length // RADIX).astype(np.float32)


def filter_kernel(frames, voltage_ref, next_ref, taps_ref, twiddle_ref, *refs):
    out_refs = refs[-2 * RADIX :]
    tap_count, length = taps_ref.shape
    held = voltage_ref.shape[1]
    points = length // RADIX

    def quarter(part, frame, index):
        lanes = slice(index * points, (index + 1) * points)
        total = None
        for tap in range(tap_count):
            at = frame + tap
            source = voltage_ref[part, at, :, lanes] if at < held else next_ref[part, at - held, :, lanes]
            term = source * taps_ref[pl.ds(tap, 1), lanes]
            total = term if total is None else total + term
        return total

    for frame in range(frames):
        real = [quarter(0, frame, index) for index in range(RADIX)]
        imag = [quarter(1, frame, index) for index in range(RADIX)]
        even_real, odd_real = real[0] + real[2], real[1] + real[3]
        even_imag, odd_imag = imag[0] + imag[2], imag[1] + imag[3]
        left_real, right_real = real[0] - real[2], real[1] - real[3]
        left_imag, right_imag = imag[0] - imag[2], imag[1] - imag[3]
        residues = [
            (even_real + odd_real, even_imag + odd_imag),
            (left_real + right_imag, left_imag - right_real),
            (even_real - odd_real, even_imag - odd_imag),
            (left_real - right_imag, left_imag + right_real),
        ]
        for index, (re, im) in enumerate(residues):
            if index:
                cosine = twiddle_ref[pl.ds(2 * index - 2, 1), :]
                sine = twiddle_ref[pl.ds(2 * index - 1, 1), :]
                re, im = re * cosine + im * sine, im * cosine - re * sine
            for part, value in enumerate((re, im)):
                high, low = split(value)
                lanes = slice(part * points, (part + 1) * points)
                out_refs[2 * index][frame, :, lanes] = high
                out_refs[2 * index + 1][frame, :, lanes] = low


def filtered_samples(voltage, following, fir_taps, late, earlier, after):
    _, frames, inputs, length = voltage.shape
    width = 16
    depth = 2 * length // RADIX
    twiddles = jnp.asarray(twiddle_table(length))
    out = jax.ShapeDtypeStruct((frames, inputs, depth), BF16)
    if earlier:
        count, held, place = late, late, frames // late - 1
    else:
        count, held, place = frames - late, frames, 0
    others = list(earlier) + list(after)
    return pl.pallas_call(
        functools.partial(filter_kernel, count),
        grid=(inputs // width,),
        in_specs=[
            pl.BlockSpec((2, held, width, length), lambda i: (0, place, i, 0)),
            pl.BlockSpec((2, following.shape[1], width, length), lambda i: (0, 0, i, 0)),
            pl.BlockSpec(fir_taps.shape, lambda i: (0, 0)),
            pl.BlockSpec(twiddles.shape, lambda i: (0, 0)),
        ]
        + [pl.BlockSpec(memory_space=pl.ANY)] * len(others),
        out_specs=[pl.BlockSpec((count, width, depth), lambda i: (place, i, 0))] * (2 * RADIX),
        out_shape=[out] * (2 * RADIX),
        input_output_aliases={4 + index: index for index in range(len(earlier))},
        compiler_params=params(),
        cost_estimate=pl.CostEstimate(
            flops=16 * voltage.size * count // frames,
            bytes_accessed=8 * voltage.size * count // frames,
            transcendentals=0,
        ),
        name="filter",
    )(voltage, following, fir_taps, twiddles, *others)


def dot_rows(left, right):
    return lax.dot_general(left, right, (((1,), (1,)), ((), ())), preferred_element_type=F32)


def transform_kernel(groups, pieces, table_ref, xh_ref, xl_ref, *refs):
    out_refs, (th_ref, tl_ref) = refs[-2 - len(groups) * pieces : -2], refs[-2:]
    height = table_ref.shape[1]
    masks = [mask for group in groups for mask in group]

    @pl.when(pl.program_id(0) == 0)
    def _():
        me = lax.axis_index("chan")
        for index, mask in enumerate(masks):
            rows = slice(index * height, (index + 1) * height)
            th_ref[rows], tl_ref[rows] = split(table_ref[me ^ mask])

    high = xh_ref[...]
    result = dot_rows(th_ref[...], high) + dot_rows(th_ref[...], xl_ref[...])
    result = result + dot_rows(tl_ref[...], high)
    count = height // 2
    size = count // pieces
    places = [(which, at) for which, group in enumerate(groups) for at in range(len(group))]
    for index, (which, at) in enumerate(places):
        for part in range(2):
            for piece in range(pieces):
                first = index * height + part * count + piece * size
                for column in range(result.shape[1] // BLOCK):
                    out_refs[which * pieces + piece][at, part, column] = result[
                        first : first + size, column * BLOCK : (column + 1) * BLOCK
                    ]


def transformed(groups, pieces, table, samples, after, first, last):
    depth = samples[0].shape[1]
    owners, height, _ = table.shape
    size = height // 2 // pieces
    step = STEP
    rows = (last - first) * step
    row_spec = pl.BlockSpec((step, depth), lambda i: (first + i, 0))
    total = sum(map(len, groups)) * height
    counts = [len(group) for group in groups for _ in range(pieces)]
    return pl.pallas_call(
        functools.partial(transform_kernel, groups, pieces),
        grid=(rows // step,),
        in_specs=[pl.BlockSpec(table.shape, lambda i: (0, 0, 0)), row_spec, row_spec]
        + [pl.BlockSpec(memory_space=pl.ANY)] * len(after),
        out_specs=[
            pl.BlockSpec((count, 2, step // BLOCK, size, BLOCK), lambda i: (0, 0, i, 0, 0))
            for count in counts
        ],
        out_shape=[
            jax.ShapeDtypeStruct((count, 2, rows // BLOCK, size, BLOCK), F32) for count in counts
        ],
        scratch_shapes=[pltpu.VMEM((total, depth), BF16)] * 2,
        compiler_params=params(),
        cost_estimate=pl.CostEstimate(
            flops=3 * 2 * total * depth * rows,
            bytes_accessed=4 * depth * rows + 4 * table.size + 4 * total * rows,
            transcendentals=0,
        ),
        name="transform",
    )(table, *samples, *after)


def merge_kernel(count, groups, piece, *refs):
    near_refs, far_refs, out_refs = refs[: len(groups)], refs[len(groups) : 2 * len(groups)], refs[-count:]
    total = sum(groups)
    odd = lax.axis_index("chan") % 2 == 1
    other = 1 - lax.axis_index("chan") % 2
    lower = lax.broadcasted_iota(jnp.int32, (total, BLOCK), 1) < BLOCK // 2
    for unit, out_ref in enumerate(out_refs):
        for channel in range(piece):
            for part in range(2):

                def rows_of(segment_refs):
                    rows = [
                        (ref if len(ref.shape) == 2 else ref.at[other])[
                            pl.ds((unit * 2 + part) * held * piece + channel, held, stride=piece), :
                        ]
                        for ref, held in zip(segment_refs, groups)
                    ]
                    return rows[0] if len(rows) == 1 else jnp.concatenate(rows, axis=0)

                near, far = rows_of(near_refs), rows_of(far_refs)
                first = jnp.where(odd, far, near)
                second = jnp.where(odd, near, far)
                at = part * 2 * total
                out_ref[channel, at : at + total] = jnp.where(
                    lower, first, pltpu.roll(second, BLOCK // 2, 1)
                )
                out_ref[channel, at + total : at + 2 * total] = jnp.where(
                    lower, pltpu.roll(first, BLOCK // 2, 1), second
                )


def merged(near, far, after):
    count, _, _, piece, lanes = near[0].shape
    groups = [value.shape[2] for value in near]
    size = sum(value.size for value in near)
    return pl.pallas_call(
        functools.partial(merge_kernel, count, groups, piece),
        in_specs=[pl.BlockSpec(memory_space=pltpu.VMEM)] * (2 * len(near))
        + [pl.BlockSpec(memory_space=pl.ANY)] * len(after),
        out_specs=[pl.BlockSpec(memory_space=pltpu.VMEM)] * count,
        out_shape=[jax.ShapeDtypeStruct((piece, 4 * sum(groups), lanes), F32)] * count,
        compiler_params=params(),
        cost_estimate=pl.CostEstimate(flops=4 * size, bytes_accessed=16 * size, transcendentals=0),
        name="merge",
    )(*[value.reshape(value.shape[:-5] + (-1, lanes)) for value in list(near) + list(far)], *after)


def pack_kernel(counts, *refs):
    sources = iter(refs)
    for count, out_ref in zip(counts, refs[-len(counts) :]):
        for index in range(count):
            out_ref[index] = next(sources)[...]


def packed(batches, after, moves=None):
    counts = [len(batch) for batch in batches]
    values = [value for batch in batches for value in batch]
    width = 8

    def spec(shape):
        lead = shape[:-3]
        return pl.BlockSpec(
            lead + (min(width, shape[-3]),) + shape[-2:], lambda i: (0,) * len(lead) + (i, 0, 0)
        )

    shapes = [(len(batch),) + batch[0].shape for batch in batches]
    return pl.pallas_call(
        functools.partial(pack_kernel, counts),
        grid=(values[0].shape[-3] // min(width, values[0].shape[-3]),),
        in_specs=[spec(value.shape) for value in values]
        + [pl.BlockSpec(memory_space=pl.ANY)] * len(after),
        out_specs=[spec(shape) for shape in shapes],
        out_shape=[jax.ShapeDtypeStruct(shape, F32) for shape in shapes],
        compiler_params=params(),
        cost_estimate=pl.CostEstimate(
            flops=moves or 0,
            bytes_accessed=moves or 8 * sum(value.size for value in values),
            transcendentals=0,
        ),
        name="pack",
    )(*values, *after)


def dot_columns(left, right):
    return lax.dot_general(left, right, (((0,), (0,)), ((), ())), preferred_element_type=F32)


def correlate_kernel(slots, order, where, slot_ref, blocks_ref, *refs):
    out_ref, done_ref, high_ref, low_ref, place_ref = refs[-5:]
    done_ref[...] = jnp.zeros(done_ref.shape, F32)
    tiles = len(where)
    blocks = len(order)
    width = out_ref.shape[1]
    depth = high_ref.shape[2] // tiles
    rows = depth // 2
    half = tiles * rows

    def unit_rows(tile, mask, channel, span):
        index, lead = where[tile][mask // HALF]
        if lead is None:
            return refs[index][mask % HALF, channel, span]
        return refs[index][lead, mask % HALF, channel, span]

    @pl.when(pl.program_id(0) == 0)
    def _():
        first_slot = lax.axis_index("tile") * slots
        for slot in range(slots):
            row = jnp.int32(0)
            col = jnp.int32(0)
            present = jnp.int32(0)
            for tile in range(slot_ref.shape[0]):
                match = (slot_ref[tile] == first_slot + slot).astype(jnp.int32)
                row = row + match * blocks_ref[2 * tile]
                col = col + match * blocks_ref[2 * tile + 1]
                present = present + match
            place_ref[3 * slot] = row
            place_ref[3 * slot + 1] = col
            place_ref[3 * slot + 2] = present

    own = lax.axis_index("chan") // 2
    for channel in range(width):
        for mask in range(blocks):
            block = own ^ order[mask]
            for part in range(2):
                joined = jnp.concatenate(
                    [
                        unit_rows(tile, mask, channel, slice(part * rows, (part + 1) * rows))
                        for tile in range(tiles)
                    ],
                    axis=0,
                )
                high, low = split(joined)
                high_ref[channel, block, part * half : (part + 1) * half] = high
                low_ref[channel, block, part * half : (part + 1) * half] = low
        for slot in range(slots):
            row = place_ref[3 * slot]
            col = place_ref[3 * slot + 1]
            weight = place_ref[3 * slot + 2].astype(F32)
            row_high = high_ref[channel, row]
            row_low = low_ref[channel, row]
            col_high = high_ref[channel, col]
            col_low = low_ref[channel, col]
            turned_high = jnp.concatenate([-col_high[half:], col_high[:half]], axis=0)
            turned_low = jnp.concatenate([-col_low[half:], col_low[:half]], axis=0)
            right_high = jnp.concatenate([col_high, turned_high], axis=1)
            right_low = jnp.concatenate([col_low, turned_low], axis=1)
            value = dot_columns(
                jnp.concatenate([row_high, row_low], axis=0),
                jnp.concatenate([right_high, right_high], axis=0),
            ) + dot_columns(row_high, right_low)
            value = value * weight
            out_ref[slot, channel, 0] = value[:, :BLOCK]
            out_ref[slot, channel, 1] = value[:, BLOCK:]


def correlated(order, tile_slot, tile_blocks, units, where, visibility, residue, first, total, slots):
    tiles = len(where)
    blocks = len(order)
    piece, depth, lanes = units[0].shape[-3:]
    width = 4
    out = jax.ShapeDtypeStruct((slots, total, RADIX, 2, BLOCK, BLOCK), F32)
    operands = [tile_slot, tile_blocks.reshape(-1)] + units
    in_specs = [
        pl.BlockSpec((HALF, width, depth, lanes), lambda i, *_: (0, i, 0, 0))
        if unit.ndim == 4
        else pl.BlockSpec(unit.shape[:2] + (width, depth, lanes), lambda i, *_: (0, 0, i, 0, 0))
        for unit in units
    ]
    aliases = {}
    if visibility is not None:
        operands.append(visibility)
        in_specs.append(pl.BlockSpec(memory_space=pl.ANY))
        aliases = {len(operands) - 1: 0}
    return pl.pallas_call(
        functools.partial(correlate_kernel, slots, order, where),
        grid_spec=pltpu.PrefetchScalarGridSpec(
            num_scalar_prefetch=2,
            grid=(piece // width,),
            in_specs=in_specs,
            out_specs=[
                pl.BlockSpec(
                    (slots, width, None, 2, BLOCK, BLOCK), lambda i, *_: (0, first // width + i, residue, 0, 0, 0)
                ),
                pl.BlockSpec((8, BLOCK), lambda i, *_: (0, 0)),
            ],
            scratch_shapes=[pltpu.VMEM((width, blocks, tiles * depth, lanes), BF16)] * 2
            + [pltpu.SMEM((3 * slots,), jnp.int32)],
        ),
        out_shape=[out, jax.ShapeDtypeStruct((8, BLOCK), F32)],
        input_output_aliases=aliases,
        compiler_params=params(),
        cost_estimate=pl.CostEstimate(flops=1, bytes_accessed=1, transcendentals=0),
        name="correlate",
    )(*operands)


def body(voltage, fir_taps, tile_slot, tile_blocks):
    _, frames, inputs, length = voltage.shape
    tap_count = fir_taps.shape[0]
    owners = lax.axis_size("chan")
    tiles = lax.axis_size("tile")
    channels = length // owners
    blocks = owners // 2
    slots = -(-tile_blocks.shape[0] // tiles)
    scale = 1.0 / math.sqrt(length * frames * tiles)
    table = jnp.asarray(fourier_table(length // RADIX, owners, scale))

    order = [2, 1, 3, 0]
    groups = [tuple(2 * block + x for block in order) for x in range(2)]
    halves = 2
    size = channels // RADIX // halves
    count = RADIX * halves
    near = [[] for _ in range(count)]
    share = [[] for _ in range(count)]
    away = [None] * count
    units = [None] * count

    steps = frames * inputs // STEP
    late = STEP // inputs
    following = shifted(voltage[:, : tap_count - 1], "tile", -1)
    early = filtered_samples(voltage, voltage[:, : tap_count - 1], fir_taps, late, [], [])

    def spectra(samples, residue, after, first, last):
        rows = [value.reshape(frames * inputs, -1) for value in samples[2 * residue : 2 * residue + 2]]
        values = transformed(groups, halves, table, rows, after, first, last)
        for half in range(halves):
            near[residue * halves + half].append(values[half])
            share[residue * halves + half].append(values[halves + half])

    spectra(early, 0, [], 0, steps - 1)
    samples = filtered_samples(voltage, following, fir_taps, late, early, [near[0][0]])
    spectra(samples, 0, [], steps - 1, steps)
    spectra(samples, 1, [], 0, steps)

    def leave(piece):
        values = share[piece]
        if piece < halves:
            if piece:
                after = [away[piece - 1][-1]]
                values = [packed([[value]], after)[0].reshape(value.shape) for value in values]
            away[piece] = [swapped(value, "chan", 1) for value in values]
        else:
            pairs = [[2 * block, 2 * block + 1] for block in range(blocks)]
            away[piece] = [lax.all_gather(value, "chan", axis_index_groups=pairs) for value in values]

    def merge(piece, after):
        units[piece] = merged(near[piece], away[piece], after)

    def along(piece, place, after):
        unit, block = units[piece][place], order[place]
        if after:
            unit = packed([[unit]], after)[0][0]
        return swapped(unit, "chan", 2 * block) if block else unit

    leave(0)
    merge(0, near[halves][:1])
    turned = [[along(0, place, []) for place in range(blocks)]] + [[None] * blocks for _ in range(count)]
    for residue in range(2, RADIX):
        spectra(samples, residue, turned[0][1:2], 0, steps)
    leave(1)
    merge(1, [])

    def products(piece, arrays, where, visibility):
        return correlated(
            order, tile_slot, tile_blocks, arrays, where, visibility,
            piece // halves, piece % halves * size, channels // RADIX, slots,
        )

    visibility = None
    finished = []
    own = [[None, None] for _ in range(count)]
    across = [[None, None] for _ in range(count)]
    crossed = []
    where = [[(0, None), (1, None)], [(2, None), (3, None)], [(4, 0), (4, 1)], [(4, 2), (4, 3)]]

    def half_step(piece, half, after):
        values = turned[piece][half * HALF : (half + 1) * HALF]
        (own[piece][half],) = packed([values], after, LONG)
        across[piece][half] = swapped(own[piece][half], "tile", 2)

    def between_cores(piece, after, visibility):
        arrays = own[piece] + across[piece]
        (both,) = packed([arrays], after)
        crossed.append(swapped(both, "tile", 1))
        visibility, token = products(piece, arrays + crossed[-1:], where, visibility)
        finished.append(token)
        return visibility

    for piece in range(count):
        after = [across[piece - 1][0], own[piece - 1][1]] if piece else []
        if piece + 1 < count:
            if units[piece + 1] is None:
                leave(piece + 1)
                merge(piece + 1, [])
            after.append(units[piece + 1][0])
        if not piece:
            after += [near[residue * halves][0] for residue in range(2, RADIX)]
        after += finished[piece - 3 : piece - 2] if piece >= 3 else []
        half_step(piece, 0, after)
        if piece + 1 < count:
            turned[piece + 1][0] = along(piece + 1, 0, [own[piece][0]])
        after = ([across[piece - 1][1]] if piece else []) + [own[piece][0]]
        if piece >= 2:
            visibility = between_cores(piece - 2, [own[piece][0]], visibility)
        half_step(piece, 1, after)
        if piece + 1 < count:
            turned[piece + 1][2] = along(piece + 1, 2, [])
            turned[piece + 1][1] = along(piece + 1, 1, [own[piece][1]] + crossed[piece - 2 :] if piece >= 2 else [own[piece][1]])
            turned[piece + 1][3] = along(piece + 1, 3, [])
    visibility = between_cores(count - 2, own[count - 1][1:], visibility)
    last = count - 1
    (final,) = packed([across[last][1:]], finished[-1:])
    arrays = own[last] + across[last]
    arrays += [swapped(value, "tile", 1) for value in own[last] + across[last][:1] + [final[0]]]
    where = [[(2 * tile, None), (2 * tile + 1, None)] for tile in range(tiles)]
    visibility, _ = products(last, arrays, where, visibility)
    return visibility.reshape(slots, channels, 2, BLOCK, BLOCK)


def solution(mesh):
    in_specs = (P(None, "tile", "chan", None), P(), P(), P())
    out_specs = P("tile", "chan", None, None, None)
    owners, tiles = mesh.shape["chan"], mesh.shape["tile"]

    def run(voltage, fir_taps, tile_slot, tile_blocks):
        paired = 2 * voltage.shape[2] == BLOCK * owners and tiles == 4 and owners == 8
        chosen = body if paired else generic_body
        return jax.shard_map(
            chosen, mesh=mesh, in_specs=in_specs, out_specs=out_specs, check_vma=False
        )(voltage, fir_taps, tile_slot, tile_blocks)

    return run
```

```python
import functools
import math

import jax
import jax.numpy as jnp
import numpy as np
from jax import lax
from jax.experimental import pallas as pl
from jax.experimental.pallas import tpu as pltpu
from jax.sharding import PartitionSpec as P

BLOCK = 128
RADIX = 4
STEP = 256
LONG = 2_000_000_000_000
VMEM_BYTES = 14 * 1024 * 1024
BF16 = jnp.bfloat16
F32 = jnp.float32


def shifted(value, axis, steps):
    count = lax.axis_size(axis)
    initial, last = (max(0, -steps), min(count, count - steps))
    return lax.ppermute(value, axis, [(source, source + steps) for source in range(initial, last)])


def swapped(value, axis, mask):
    count = lax.axis_size(axis)
    return lax.ppermute(value, axis, [(source, source ^ mask) for source in range(count)])


def params():
    return pltpu.CompilerParams(vmem_limit_bytes=VMEM_BYTES)


def split(value):
    high = value.astype(BF16)
    return high, (value - high.astype(F32)).astype(BF16)


def filter_frames(voltage, fir_taps):
    tap_count = fir_taps.shape[0]
    frames = voltage.shape[1]
    history = shifted(voltage[:, : tap_count - 1], "tile", -1)
    extended = jnp.concatenate([voltage, history], axis=1)
    filtered = jnp.zeros(voltage.shape, jnp.float32)
    for tap_index in range(tap_count):
        filtered = (
            filtered
            + fir_taps[tap_index][None, None, None, :] * extended[:, tap_index : tap_index + frames]
        )
    return filtered


def transform(filtered):
    channel_count = filtered.shape[3]
    row_count = filtered.shape[1] * filtered.shape[2]
    position = lax.broadcasted_iota(jnp.int32, (channel_count, channel_count), 0)
    frequency = lax.broadcasted_iota(jnp.int32, (channel_count, channel_count), 1)
    phase_angle = (position * frequency % channel_count).astype(jnp.float32) * (
        2.0 * math.pi / channel_count
    )
    factor = 1.0 / math.sqrt(channel_count)
    cosine = jnp.cos(phase_angle) * factor
    sine_table = jnp.sin(phase_angle) * factor
    samples = filtered.reshape(2 * row_count, channel_count)
    cos_part = jnp.dot(
        cosine, samples.T, precision=lax.Precision.HIGHEST, preferred_element_type=jnp.float32
    )
    sin_part = jnp.dot(
        sine_table, samples.T, precision=lax.Precision.HIGHEST, preferred_element_type=jnp.float32
    )
    real_part = cos_part[:, :row_count] + sin_part[:, row_count:]
    imag_part = cos_part[:, row_count:] - sin_part[:, :row_count]
    joined = jnp.concatenate([real_part, imag_part], axis=1)
    return joined.reshape(channel_count, 2, filtered.shape[1], filtered.shape[2])


def tile_product(gathered, row_block, col_block, block_width):
    left_block = lax.dynamic_slice_in_dim(gathered, row_block * block_width, block_width, 3)
    right_block = lax.dynamic_slice_in_dim(gathered, col_block * block_width, block_width, 3)
    channel_count = gathered.shape[0]
    depth = 2 * gathered.shape[2]
    left_real = left_block.reshape(channel_count, depth, block_width)
    left_imag = jnp.concatenate([left_block[:, 1], -left_block[:, 0]], axis=1)
    left_both = jnp.concatenate([left_real, left_imag], axis=2)
    right_both = right_block.reshape(channel_count, depth, block_width)
    return jnp.einsum(
        "cki,ckj->cij",
        left_both,
        right_both,
        precision=lax.Precision.HIGHEST,
        preferred_element_type=jnp.float32,
    )


def own_slots(tile_slot, tile_blocks, slot_count):
    first_slot = lax.axis_index("tile") * slot_count
    row_blocks = []
    col_blocks = []
    present = []
    for slot_index in range(slot_count):
        matches = (tile_slot == first_slot + slot_index).astype(jnp.int32)
        row_blocks.append(jnp.sum(matches * tile_blocks[:, 0]))
        col_blocks.append(jnp.sum(matches * tile_blocks[:, 1]))
        present.append(jnp.sum(matches))
    return row_blocks, col_blocks, present


def generic_body(voltage, fir_taps, tile_slot, tile_blocks):
    spectra = transform(filter_frames(voltage, fir_taps))
    tile_count = tile_blocks.shape[0]
    tile_size = lax.axis_size("tile")
    slot_count = (tile_count + tile_size - 1) // tile_size
    turned = lax.all_to_all(spectra, "chan", split_axis=0, concat_axis=3, tiled=True)
    spectra_total = turned.shape[2] * tile_size
    row_blocks, col_blocks, present = own_slots(tile_slot, tile_blocks, slot_count)
    portion = lax.all_gather(turned, "tile", axis=2, tiled=True)
    summed = jnp.stack(
        [
            tile_product(portion, row_blocks[slot_index], col_blocks[slot_index], BLOCK)
            for slot_index in range(slot_count)
        ]
    )
    weights = jnp.stack(present).astype(F32)[:, None, None, None] / spectra_total
    return (summed * weights).reshape(slot_count, turned.shape[0], 2, BLOCK, BLOCK)


def fourier_table(points, owners, scale):
    phase = np.outer(np.arange(points), np.arange(points)) % points
    angle = phase * (2.0 * math.pi / points)
    cosine = np.cos(angle) * scale
    sine = np.sin(angle) * scale
    both = np.stack([np.concatenate([cosine, sine], 1), np.concatenate([-sine, cosine], 1)], 0)
    both = both.reshape(2, owners, points // owners, 2 * points).transpose(1, 0, 2, 3)
    return both.reshape(owners, -1, 2 * points).astype(np.float32)


def twiddle_table(length):
    angle = np.outer(np.arange(1, RADIX), np.arange(length // RADIX)) * (2.0 * math.pi / length)
    return np.stack([np.cos(angle), np.sin(angle)], 1).reshape(-1, length // RADIX).astype(np.float32)


def filter_kernel(frames, voltage_ref, next_ref, taps_ref, twiddle_ref, *refs):
    out_refs = refs[-2 * RADIX :]
    tap_count, length = taps_ref.shape
    held = voltage_ref.shape[1]
    points = length // RADIX

    def quarter(part, frame, index):
        lanes = slice(index * points, (index + 1) * points)
        total = None
        for tap in range(tap_count):
            at = frame + tap
            source = voltage_ref[part, at, :, lanes] if at < held else next_ref[part, at - held, :, lanes]
            term = source * taps_ref[pl.ds(tap, 1), lanes]
            total = term if total is None else total + term
        return total

    for frame in range(frames):
        real = [quarter(0, frame, index) for index in range(RADIX)]
        imag = [quarter(1, frame, index) for index in range(RADIX)]
        even_real, odd_real = real[0] + real[2], real[1] + real[3]
        even_imag, odd_imag = imag[0] + imag[2], imag[1] + imag[3]
        left_real, right_real = real[0] - real[2], real[1] - real[3]
        left_imag, right_imag = imag[0] - imag[2], imag[1] - imag[3]
        residues = [
            (even_real + odd_real, even_imag + odd_imag),
            (left_real + right_imag, left_imag - right_real),
            (even_real - odd_real, even_imag - odd_imag),
            (left_real - right_imag, left_imag + right_real),
        ]
        for index, (re, im) in enumerate(residues):
            if index:
                cosine = twiddle_ref[pl.ds(2 * index - 2, 1), :]
                sine = twiddle_ref[pl.ds(2 * index - 1, 1), :]
                re, im = re * cosine + im * sine, im * cosine - re * sine
            for part, value in enumerate((re, im)):
                high, low = split(value)
                lanes = slice(part * points, (part + 1) * points)
                out_refs[2 * index][frame, :, lanes] = high
                out_refs[2 * index + 1][frame, :, lanes] = low


def filtered_samples(voltage, following, fir_taps, late, earlier, after):
    _, frames, inputs, length = voltage.shape
    width = 16
    depth = 2 * length // RADIX
    twiddles = jnp.asarray(twiddle_table(length))
    out = jax.ShapeDtypeStruct((frames, inputs, depth), BF16)
    if earlier:
        count, held, place = late, late, frames // late - 1
    else:
        count, held, place = frames - late, frames, 0
    others = list(earlier) + list(after)
    return pl.pallas_call(
        functools.partial(filter_kernel, count),
        grid=(inputs // width,),
        in_specs=[
            pl.BlockSpec((2, held, width, length), lambda i: (0, place, i, 0)),
            pl.BlockSpec((2, following.shape[1], width, length), lambda i: (0, 0, i, 0)),
            pl.BlockSpec(fir_taps.shape, lambda i: (0, 0)),
            pl.BlockSpec(twiddles.shape, lambda i: (0, 0)),
        ]
        + [pl.BlockSpec(memory_space=pl.ANY)] * len(others),
        out_specs=[pl.BlockSpec((count, width, depth), lambda i: (place, i, 0))] * (2 * RADIX),
        out_shape=[out] * (2 * RADIX),
        input_output_aliases={4 + index: index for index in range(len(earlier))},
        compiler_params=params(),
        cost_estimate=pl.CostEstimate(
            flops=16 * voltage.size * count // frames,
            bytes_accessed=8 * voltage.size * count // frames,
            transcendentals=0,
        ),
        name="filter",
    )(voltage, following, fir_taps, twiddles, *others)


def dot_rows(left, right):
    return lax.dot_general(left, right, (((1,), (1,)), ((), ())), preferred_element_type=F32)


def transform_kernel(groups, pieces, table_ref, xh_ref, xl_ref, *refs):
    out_refs, (th_ref, tl_ref) = refs[-2 - len(groups) * pieces : -2], refs[-2:]
    height = table_ref.shape[1]
    masks = [mask for group in groups for mask in group]

    @pl.when(pl.program_id(0) == 0)
    def _():
        me = lax.axis_index("chan")
        for index, mask in enumerate(masks):
            rows = slice(index * height, (index + 1) * height)
            th_ref[rows], tl_ref[rows] = split(table_ref[me ^ mask])

    high = xh_ref[...]
    result = dot_rows(th_ref[...], high) + dot_rows(th_ref[...], xl_ref[...])
    result = result + dot_rows(tl_ref[...], high)
    count = height // 2
    size = count // pieces
    places = [(which, at) for which, group in enumerate(groups) for at in range(len(group))]
    for index, (which, at) in enumerate(places):
        for part in range(2):
            for piece in range(pieces):
                first = index * height + part * count + piece * size
                for column in range(result.shape[1] // BLOCK):
                    out_refs[which * pieces + piece][at, part, column] = result[
                        first : first + size, column * BLOCK : (column + 1) * BLOCK
                    ]


def transformed(groups, pieces, table, samples, after, first, last):
    depth = samples[0].shape[1]
    owners, height, _ = table.shape
    size = height // 2 // pieces
    step = STEP
    rows = (last - first) * step
    row_spec = pl.BlockSpec((step, depth), lambda i: (first + i, 0))
    total = sum(map(len, groups)) * height
    counts = [len(group) for group in groups for _ in range(pieces)]
    return pl.pallas_call(
        functools.partial(transform_kernel, groups, pieces),
        grid=(rows // step,),
        in_specs=[pl.BlockSpec(table.shape, lambda i: (0, 0, 0)), row_spec, row_spec]
        + [pl.BlockSpec(memory_space=pl.ANY)] * len(after),
        out_specs=[
            pl.BlockSpec((count, 2, step // BLOCK, size, BLOCK), lambda i: (0, 0, i, 0, 0))
            for count in counts
        ],
        out_shape=[
            jax.ShapeDtypeStruct((count, 2, rows // BLOCK, size, BLOCK), F32) for count in counts
        ],
        scratch_shapes=[pltpu.VMEM((total, depth), BF16)] * 2,
        compiler_params=params(),
        cost_estimate=pl.CostEstimate(
            flops=3 * 2 * total * depth * rows,
            bytes_accessed=4 * depth * rows + 4 * table.size + 4 * total * rows,
            transcendentals=0,
        ),
        name="transform",
    )(table, *samples, *after)


def merge_kernel(count, groups, piece, *refs):
    near_refs, far_refs, out_refs = refs[: len(groups)], refs[len(groups) : 2 * len(groups)], refs[-count:]
    total = sum(groups)
    odd = lax.axis_index("chan") % 2 == 1
    lower = lax.broadcasted_iota(jnp.int32, (total, BLOCK), 1) < BLOCK // 2
    for unit, out_ref in enumerate(out_refs):
        for channel in range(piece):
            for part in range(2):

                def rows_of(segment_refs):
                    rows = [
                        ref[pl.ds((unit * 2 + part) * held * piece + channel, held, stride=piece), :]
                        for ref, held in zip(segment_refs, groups)
                    ]
                    return rows[0] if len(rows) == 1 else jnp.concatenate(rows, axis=0)

                near, far = rows_of(near_refs), rows_of(far_refs)
                first = jnp.where(odd, far, near)
                second = jnp.where(odd, near, far)
                at = part * 2 * total
                out_ref[channel, at : at + total] = jnp.where(
                    lower, first, pltpu.roll(second, BLOCK // 2, 1)
                )
                out_ref[channel, at + total : at + 2 * total] = jnp.where(
                    lower, pltpu.roll(first, BLOCK // 2, 1), second
                )


def merged(near, far, after):
    count, _, _, piece, lanes = near[0].shape
    groups = [value.shape[2] for value in near]
    size = sum(value.size for value in near)
    return pl.pallas_call(
        functools.partial(merge_kernel, count, groups, piece),
        in_specs=[pl.BlockSpec(memory_space=pltpu.VMEM)] * (2 * len(near))
        + [pl.BlockSpec(memory_space=pl.ANY)] * len(after),
        out_specs=[pl.BlockSpec(memory_space=pltpu.VMEM)] * count,
        out_shape=[jax.ShapeDtypeStruct((piece, 4 * sum(groups), lanes), F32)] * count,
        compiler_params=params(),
        cost_estimate=pl.CostEstimate(flops=4 * size, bytes_accessed=16 * size, transcendentals=0),
        name="merge",
    )(*[value.reshape(-1, lanes) for value in list(near) + list(far)], *after)


def pack_kernel(counts, *refs):
    sources = iter(refs)
    for count, out_ref in zip(counts, refs[-len(counts) :]):
        for index in range(count):
            out_ref[index] = next(sources)[...]


def packed(batches, after, work=0):
    counts = [len(batch) for batch in batches]
    values = [value for batch in batches for value in batch]
    width = 8

    def spec(shape):
        lead = shape[:-3]
        return pl.BlockSpec(
            lead + (min(width, shape[-3]),) + shape[-2:], lambda i: (0,) * len(lead) + (i, 0, 0)
        )

    shapes = [(len(batch),) + batch[0].shape for batch in batches]
    return pl.pallas_call(
        functools.partial(pack_kernel, counts),
        grid=(values[0].shape[-3] // min(width, values[0].shape[-3]),),
        in_specs=[spec(value.shape) for value in values]
        + [pl.BlockSpec(memory_space=pl.ANY)] * len(after),
        out_specs=[spec(shape) for shape in shapes],
        out_shape=[jax.ShapeDtypeStruct(shape, F32) for shape in shapes],
        compiler_params=params(),
        cost_estimate=pl.CostEstimate(
            flops=work,
            bytes_accessed=8 * sum(value.size for value in values),
            transcendentals=0,
        ),
        name="pack",
    )(*values, *after)


def dot_columns(left, right):
    return lax.dot_general(left, right, (((0,), (0,)), ((), ())), preferred_element_type=F32)


def correlate_kernel(slots, tiles, order, slot_ref, blocks_ref, *refs):
    unit_refs = []
    for ref in refs[:-5]:
        if len(ref.shape) == 4:
            unit_refs.append(ref)
        elif len(ref.shape) == 5 and len(unit_refs) < tiles:
            unit_refs += [ref.at[0], ref.at[1]]
    out_ref, done_ref, high_ref, low_ref, place_ref = refs[-5:]
    done_ref[...] = jnp.zeros(done_ref.shape, F32)
    blocks, width, depth, _ = unit_refs[0].shape
    rows = depth // 2
    half = tiles * rows

    @pl.when(pl.program_id(0) == 0)
    def _():
        first_slot = lax.axis_index("tile") * slots
        for slot in range(slots):
            row = jnp.int32(0)
            col = jnp.int32(0)
            present = jnp.int32(0)
            for tile in range(slot_ref.shape[0]):
                match = (slot_ref[tile] == first_slot + slot).astype(jnp.int32)
                row = row + match * blocks_ref[2 * tile]
                col = col + match * blocks_ref[2 * tile + 1]
                present = present + match
            place_ref[3 * slot] = row
            place_ref[3 * slot + 1] = col
            place_ref[3 * slot + 2] = present

    own = lax.axis_index("chan") // 2
    for channel in range(width):
        for mask in range(blocks):
            block = own ^ order[mask]
            for part in range(2):
                joined = jnp.concatenate(
                    [
                        unit_ref[mask, channel, part * rows : (part + 1) * rows]
                        for unit_ref in unit_refs
                    ],
                    axis=0,
                )
                high, low = split(joined)
                high_ref[channel, block, part * half : (part + 1) * half] = high
                low_ref[channel, block, part * half : (part + 1) * half] = low
        for slot in range(slots):
            row = place_ref[3 * slot]
            col = place_ref[3 * slot + 1]
            weight = place_ref[3 * slot + 2].astype(F32)
            row_high = high_ref[channel, row]
            row_low = low_ref[channel, row]
            col_high = high_ref[channel, col]
            col_low = low_ref[channel, col]
            turned_high = jnp.concatenate([-col_high[half:], col_high[:half]], axis=0)
            turned_low = jnp.concatenate([-col_low[half:], col_low[:half]], axis=0)
            right_high = jnp.concatenate([col_high, turned_high], axis=1)
            right_low = jnp.concatenate([col_low, turned_low], axis=1)
            value = dot_columns(
                jnp.concatenate([row_high, row_low], axis=0),
                jnp.concatenate([right_high, right_high], axis=0),
            ) + dot_columns(row_high, right_low)
            value = value * weight
            out_ref[slot, channel, 0] = value[:, :BLOCK]
            out_ref[slot, channel, 1] = value[:, BLOCK:]


def correlated(order, tile_slot, tile_blocks, units, visibility, residue, first, total, slots):
    tiles = sum(1 if unit.ndim == 4 else unit.shape[0] for unit in units)
    blocks, piece, depth, lanes = units[0].shape
    width = 4
    out = jax.ShapeDtypeStruct((slots, total, RADIX, 2, BLOCK, BLOCK), F32)
    operands = [tile_slot, tile_blocks.reshape(-1)] + units
    in_specs = [
        pl.BlockSpec((blocks, width, depth, lanes), lambda i, *_: (0, i, 0, 0))
        if unit.ndim == 4
        else pl.BlockSpec(unit.shape[:2] + (width, depth, lanes), lambda i, *_: (0, 0, i, 0, 0))
        for unit in units
    ]
    aliases = {}
    if visibility is not None:
        operands.append(visibility)
        in_specs.append(pl.BlockSpec(memory_space=pl.ANY))
        aliases = {len(operands) - 1: 0}
    return pl.pallas_call(
        functools.partial(correlate_kernel, slots, tiles, order),
        grid_spec=pltpu.PrefetchScalarGridSpec(
            num_scalar_prefetch=2,
            grid=(piece // width,),
            in_specs=in_specs,
            out_specs=[
                pl.BlockSpec(
                    (slots, width, None, 2, BLOCK, BLOCK), lambda i, *_: (0, first // width + i, residue, 0, 0, 0)
                ),
                pl.BlockSpec((8, BLOCK), lambda i, *_: (0, 0)),
            ],
            scratch_shapes=[pltpu.VMEM((width, blocks, tiles * depth, lanes), BF16)] * 2
            + [pltpu.SMEM((3 * slots,), jnp.int32)],
        ),
        out_shape=[out, jax.ShapeDtypeStruct((8, BLOCK), F32)],
        input_output_aliases=aliases,
        compiler_params=params(),
        cost_estimate=pl.CostEstimate(
            flops=3 * 2 * slots * piece * tiles * depth * BLOCK * 2 * BLOCK,
            bytes_accessed=4 * piece * lanes * (tiles * blocks * depth + slots * 2 * BLOCK),
            transcendentals=0,
        ),
        name="correlate",
    )(*operands)


def body(voltage, fir_taps, tile_slot, tile_blocks):
    _, frames, inputs, length = voltage.shape
    tap_count = fir_taps.shape[0]
    owners = lax.axis_size("chan")
    tiles = lax.axis_size("tile")
    channels = length // owners
    blocks = owners // 2
    slots = -(-tile_blocks.shape[0] // tiles)
    scale = 1.0 / math.sqrt(length * frames * tiles)
    table = jnp.asarray(fourier_table(length // RADIX, owners, scale))

    order = list(range(2, blocks)) + [1, 0]
    groups = [tuple(2 * block + x for block in order) for x in range(2)]
    halves = 2
    size = channels // RADIX // halves
    count = RADIX * halves
    near = [[] for _ in range(count)]
    share = [[] for _ in range(count)]
    away = [None] * count
    units = [None] * count
    paired = [None] * count

    steps = frames * inputs // STEP
    late = STEP // inputs
    following = shifted(voltage[:, : tap_count - 1], "tile", -1)
    early = filtered_samples(voltage, voltage[:, : tap_count - 1], fir_taps, late, [], [])

    def spectra(samples, residue, after, first, last):
        rows = [value.reshape(frames * inputs, -1) for value in samples[2 * residue : 2 * residue + 2]]
        values = transformed(groups, halves, table, rows, after, first, last)
        for half in range(halves):
            near[residue * halves + half].append(values[half])
            share[residue * halves + half].append(values[halves + half])

    spectra(early, 0, [], 0, steps - 1)
    samples = filtered_samples(voltage, following, fir_taps, late, early, [near[0][0]])
    spectra(samples, 0, [], steps - 1, steps)
    spectra(samples, 1, [], 0, steps)

    def leave(piece):
        values = share[piece]
        if 0 < piece < 5:
            after = [away[piece - 1][-1]]
            values = [packed([[value]], after)[0].reshape(value.shape) for value in values]
        away[piece] = [swapped(value, "chan", 1) for value in values]

    def merge(piece, after):
        units[piece] = merged(near[piece], away[piece], after)

    def along(piece):
        return [
            swapped(unit, "chan", 2 * block) if block else unit
            for block, unit in zip(order, units[piece])
        ]

    leave(0)
    merge(0, near[halves][:1])
    turned = along(0)
    for residue in range(2, RADIX):
        spectra(samples, residue, turned[-2:-1], 0, steps)
    leave(1)
    merge(1, [])
    leave(2)

    def products(piece, arrays, visibility):
        return correlated(
            order, tile_slot, tile_blocks, arrays, visibility,
            piece // halves, piece % halves * size, channels // RADIX, slots,
        )

    visibility = None
    finished = []
    pair = None
    for piece in range(count):
        if piece:
            after = [pair[1]]
            for later in range(piece + 1, min(piece + 3, count)):
                if units[later] is None:
                    merge(later, [])
                after.append(units[later][0])
        else:
            after = [units[1][0]] + [near[residue * halves][0] for residue in range(2, RADIX)]
        after += finished[piece - 2 : piece - 1] if piece >= 2 else []
        (own,) = packed([turned], after, LONG)
        if piece + 1 < count:
            turned = along(piece + 1)
        across = swapped(own, "tile", 2)
        if piece + 3 < count:
            leave(piece + 3)
        if pair:
            (both,) = packed([pair], [own] + (away[piece + 3][-1:] if piece + 3 < count else []))
            paired[piece - 1] = swapped(both, "tile", 1)
            visibility, token = products(piece - 1, pair + [paired[piece - 1]], visibility)
            finished.append(token)
        pair = [own, across]
    (last,) = packed([[across]], finished[-1:])
    arrays = pair + [swapped(own, "tile", 1), swapped(last[0], "tile", 1)]
    visibility, _ = products(count - 1, arrays, visibility)
    return visibility.reshape(slots, channels, 2, BLOCK, BLOCK)


def solution(mesh):
    in_specs = (P(None, "tile", "chan", None), P(), P(), P())
    out_specs = P("tile", "chan", None, None, None)
    owners, tiles = mesh.shape["chan"], mesh.shape["tile"]

    def run(voltage, fir_taps, tile_slot, tile_blocks):
        paired = 2 * voltage.shape[2] == BLOCK * owners and tiles == 4
        chosen = body if paired else generic_body
        return jax.shard_map(
            chosen, mesh=mesh, in_specs=in_specs, out_specs=out_specs, check_vma=False
        )(voltage, fir_taps, tile_slot, tile_blocks)

    return run
```

```python
import functools
import math

import jax
import jax.numpy as jnp
import numpy as np
from jax import lax
from jax.experimental import pallas as pl
from jax.experimental.pallas import tpu as pltpu
from jax.sharding import PartitionSpec as P

BLOCK = 128
RADIX = 4
STEP = 256
LONG = 2_000_000_000_000
VMEM_BYTES = 14 * 1024 * 1024
BF16 = jnp.bfloat16
F32 = jnp.float32


def shifted(value, axis, steps):
    count = lax.axis_size(axis)
    initial, last = (max(0, -steps), min(count, count - steps))
    return lax.ppermute(value, axis, [(source, source + steps) for source in range(initial, last)])


def swapped(value, axis, mask):
    count = lax.axis_size(axis)
    return lax.ppermute(value, axis, [(source, source ^ mask) for source in range(count)])


def params():
    return pltpu.CompilerParams(vmem_limit_bytes=VMEM_BYTES)


def split(value):
    high = value.astype(BF16)
    return high, (value - high.astype(F32)).astype(BF16)


def filter_frames(voltage, fir_taps):
    tap_count = fir_taps.shape[0]
    frames = voltage.shape[1]
    history = shifted(voltage[:, : tap_count - 1], "tile", -1)
    extended = jnp.concatenate([voltage, history], axis=1)
    filtered = jnp.zeros(voltage.shape, jnp.float32)
    for tap_index in range(tap_count):
        filtered = (
            filtered
            + fir_taps[tap_index][None, None, None, :] * extended[:, tap_index : tap_index + frames]
        )
    return filtered


def transform(filtered):
    channel_count = filtered.shape[3]
    row_count = filtered.shape[1] * filtered.shape[2]
    position = lax.broadcasted_iota(jnp.int32, (channel_count, channel_count), 0)
    frequency = lax.broadcasted_iota(jnp.int32, (channel_count, channel_count), 1)
    phase_angle = (position * frequency % channel_count).astype(jnp.float32) * (
        2.0 * math.pi / channel_count
    )
    factor = 1.0 / math.sqrt(channel_count)
    cosine = jnp.cos(phase_angle) * factor
    sine_table = jnp.sin(phase_angle) * factor
    samples = filtered.reshape(2 * row_count, channel_count)
    cos_part = jnp.dot(
        cosine, samples.T, precision=lax.Precision.HIGHEST, preferred_element_type=jnp.float32
    )
    sin_part = jnp.dot(
        sine_table, samples.T, precision=lax.Precision.HIGHEST, preferred_element_type=jnp.float32
    )
    real_part = cos_part[:, :row_count] + sin_part[:, row_count:]
    imag_part = cos_part[:, row_count:] - sin_part[:, :row_count]
    joined = jnp.concatenate([real_part, imag_part], axis=1)
    return joined.reshape(channel_count, 2, filtered.shape[1], filtered.shape[2])


def tile_product(gathered, row_block, col_block, block_width):
    left_block = lax.dynamic_slice_in_dim(gathered, row_block * block_width, block_width, 3)
    right_block = lax.dynamic_slice_in_dim(gathered, col_block * block_width, block_width, 3)
    channel_count = gathered.shape[0]
    depth = 2 * gathered.shape[2]
    left_real = left_block.reshape(channel_count, depth, block_width)
    left_imag = jnp.concatenate([left_block[:, 1], -left_block[:, 0]], axis=1)
    left_both = jnp.concatenate([left_real, left_imag], axis=2)
    right_both = right_block.reshape(channel_count, depth, block_width)
    return jnp.einsum(
        "cki,ckj->cij",
        left_both,
        right_both,
        precision=lax.Precision.HIGHEST,
        preferred_element_type=jnp.float32,
    )


def own_slots(tile_slot, tile_blocks, slot_count):
    first_slot = lax.axis_index("tile") * slot_count
    row_blocks = []
    col_blocks = []
    present = []
    for slot_index in range(slot_count):
        matches = (tile_slot == first_slot + slot_index).astype(jnp.int32)
        row_blocks.append(jnp.sum(matches * tile_blocks[:, 0]))
        col_blocks.append(jnp.sum(matches * tile_blocks[:, 1]))
        present.append(jnp.sum(matches))
    return row_blocks, col_blocks, present


def generic_body(voltage, fir_taps, tile_slot, tile_blocks):
    spectra = transform(filter_frames(voltage, fir_taps))
    tile_count = tile_blocks.shape[0]
    tile_size = lax.axis_size("tile")
    slot_count = (tile_count + tile_size - 1) // tile_size
    turned = lax.all_to_all(spectra, "chan", split_axis=0, concat_axis=3, tiled=True)
    spectra_total = turned.shape[2] * tile_size
    row_blocks, col_blocks, present = own_slots(tile_slot, tile_blocks, slot_count)
    portion = lax.all_gather(turned, "tile", axis=2, tiled=True)
    summed = jnp.stack(
        [
            tile_product(portion, row_blocks[slot_index], col_blocks[slot_index], BLOCK)
            for slot_index in range(slot_count)
        ]
    )
    weights = jnp.stack(present).astype(F32)[:, None, None, None] / spectra_total
    return (summed * weights).reshape(slot_count, turned.shape[0], 2, BLOCK, BLOCK)


def fourier_table(points, owners, scale):
    phase = np.outer(np.arange(points), np.arange(points)) % points
    angle = phase * (2.0 * math.pi / points)
    cosine = np.cos(angle) * scale
    sine = np.sin(angle) * scale
    both = np.stack([np.concatenate([cosine, sine], 1), np.concatenate([-sine, cosine], 1)], 0)
    both = both.reshape(2, owners, points // owners, 2 * points).transpose(1, 0, 2, 3)
    return both.reshape(owners, -1, 2 * points).astype(np.float32)


def twiddle_table(length):
    angle = np.outer(np.arange(1, RADIX), np.arange(length // RADIX)) * (2.0 * math.pi / length)
    return np.stack([np.cos(angle), np.sin(angle)], 1).reshape(-1, length // RADIX).astype(np.float32)


def filter_kernel(frames, voltage_ref, next_ref, taps_ref, twiddle_ref, *refs):
    out_refs = refs[-2 * RADIX :]
    tap_count, length = taps_ref.shape
    held = voltage_ref.shape[1]
    points = length // RADIX

    def quarter(part, frame, index):
        lanes = slice(index * points, (index + 1) * points)
        total = None
        for tap in range(tap_count):
            at = frame + tap
            source = voltage_ref[part, at, :, lanes] if at < held else next_ref[part, at - held, :, lanes]
            term = source * taps_ref[pl.ds(tap, 1), lanes]
            total = term if total is None else total + term
        return total

    for frame in range(frames):
        real = [quarter(0, frame, index) for index in range(RADIX)]
        imag = [quarter(1, frame, index) for index in range(RADIX)]
        even_real, odd_real = real[0] + real[2], real[1] + real[3]
        even_imag, odd_imag = imag[0] + imag[2], imag[1] + imag[3]
        left_real, right_real = real[0] - real[2], real[1] - real[3]
        left_imag, right_imag = imag[0] - imag[2], imag[1] - imag[3]
        residues = [
            (even_real + odd_real, even_imag + odd_imag),
            (left_real + right_imag, left_imag - right_real),
            (even_real - odd_real, even_imag - odd_imag),
            (left_real - right_imag, left_imag + right_real),
        ]
        for index, (re, im) in enumerate(residues):
            if index:
                cosine = twiddle_ref[pl.ds(2 * index - 2, 1), :]
                sine = twiddle_ref[pl.ds(2 * index - 1, 1), :]
                re, im = re * cosine + im * sine, im * cosine - re * sine
            for part, value in enumerate((re, im)):
                high, low = split(value)
                lanes = slice(part * points, (part + 1) * points)
                out_refs[2 * index][frame, :, lanes] = high
                out_refs[2 * index + 1][frame, :, lanes] = low


def filtered_samples(voltage, following, fir_taps, late, earlier, after):
    _, frames, inputs, length = voltage.shape
    width = 16
    depth = 2 * length // RADIX
    twiddles = jnp.asarray(twiddle_table(length))
    out = jax.ShapeDtypeStruct((frames, inputs, depth), BF16)
    if earlier:
        count, held, place = late, late, frames // late - 1
    else:
        count, held, place = frames - late, frames, 0
    others = list(earlier) + list(after)
    return pl.pallas_call(
        functools.partial(filter_kernel, count),
        grid=(inputs // width,),
        in_specs=[
            pl.BlockSpec((2, held, width, length), lambda i: (0, place, i, 0)),
            pl.BlockSpec((2, following.shape[1], width, length), lambda i: (0, 0, i, 0)),
            pl.BlockSpec(fir_taps.shape, lambda i: (0, 0)),
            pl.BlockSpec(twiddles.shape, lambda i: (0, 0)),
        ]
        + [pl.BlockSpec(memory_space=pl.ANY)] * len(others),
        out_specs=[pl.BlockSpec((count, width, depth), lambda i: (place, i, 0))] * (2 * RADIX),
        out_shape=[out] * (2 * RADIX),
        input_output_aliases={4 + index: index for index in range(len(earlier))},
        compiler_params=params(),
        cost_estimate=pl.CostEstimate(
            flops=16 * voltage.size * count // frames,
            bytes_accessed=8 * voltage.size * count // frames,
            transcendentals=0,
        ),
        name="filter",
    )(voltage, following, fir_taps, twiddles, *others)


def dot_rows(left, right):
    return lax.dot_general(left, right, (((1,), (1,)), ((), ())), preferred_element_type=F32)


def transform_kernel(groups, pieces, table_ref, xh_ref, xl_ref, *refs):
    out_refs, (th_ref, tl_ref) = refs[-2 - len(groups) * pieces : -2], refs[-2:]
    height = table_ref.shape[1]
    masks = [mask for group in groups for mask in group]

    @pl.when(pl.program_id(0) == 0)
    def _():
        me = lax.axis_index("chan")
        for index, mask in enumerate(masks):
            rows = slice(index * height, (index + 1) * height)
            th_ref[rows], tl_ref[rows] = split(table_ref[me ^ mask])

    high = xh_ref[...]
    result = dot_rows(th_ref[...], high) + dot_rows(th_ref[...], xl_ref[...])
    result = result + dot_rows(tl_ref[...], high)
    count = height // 2
    size = count // pieces
    places = [(which, at) for which, group in enumerate(groups) for at in range(len(group))]
    for index, (which, at) in enumerate(places):
        for part in range(2):
            for piece in range(pieces):
                first = index * height + part * count + piece * size
                for column in range(result.shape[1] // BLOCK):
                    out_refs[which * pieces + piece][at, part, column] = result[
                        first : first + size, column * BLOCK : (column + 1) * BLOCK
                    ]


def transformed(groups, pieces, table, samples, after, first, last, work):
    depth = samples[0].shape[1]
    owners, height, _ = table.shape
    size = height // 2 // pieces
    step = STEP
    rows = (last - first) * step
    row_spec = pl.BlockSpec((step, depth), lambda i: (first + i, 0))
    total = sum(map(len, groups)) * height
    counts = [len(group) for group in groups for _ in range(pieces)]
    return pl.pallas_call(
        functools.partial(transform_kernel, groups, pieces),
        grid=(rows // step,),
        in_specs=[pl.BlockSpec(table.shape, lambda i: (0, 0, 0)), row_spec, row_spec]
        + [pl.BlockSpec(memory_space=pl.ANY)] * len(after),
        out_specs=[
            pl.BlockSpec((count, 2, step // BLOCK, size, BLOCK), lambda i: (0, 0, i, 0, 0))
            for count in counts
        ],
        out_shape=[
            jax.ShapeDtypeStruct((count, 2, rows // BLOCK, size, BLOCK), F32) for count in counts
        ],
        scratch_shapes=[pltpu.VMEM((total, depth), BF16)] * 2,
        compiler_params=params(),
        cost_estimate=pl.CostEstimate(
            flops=work or 3 * 2 * total * depth * rows,
            bytes_accessed=4 * depth * rows + 4 * table.size + 4 * total * rows,
            transcendentals=0,
        ),
        name="transform",
    )(table, *samples, *after)


def merge_kernel(count, groups, piece, *refs):
    near_refs, far_refs, out_refs = refs[: len(groups)], refs[len(groups) : 2 * len(groups)], refs[-count:]
    total = sum(groups)
    odd = lax.axis_index("chan") % 2 == 1
    lower = lax.broadcasted_iota(jnp.int32, (total, BLOCK), 1) < BLOCK // 2
    for unit, out_ref in enumerate(out_refs):
        for channel in range(piece):
            for part in range(2):

                def rows_of(segment_refs):
                    rows = [
                        ref[pl.ds((unit * 2 + part) * held * piece + channel, held, stride=piece), :]
                        for ref, held in zip(segment_refs, groups)
                    ]
                    return rows[0] if len(rows) == 1 else jnp.concatenate(rows, axis=0)

                near, far = rows_of(near_refs), rows_of(far_refs)
                first = jnp.where(odd, far, near)
                second = jnp.where(odd, near, far)
                at = part * 2 * total
                out_ref[channel, at : at + total] = jnp.where(
                    lower, first, pltpu.roll(second, BLOCK // 2, 1)
                )
                out_ref[channel, at + total : at + 2 * total] = jnp.where(
                    lower, pltpu.roll(first, BLOCK // 2, 1), second
                )


def merged(near, far, after):
    count, _, _, piece, lanes = near[0].shape
    groups = [value.shape[2] for value in near]
    size = sum(value.size for value in near)
    return pl.pallas_call(
        functools.partial(merge_kernel, count, groups, piece),
        in_specs=[pl.BlockSpec(memory_space=pltpu.VMEM)] * (2 * len(near))
        + [pl.BlockSpec(memory_space=pl.ANY)] * len(after),
        out_specs=[pl.BlockSpec(memory_space=pltpu.VMEM)] * count,
        out_shape=[jax.ShapeDtypeStruct((piece, 4 * sum(groups), lanes), F32)] * count,
        compiler_params=params(),
        cost_estimate=pl.CostEstimate(flops=4 * size, bytes_accessed=16 * size, transcendentals=0),
        name="merge",
    )(*[value.reshape(-1, lanes) for value in list(near) + list(far)], *after)


def pack_kernel(counts, *refs):
    sources = iter(refs)
    for count, out_ref in zip(counts, refs[-len(counts) :]):
        for index in range(count):
            out_ref[index] = next(sources)[...]


def packed(batches, after, work=0):
    counts = [len(batch) for batch in batches]
    values = [value for batch in batches for value in batch]
    width = 8

    def spec(shape):
        lead = shape[:-3]
        return pl.BlockSpec(
            lead + (min(width, shape[-3]),) + shape[-2:], lambda i: (0,) * len(lead) + (i, 0, 0)
        )

    shapes = [(len(batch),) + batch[0].shape for batch in batches]
    return pl.pallas_call(
        functools.partial(pack_kernel, counts),
        grid=(values[0].shape[-3] // min(width, values[0].shape[-3]),),
        in_specs=[spec(value.shape) for value in values]
        + [pl.BlockSpec(memory_space=pl.ANY)] * len(after),
        out_specs=[spec(shape) for shape in shapes],
        out_shape=[jax.ShapeDtypeStruct(shape, F32) for shape in shapes],
        compiler_params=params(),
        cost_estimate=pl.CostEstimate(
            flops=work,
            bytes_accessed=8 * sum(value.size for value in values),
            transcendentals=0,
        ),
        name="pack",
    )(*values, *after)


def dot_columns(left, right):
    return lax.dot_general(left, right, (((0,), (0,)), ((), ())), preferred_element_type=F32)


def correlate_kernel(slots, tiles, order, slot_ref, blocks_ref, *refs):
    unit_refs = []
    for ref in refs[:-5]:
        if len(ref.shape) == 4:
            unit_refs.append(ref)
        elif len(ref.shape) == 5 and len(unit_refs) < tiles:
            unit_refs += [ref.at[0], ref.at[1]]
    out_ref, done_ref, high_ref, low_ref, place_ref = refs[-5:]
    done_ref[...] = jnp.zeros(done_ref.shape, F32)
    blocks, width, depth, _ = unit_refs[0].shape
    rows = depth // 2
    half = tiles * rows

    @pl.when(pl.program_id(0) == 0)
    def _():
        first_slot = lax.axis_index("tile") * slots
        for slot in range(slots):
            row = jnp.int32(0)
            col = jnp.int32(0)
            present = jnp.int32(0)
            for tile in range(slot_ref.shape[0]):
                match = (slot_ref[tile] == first_slot + slot).astype(jnp.int32)
                row = row + match * blocks_ref[2 * tile]
                col = col + match * blocks_ref[2 * tile + 1]
                present = present + match
            place_ref[3 * slot] = row
            place_ref[3 * slot + 1] = col
            place_ref[3 * slot + 2] = present

    own = lax.axis_index("chan") // 2
    for channel in range(width):
        for mask in range(blocks):
            block = own ^ order[mask]
            for part in range(2):
                joined = jnp.concatenate(
                    [
                        unit_ref[mask, channel, part * rows : (part + 1) * rows]
                        for unit_ref in unit_refs
                    ],
                    axis=0,
                )
                high, low = split(joined)
                high_ref[channel, block, part * half : (part + 1) * half] = high
                low_ref[channel, block, part * half : (part + 1) * half] = low
        for slot in range(slots):
            row = place_ref[3 * slot]
            col = place_ref[3 * slot + 1]
            weight = place_ref[3 * slot + 2].astype(F32)
            row_high = high_ref[channel, row]
            row_low = low_ref[channel, row]
            col_high = high_ref[channel, col]
            col_low = low_ref[channel, col]
            turned_high = jnp.concatenate([-col_high[half:], col_high[:half]], axis=0)
            turned_low = jnp.concatenate([-col_low[half:], col_low[:half]], axis=0)
            right_high = jnp.concatenate([col_high, turned_high], axis=1)
            right_low = jnp.concatenate([col_low, turned_low], axis=1)
            value = dot_columns(
                jnp.concatenate([row_high, row_low], axis=0),
                jnp.concatenate([right_high, right_high], axis=0),
            ) + dot_columns(row_high, right_low)
            value = value * weight
            out_ref[slot, channel, 0] = value[:, :BLOCK]
            out_ref[slot, channel, 1] = value[:, BLOCK:]


def correlated(order, tile_slot, tile_blocks, units, visibility, residue, first, total, slots):
    tiles = sum(1 if unit.ndim == 4 else unit.shape[0] for unit in units)
    blocks, piece, depth, lanes = units[0].shape
    width = 4
    out = jax.ShapeDtypeStruct((slots, total, RADIX, 2, BLOCK, BLOCK), F32)
    operands = [tile_slot, tile_blocks.reshape(-1)] + units
    in_specs = [
        pl.BlockSpec((blocks, width, depth, lanes), lambda i, *_: (0, i, 0, 0))
        if unit.ndim == 4
        else pl.BlockSpec(unit.shape[:2] + (width, depth, lanes), lambda i, *_: (0, 0, i, 0, 0))
        for unit in units
    ]
    aliases = {}
    if visibility is not None:
        operands.append(visibility)
        in_specs.append(pl.BlockSpec(memory_space=pl.ANY))
        aliases = {len(operands) - 1: 0}
    return pl.pallas_call(
        functools.partial(correlate_kernel, slots, tiles, order),
        grid_spec=pltpu.PrefetchScalarGridSpec(
            num_scalar_prefetch=2,
            grid=(piece // width,),
            in_specs=in_specs,
            out_specs=[
                pl.BlockSpec(
                    (slots, width, None, 2, BLOCK, BLOCK), lambda i, *_: (0, first // width + i, residue, 0, 0, 0)
                ),
                pl.BlockSpec((8, BLOCK), lambda i, *_: (0, 0)),
            ],
            scratch_shapes=[pltpu.VMEM((width, blocks, tiles * depth, lanes), BF16)] * 2
            + [pltpu.SMEM((3 * slots,), jnp.int32)],
        ),
        out_shape=[out, jax.ShapeDtypeStruct((8, BLOCK), F32)],
        input_output_aliases=aliases,
        compiler_params=params(),
        cost_estimate=pl.CostEstimate(
            flops=3 * 2 * slots * piece * tiles * depth * BLOCK * 2 * BLOCK,
            bytes_accessed=4 * piece * lanes * (tiles * blocks * depth + slots * 2 * BLOCK),
            transcendentals=0,
        ),
        name="correlate",
    )(*operands)


def body(voltage, fir_taps, tile_slot, tile_blocks):
    _, frames, inputs, length = voltage.shape
    tap_count = fir_taps.shape[0]
    owners = lax.axis_size("chan")
    tiles = lax.axis_size("tile")
    channels = length // owners
    blocks = owners // 2
    slots = -(-tile_blocks.shape[0] // tiles)
    scale = 1.0 / math.sqrt(length * frames * tiles)
    table = jnp.asarray(fourier_table(length // RADIX, owners, scale))

    order = list(range(2, blocks)) + [1, 0]
    groups = [tuple(2 * block + x for block in order) for x in range(2)]
    halves = 2
    size = channels // RADIX // halves
    count = RADIX * halves
    near = [[] for _ in range(count)]
    share = [[] for _ in range(count)]
    away = [None] * count
    units = [None] * count
    paired = [None] * count

    steps = frames * inputs // STEP
    late = STEP // inputs
    following = shifted(voltage[:, : tap_count - 1], "tile", -1)
    early = filtered_samples(voltage, voltage[:, : tap_count - 1], fir_taps, late, [], [])

    def spectra(samples, residue, after, first, last, work=0):
        rows = [value.reshape(frames * inputs, -1) for value in samples[2 * residue : 2 * residue + 2]]
        values = transformed(groups, halves, table, rows, after, first, last, work)
        for half in range(halves):
            near[residue * halves + half].append(values[half])
            share[residue * halves + half].append(values[halves + half])

    spectra(early, 0, [], 0, steps - 1)
    samples = filtered_samples(voltage, following, fir_taps, late, early, [near[0][0]])
    spectra(samples, 0, [], steps - 1, steps)
    spectra(samples, 1, [], 0, steps)

    def leave(piece):
        values = share[piece]
        if 0 < piece < 5:
            after = [away[piece - 1][-1]]
            values = [packed([[value]], after)[0].reshape(value.shape) for value in values]
        away[piece] = [swapped(value, "chan", 1) for value in values]

    def merge(piece, after):
        units[piece] = merged(near[piece], away[piece], after)

    def along(piece):
        return [
            swapped(unit, "chan", 2 * block) if block else unit
            for block, unit in zip(order, units[piece])
        ]

    leave(0)
    merge(0, near[halves][:1])
    turned = along(0)
    for residue in range(2, RADIX):
        spectra(samples, residue, units[0][:1], 0, steps, LONG)
    leave(1)
    merge(1, [])
    leave(2)

    def products(piece, arrays, visibility):
        return correlated(
            order, tile_slot, tile_blocks, arrays, visibility,
            piece // halves, piece % halves * size, channels // RADIX, slots,
        )

    visibility = None
    finished = []
    pair = None
    for piece in range(count):
        if piece:
            after = [pair[1]]
            for later in range(piece + 1, min(piece + 3, count)):
                if units[later] is None:
                    merge(later, [])
                after.append(units[later][0])
        else:
            after = [units[1][0], away[2][0]] + [near[residue * halves][0] for residue in range(2, RADIX)]
        after += finished[piece - 2 : piece - 1] if piece >= 2 else []
        (own,) = packed([turned], after, LONG)
        if piece + 1 < count:
            turned = along(piece + 1)
        across = swapped(own, "tile", 2)
        if piece + 3 < count:
            leave(piece + 3)
        if pair:
            (both,) = packed([pair], [own] + (away[piece + 3][-1:] if piece + 3 < count else []))
            paired[piece - 1] = swapped(both, "tile", 1)
            visibility, token = products(piece - 1, pair + [paired[piece - 1]], visibility)
            finished.append(token)
        pair = [own, across]
    (last,) = packed([[across]], finished[-1:])
    arrays = pair + [swapped(own, "tile", 1), swapped(last[0], "tile", 1)]
    visibility, _ = products(count - 1, arrays, visibility)
    return visibility.reshape(slots, channels, 2, BLOCK, BLOCK)


def solution(mesh):
    in_specs = (P(None, "tile", "chan", None), P(), P(), P())
    out_specs = P("tile", "chan", None, None, None)
    owners, tiles = mesh.shape["chan"], mesh.shape["tile"]

    def run(voltage, fir_taps, tile_slot, tile_blocks):
        paired = 2 * voltage.shape[2] == BLOCK * owners and tiles == 4
        chosen = body if paired else generic_body
        return jax.shard_map(
            chosen, mesh=mesh, in_specs=in_specs, out_specs=out_specs, check_vma=False
        )(voltage, fir_taps, tile_slot, tile_blocks)

    return run
```

```python
import functools
import math

import jax
import jax.numpy as jnp
import numpy as np
from jax import lax
from jax.experimental import pallas as pl
from jax.experimental.pallas import tpu as pltpu
from jax.sharding import PartitionSpec as P

BLOCK = 128
RADIX = 4
STEP = 256
LONG = 2_000_000_000_000
VMEM_BYTES = 14 * 1024 * 1024
BF16 = jnp.bfloat16
F32 = jnp.float32


def shifted(value, axis, steps):
    count = lax.axis_size(axis)
    initial, last = (max(0, -steps), min(count, count - steps))
    return lax.ppermute(value, axis, [(source, source + steps) for source in range(initial, last)])


def swapped(value, axis, mask):
    count = lax.axis_size(axis)
    return lax.ppermute(value, axis, [(source, source ^ mask) for source in range(count)])


def params():
    return pltpu.CompilerParams(vmem_limit_bytes=VMEM_BYTES)


def split(value):
    high = value.astype(BF16)
    return high, (value - high.astype(F32)).astype(BF16)


def filter_frames(voltage, fir_taps):
    tap_count = fir_taps.shape[0]
    frames = voltage.shape[1]
    history = shifted(voltage[:, : tap_count - 1], "tile", -1)
    extended = jnp.concatenate([voltage, history], axis=1)
    filtered = jnp.zeros(voltage.shape, jnp.float32)
    for tap_index in range(tap_count):
        filtered = (
            filtered
            + fir_taps[tap_index][None, None, None, :] * extended[:, tap_index : tap_index + frames]
        )
    return filtered


def transform(filtered):
    channel_count = filtered.shape[3]
    row_count = filtered.shape[1] * filtered.shape[2]
    position = lax.broadcasted_iota(jnp.int32, (channel_count, channel_count), 0)
    frequency = lax.broadcasted_iota(jnp.int32, (channel_count, channel_count), 1)
    phase_angle = (position * frequency % channel_count).astype(jnp.float32) * (
        2.0 * math.pi / channel_count
    )
    factor = 1.0 / math.sqrt(channel_count)
    cosine = jnp.cos(phase_angle) * factor
    sine_table = jnp.sin(phase_angle) * factor
    samples = filtered.reshape(2 * row_count, channel_count)
    cos_part = jnp.dot(
        cosine, samples.T, precision=lax.Precision.HIGHEST, preferred_element_type=jnp.float32
    )
    sin_part = jnp.dot(
        sine_table, samples.T, precision=lax.Precision.HIGHEST, preferred_element_type=jnp.float32
    )
    real_part = cos_part[:, :row_count] + sin_part[:, row_count:]
    imag_part = cos_part[:, row_count:] - sin_part[:, :row_count]
    joined = jnp.concatenate([real_part, imag_part], axis=1)
    return joined.reshape(channel_count, 2, filtered.shape[1], filtered.shape[2])


def tile_product(gathered, row_block, col_block, block_width):
    left_block = lax.dynamic_slice_in_dim(gathered, row_block * block_width, block_width, 3)
    right_block = lax.dynamic_slice_in_dim(gathered, col_block * block_width, block_width, 3)
    channel_count = gathered.shape[0]
    depth = 2 * gathered.shape[2]
    left_real = left_block.reshape(channel_count, depth, block_width)
    left_imag = jnp.concatenate([left_block[:, 1], -left_block[:, 0]], axis=1)
    left_both = jnp.concatenate([left_real, left_imag], axis=2)
    right_both = right_block.reshape(channel_count, depth, block_width)
    return jnp.einsum(
        "cki,ckj->cij",
        left_both,
        right_both,
        precision=lax.Precision.HIGHEST,
        preferred_element_type=jnp.float32,
    )


def own_slots(tile_slot, tile_blocks, slot_count):
    first_slot = lax.axis_index("tile") * slot_count
    row_blocks = []
    col_blocks = []
    present = []
    for slot_index in range(slot_count):
        matches = (tile_slot == first_slot + slot_index).astype(jnp.int32)
        row_blocks.append(jnp.sum(matches * tile_blocks[:, 0]))
        col_blocks.append(jnp.sum(matches * tile_blocks[:, 1]))
        present.append(jnp.sum(matches))
    return row_blocks, col_blocks, present


def generic_body(voltage, fir_taps, tile_slot, tile_blocks):
    spectra = transform(filter_frames(voltage, fir_taps))
    tile_count = tile_blocks.shape[0]
    tile_size = lax.axis_size("tile")
    slot_count = (tile_count + tile_size - 1) // tile_size
    turned = lax.all_to_all(spectra, "chan", split_axis=0, concat_axis=3, tiled=True)
    spectra_total = turned.shape[2] * tile_size
    row_blocks, col_blocks, present = own_slots(tile_slot, tile_blocks, slot_count)
    portion = lax.all_gather(turned, "tile", axis=2, tiled=True)
    summed = jnp.stack(
        [
            tile_product(portion, row_blocks[slot_index], col_blocks[slot_index], BLOCK)
            for slot_index in range(slot_count)
        ]
    )
    weights = jnp.stack(present).astype(F32)[:, None, None, None] / spectra_total
    return (summed * weights).reshape(slot_count, turned.shape[0], 2, BLOCK, BLOCK)


def fourier_table(points, owners, scale):
    phase = np.outer(np.arange(points), np.arange(points)) % points
    angle = phase * (2.0 * math.pi / points)
    cosine = np.cos(angle) * scale
    sine = np.sin(angle) * scale
    both = np.stack([np.concatenate([cosine, sine], 1), np.concatenate([-sine, cosine], 1)], 0)
    both = both.reshape(2, owners, points // owners, 2 * points).transpose(1, 0, 2, 3)
    return both.reshape(owners, -1, 2 * points).astype(np.float32)


def twiddle_table(length):
    angle = np.outer(np.arange(1, RADIX), np.arange(length // RADIX)) * (2.0 * math.pi / length)
    return np.stack([np.cos(angle), np.sin(angle)], 1).reshape(-1, length // RADIX).astype(np.float32)


def filter_kernel(frames, voltage_ref, next_ref, taps_ref, twiddle_ref, *refs):
    out_refs = refs[-2 * RADIX :]
    tap_count, length = taps_ref.shape
    held = voltage_ref.shape[1]
    points = length // RADIX

    def quarter(part, frame, index):
        lanes = slice(index * points, (index + 1) * points)
        total = None
        for tap in range(tap_count):
            at = frame + tap
            source = voltage_ref[part, at, :, lanes] if at < held else next_ref[part, at - held, :, lanes]
            term = source * taps_ref[pl.ds(tap, 1), lanes]
            total = term if total is None else total + term
        return total

    for frame in range(frames):
        real = [quarter(0, frame, index) for index in range(RADIX)]
        imag = [quarter(1, frame, index) for index in range(RADIX)]
        even_real, odd_real = real[0] + real[2], real[1] + real[3]
        even_imag, odd_imag = imag[0] + imag[2], imag[1] + imag[3]
        left_real, right_real = real[0] - real[2], real[1] - real[3]
        left_imag, right_imag = imag[0] - imag[2], imag[1] - imag[3]
        residues = [
            (even_real + odd_real, even_imag + odd_imag),
            (left_real + right_imag, left_imag - right_real),
            (even_real - odd_real, even_imag - odd_imag),
            (left_real - right_imag, left_imag + right_real),
        ]
        for index, (re, im) in enumerate(residues):
            if index:
                cosine = twiddle_ref[pl.ds(2 * index - 2, 1), :]
                sine = twiddle_ref[pl.ds(2 * index - 1, 1), :]
                re, im = re * cosine + im * sine, im * cosine - re * sine
            for part, value in enumerate((re, im)):
                high, low = split(value)
                lanes = slice(part * points, (part + 1) * points)
                out_refs[2 * index][frame, :, lanes] = high
                out_refs[2 * index + 1][frame, :, lanes] = low


def filtered_samples(voltage, following, fir_taps, late, earlier, after):
    _, frames, inputs, length = voltage.shape
    width = 16
    depth = 2 * length // RADIX
    twiddles = jnp.asarray(twiddle_table(length))
    out = jax.ShapeDtypeStruct((frames, inputs, depth), BF16)
    if earlier:
        count, held, place = late, late, frames // late - 1
    else:
        count, held, place = frames - late, frames, 0
    others = list(earlier) + list(after)
    return pl.pallas_call(
        functools.partial(filter_kernel, count),
        grid=(inputs // width,),
        in_specs=[
            pl.BlockSpec((2, held, width, length), lambda i: (0, place, i, 0)),
            pl.BlockSpec((2, following.shape[1], width, length), lambda i: (0, 0, i, 0)),
            pl.BlockSpec(fir_taps.shape, lambda i: (0, 0)),
            pl.BlockSpec(twiddles.shape, lambda i: (0, 0)),
        ]
        + [pl.BlockSpec(memory_space=pl.ANY)] * len(others),
        out_specs=[pl.BlockSpec((count, width, depth), lambda i: (place, i, 0))] * (2 * RADIX),
        out_shape=[out] * (2 * RADIX),
        input_output_aliases={4 + index: index for index in range(len(earlier))},
        compiler_params=params(),
        cost_estimate=pl.CostEstimate(
            flops=16 * voltage.size * count // frames,
            bytes_accessed=8 * voltage.size * count // frames,
            transcendentals=0,
        ),
        name="filter",
    )(voltage, following, fir_taps, twiddles, *others)


def dot_rows(left, right):
    return lax.dot_general(left, right, (((1,), (1,)), ((), ())), preferred_element_type=F32)


def transform_kernel(groups, pieces, table_ref, xh_ref, xl_ref, *refs):
    out_refs, (th_ref, tl_ref) = refs[-2 - len(groups) * pieces : -2], refs[-2:]
    height = table_ref.shape[1]
    masks = [mask for group in groups for mask in group]

    @pl.when(pl.program_id(0) == 0)
    def _():
        me = lax.axis_index("chan")
        for index, mask in enumerate(masks):
            rows = slice(index * height, (index + 1) * height)
            th_ref[rows], tl_ref[rows] = split(table_ref[me ^ mask])

    high = xh_ref[...]
    result = dot_rows(th_ref[...], high) + dot_rows(th_ref[...], xl_ref[...])
    result = result + dot_rows(tl_ref[...], high)
    count = height // 2
    size = count // pieces
    places = [(which, at) for which, group in enumerate(groups) for at in range(len(group))]
    for index, (which, at) in enumerate(places):
        for part in range(2):
            for piece in range(pieces):
                first = index * height + part * count + piece * size
                for column in range(result.shape[1] // BLOCK):
                    out_refs[which * pieces + piece][at, part, column] = result[
                        first : first + size, column * BLOCK : (column + 1) * BLOCK
                    ]


def transformed(groups, pieces, table, samples, after, first, last, work):
    depth = samples[0].shape[1]
    owners, height, _ = table.shape
    size = height // 2 // pieces
    step = STEP
    rows = (last - first) * step
    row_spec = pl.BlockSpec((step, depth), lambda i: (first + i, 0))
    total = sum(map(len, groups)) * height
    counts = [len(group) for group in groups for _ in range(pieces)]
    return pl.pallas_call(
        functools.partial(transform_kernel, groups, pieces),
        grid=(rows // step,),
        in_specs=[pl.BlockSpec(table.shape, lambda i: (0, 0, 0)), row_spec, row_spec]
        + [pl.BlockSpec(memory_space=pl.ANY)] * len(after),
        out_specs=[
            pl.BlockSpec((count, 2, step // BLOCK, size, BLOCK), lambda i: (0, 0, i, 0, 0))
            for count in counts
        ],
        out_shape=[
            jax.ShapeDtypeStruct((count, 2, rows // BLOCK, size, BLOCK), F32) for count in counts
        ],
        scratch_shapes=[pltpu.VMEM((total, depth), BF16)] * 2,
        compiler_params=params(),
        cost_estimate=pl.CostEstimate(
            flops=work or 3 * 2 * total * depth * rows,
            bytes_accessed=4 * depth * rows + 4 * table.size + 4 * total * rows,
            transcendentals=0,
        ),
        name="transform",
    )(table, *samples, *after)


def merge_kernel(count, groups, piece, *refs):
    near_refs, far_refs, out_refs = refs[: len(groups)], refs[len(groups) : 2 * len(groups)], refs[-count:]
    total = sum(groups)
    odd = lax.axis_index("chan") % 2 == 1
    lower = lax.broadcasted_iota(jnp.int32, (total, BLOCK), 1) < BLOCK // 2
    for unit, out_ref in enumerate(out_refs):
        for channel in range(piece):
            for part in range(2):

                def rows_of(segment_refs):
                    rows = [
                        ref[pl.ds((unit * 2 + part) * held * piece + channel, held, stride=piece), :]
                        for ref, held in zip(segment_refs, groups)
                    ]
                    return rows[0] if len(rows) == 1 else jnp.concatenate(rows, axis=0)

                near, far = rows_of(near_refs), rows_of(far_refs)
                first = jnp.where(odd, far, near)
                second = jnp.where(odd, near, far)
                at = part * 2 * total
                out_ref[channel, at : at + total] = jnp.where(
                    lower, first, pltpu.roll(second, BLOCK // 2, 1)
                )
                out_ref[channel, at + total : at + 2 * total] = jnp.where(
                    lower, pltpu.roll(first, BLOCK // 2, 1), second
                )


def merged(near, far, after):
    count, _, _, piece, lanes = near[0].shape
    groups = [value.shape[2] for value in near]
    size = sum(value.size for value in near)
    return pl.pallas_call(
        functools.partial(merge_kernel, count, groups, piece),
        in_specs=[pl.BlockSpec(memory_space=pltpu.VMEM)] * (2 * len(near))
        + [pl.BlockSpec(memory_space=pl.ANY)] * len(after),
        out_specs=[pl.BlockSpec(memory_space=pltpu.VMEM)] * count,
        out_shape=[jax.ShapeDtypeStruct((piece, 4 * sum(groups), lanes), F32)] * count,
        compiler_params=params(),
        cost_estimate=pl.CostEstimate(flops=4 * size, bytes_accessed=16 * size, transcendentals=0),
        name="merge",
    )(*[value.reshape(-1, lanes) for value in list(near) + list(far)], *after)


def pack_kernel(counts, *refs):
    sources = iter(refs)
    for count, out_ref in zip(counts, refs[-len(counts) :]):
        for index in range(count):
            out_ref[index] = next(sources)[...]


def packed(batches, after, work=0):
    counts = [len(batch) for batch in batches]
    values = [value for batch in batches for value in batch]
    width = 8

    def spec(shape):
        lead = shape[:-3]
        return pl.BlockSpec(
            lead + (min(width, shape[-3]),) + shape[-2:], lambda i: (0,) * len(lead) + (i, 0, 0)
        )

    shapes = [(len(batch),) + batch[0].shape for batch in batches]
    return pl.pallas_call(
        functools.partial(pack_kernel, counts),
        grid=(values[0].shape[-3] // min(width, values[0].shape[-3]),),
        in_specs=[spec(value.shape) for value in values]
        + [pl.BlockSpec(memory_space=pl.ANY)] * len(after),
        out_specs=[spec(shape) for shape in shapes],
        out_shape=[jax.ShapeDtypeStruct(shape, F32) for shape in shapes],
        compiler_params=params(),
        cost_estimate=pl.CostEstimate(
            flops=work,
            bytes_accessed=8 * sum(value.size for value in values),
            transcendentals=0,
        ),
        name="pack",
    )(*values, *after)


def dot_columns(left, right):
    return lax.dot_general(left, right, (((0,), (0,)), ((), ())), preferred_element_type=F32)


def correlate_kernel(slots, tiles, order, slot_ref, blocks_ref, *refs):
    unit_refs = []
    for ref in refs[:-5]:
        if len(ref.shape) == 4:
            unit_refs.append(ref)
        elif len(ref.shape) == 5:
            unit_refs += [ref.at[0], ref.at[1]]
    near_refs = unit_refs[tiles:]
    out_ref, done_ref, high_ref, low_ref, place_ref = refs[-5:]
    done_ref[...] = jnp.zeros(done_ref.shape, F32)
    far, width, depth, _ = unit_refs[0].shape
    blocks = far + 1
    rows = depth // 2
    half = tiles * rows

    @pl.when(pl.program_id(0) == 0)
    def _():
        first_slot = lax.axis_index("tile") * slots
        for slot in range(slots):
            row = jnp.int32(0)
            col = jnp.int32(0)
            present = jnp.int32(0)
            for tile in range(slot_ref.shape[0]):
                match = (slot_ref[tile] == first_slot + slot).astype(jnp.int32)
                row = row + match * blocks_ref[2 * tile]
                col = col + match * blocks_ref[2 * tile + 1]
                present = present + match
            place_ref[3 * slot] = row
            place_ref[3 * slot + 1] = col
            place_ref[3 * slot + 2] = present

    own = lax.axis_index("chan") // 2
    for channel in range(width):
        for mask in range(blocks):
            block = own ^ order[mask]
            for part in range(2):
                joined = jnp.concatenate(
                    [
                        (unit_refs[tile][mask, channel, part * rows : (part + 1) * rows])
                        if mask < far
                        else near_refs[tile][0, channel, part * rows : (part + 1) * rows]
                        for tile in range(tiles)
                    ],
                    axis=0,
                )
                high, low = split(joined)
                high_ref[channel, block, part * half : (part + 1) * half] = high
                low_ref[channel, block, part * half : (part + 1) * half] = low
        for slot in range(slots):
            row = place_ref[3 * slot]
            col = place_ref[3 * slot + 1]
            weight = place_ref[3 * slot + 2].astype(F32)
            row_high = high_ref[channel, row]
            row_low = low_ref[channel, row]
            col_high = high_ref[channel, col]
            col_low = low_ref[channel, col]
            turned_high = jnp.concatenate([-col_high[half:], col_high[:half]], axis=0)
            turned_low = jnp.concatenate([-col_low[half:], col_low[:half]], axis=0)
            right_high = jnp.concatenate([col_high, turned_high], axis=1)
            right_low = jnp.concatenate([col_low, turned_low], axis=1)
            value = dot_columns(
                jnp.concatenate([row_high, row_low], axis=0),
                jnp.concatenate([right_high, right_high], axis=0),
            ) + dot_columns(row_high, right_low)
            value = value * weight
            out_ref[slot, channel, 0] = value[:, :BLOCK]
            out_ref[slot, channel, 1] = value[:, BLOCK:]


def correlated(order, tile_slot, tile_blocks, units, before, visibility, residue, first, total, slots):
    tiles = sum(1 if unit.ndim == 4 else unit.shape[0] for unit in units)
    blocks = len(order)
    piece, depth, lanes = units[0].shape[-3:]
    width = 4
    out = jax.ShapeDtypeStruct((slots, total, RADIX, 2, BLOCK, BLOCK), F32)
    operands = [tile_slot, tile_blocks.reshape(-1)] + units + before

    def spec(unit, held, at):
        lead = unit.shape[:-4]
        return pl.BlockSpec(
            lead + (held, width, depth, lanes), lambda i, *_: (0,) * len(lead) + (at, i, 0, 0)
        )

    in_specs = [spec(unit, blocks - 1, 0) for unit in units]
    in_specs += [spec(unit, 1, unit.shape[-4] - 1) for unit in before]
    aliases = {}
    if visibility is not None:
        operands.append(visibility)
        in_specs.append(pl.BlockSpec(memory_space=pl.ANY))
        aliases = {len(operands) - 1: 0}
    return pl.pallas_call(
        functools.partial(correlate_kernel, slots, tiles, order),
        grid_spec=pltpu.PrefetchScalarGridSpec(
            num_scalar_prefetch=2,
            grid=(piece // width,),
            in_specs=in_specs,
            out_specs=[
                pl.BlockSpec(
                    (slots, width, None, 2, BLOCK, BLOCK), lambda i, *_: (0, first // width + i, residue, 0, 0, 0)
                ),
                pl.BlockSpec((8, BLOCK), lambda i, *_: (0, 0)),
            ],
            scratch_shapes=[pltpu.VMEM((width, blocks, tiles * depth, lanes), BF16)] * 2
            + [pltpu.SMEM((3 * slots,), jnp.int32)],
        ),
        out_shape=[out, jax.ShapeDtypeStruct((8, BLOCK), F32)],
        input_output_aliases=aliases,
        compiler_params=params(),
        cost_estimate=pl.CostEstimate(
            flops=3 * 2 * slots * piece * tiles * depth * BLOCK * 2 * BLOCK,
            bytes_accessed=4 * piece * lanes * (tiles * blocks * depth + slots * 2 * BLOCK),
            transcendentals=0,
        ),
        name="correlate",
    )(*operands)


def body(voltage, fir_taps, tile_slot, tile_blocks):
    _, frames, inputs, length = voltage.shape
    tap_count = fir_taps.shape[0]
    owners = lax.axis_size("chan")
    tiles = lax.axis_size("tile")
    channels = length // owners
    blocks = owners // 2
    slots = -(-tile_blocks.shape[0] // tiles)
    scale = 1.0 / math.sqrt(length * frames * tiles)
    table = jnp.asarray(fourier_table(length // RADIX, owners, scale))

    order = list(range(2, blocks)) + [1, 0]
    groups = [tuple(2 * block + x for block in order) for x in range(2)]
    halves = 2
    size = channels // RADIX // halves
    count = RADIX * halves
    near = [[] for _ in range(count)]
    share = [[] for _ in range(count)]
    away = [None] * count
    units = [None] * count
    paired = [None] * count

    steps = frames * inputs // STEP
    late = STEP // inputs
    following = shifted(voltage[:, : tap_count - 1], "tile", -1)
    early = filtered_samples(voltage, voltage[:, : tap_count - 1], fir_taps, late, [], [])

    def spectra(samples, residue, after, first, last, work=0):
        rows = [value.reshape(frames * inputs, -1) for value in samples[2 * residue : 2 * residue + 2]]
        values = transformed(groups, halves, table, rows, after, first, last, work)
        for half in range(halves):
            near[residue * halves + half].append(values[half])
            share[residue * halves + half].append(values[halves + half])

    spectra(early, 0, [], 0, steps - 1)
    samples = filtered_samples(voltage, following, fir_taps, late, early, [near[0][0]])
    spectra(samples, 0, [], steps - 1, steps)
    spectra(samples, 1, [], 0, steps)

    def leave(piece):
        values = share[piece]
        if 0 < piece < 5:
            after = [away[piece - 1][-1]]
            values = [packed([[value]], after)[0].reshape(value.shape) for value in values]
        away[piece] = [swapped(value, "chan", 1) for value in values]

    def merge(piece, after):
        units[piece] = merged(near[piece], away[piece], after)

    def along(piece):
        return [
            swapped(unit, "chan", 2 * block) if block else unit
            for block, unit in zip(order, units[piece])
        ]

    leave(0)
    merge(0, near[halves][:1])
    turned = along(0)
    for residue in range(2, RADIX):
        spectra(samples, residue, units[0][:1], 0, steps, LONG)
    leave(1)
    merge(1, [])
    leave(2)

    def products(piece, arrays, before, visibility):
        return correlated(
            order, tile_slot, tile_blocks, arrays, before, visibility,
            piece // halves, piece % halves * size, channels // RADIX, slots,
        )

    (seed,) = packed([list(units[0][-1:])], [])
    seed_across = swapped(seed, "tile", 2)
    (both,) = packed([[seed, seed_across]], [])
    before = [seed, seed_across, swapped(both, "tile", 1)]
    visibility = None
    finished = []
    pair = None
    for piece in range(count):
        if piece:
            after = [pair[1]]
            for later in range(piece + 1, min(piece + 3, count)):
                if units[later] is None:
                    merge(later, [])
                after.append(units[later][0])
        else:
            after = [units[1][0], away[2][0]] + [near[residue * halves][0] for residue in range(2, RADIX)]
            after += before[2:]
        after += finished[piece - 2 : piece - 1] if piece >= 2 else []
        following = list(units[piece + 1][-1:]) if piece + 1 < count else []
        (own,) = packed([turned[:-1] + following], after, LONG)
        if piece + 1 < count:
            turned = along(piece + 1)
        across = swapped(own, "tile", 2)
        if piece + 3 < count:
            leave(piece + 3)
        if pair:
            (both,) = packed([pair], [own] + (away[piece + 3][-1:] if piece + 3 < count else []))
            arrays = pair + [swapped(both, "tile", 1)]
            visibility, token = products(piece - 1, arrays, before, visibility)
            finished.append(token)
            before = arrays
        pair = [own, across]
    (last,) = packed([[across]], finished[-1:])
    arrays = pair + [swapped(own, "tile", 1), swapped(last[0], "tile", 1)]
    visibility, _ = products(count - 1, arrays, before, visibility)
    return visibility.reshape(slots, channels, 2, BLOCK, BLOCK)


def solution(mesh):
    in_specs = (P(None, "tile", "chan", None), P(), P(), P())
    out_specs = P("tile", "chan", None, None, None)
    owners, tiles = mesh.shape["chan"], mesh.shape["tile"]

    def run(voltage, fir_taps, tile_slot, tile_blocks):
        paired = 2 * voltage.shape[2] == BLOCK * owners and tiles == 4
        chosen = body if paired else generic_body
        return jax.shard_map(
            chosen, mesh=mesh, in_specs=in_specs, out_specs=out_specs, check_vma=False
        )(voltage, fir_taps, tile_slot, tile_blocks)

    return run
```

```python
import functools
import math

import jax
import jax.numpy as jnp
import numpy as np
from jax import lax
from jax.experimental import pallas as pl
from jax.experimental.pallas import tpu as pltpu
from jax.sharding import PartitionSpec as P

BLOCK = 128
RADIX = 4
STEP = 256
LONG = 2_000_000_000_000
VMEM_BYTES = 14 * 1024 * 1024
BF16 = jnp.bfloat16
F32 = jnp.float32


def shifted(value, axis, steps):
    count = lax.axis_size(axis)
    initial, last = (max(0, -steps), min(count, count - steps))
    return lax.ppermute(value, axis, [(source, source + steps) for source in range(initial, last)])


def swapped(value, axis, mask):
    count = lax.axis_size(axis)
    return lax.ppermute(value, axis, [(source, source ^ mask) for source in range(count)])


def params():
    return pltpu.CompilerParams(vmem_limit_bytes=VMEM_BYTES)


def split(value):
    high = value.astype(BF16)
    return high, (value - high.astype(F32)).astype(BF16)


def filter_frames(voltage, fir_taps):
    tap_count = fir_taps.shape[0]
    frames = voltage.shape[1]
    history = shifted(voltage[:, : tap_count - 1], "tile", -1)
    extended = jnp.concatenate([voltage, history], axis=1)
    filtered = jnp.zeros(voltage.shape, jnp.float32)
    for tap_index in range(tap_count):
        filtered = (
            filtered
            + fir_taps[tap_index][None, None, None, :] * extended[:, tap_index : tap_index + frames]
        )
    return filtered


def transform(filtered):
    channel_count = filtered.shape[3]
    row_count = filtered.shape[1] * filtered.shape[2]
    position = lax.broadcasted_iota(jnp.int32, (channel_count, channel_count), 0)
    frequency = lax.broadcasted_iota(jnp.int32, (channel_count, channel_count), 1)
    phase_angle = (position * frequency % channel_count).astype(jnp.float32) * (
        2.0 * math.pi / channel_count
    )
    factor = 1.0 / math.sqrt(channel_count)
    cosine = jnp.cos(phase_angle) * factor
    sine_table = jnp.sin(phase_angle) * factor
    samples = filtered.reshape(2 * row_count, channel_count)
    cos_part = jnp.dot(
        cosine, samples.T, precision=lax.Precision.HIGHEST, preferred_element_type=jnp.float32
    )
    sin_part = jnp.dot(
        sine_table, samples.T, precision=lax.Precision.HIGHEST, preferred_element_type=jnp.float32
    )
    real_part = cos_part[:, :row_count] + sin_part[:, row_count:]
    imag_part = cos_part[:, row_count:] - sin_part[:, :row_count]
    joined = jnp.concatenate([real_part, imag_part], axis=1)
    return joined.reshape(channel_count, 2, filtered.shape[1], filtered.shape[2])


def tile_product(gathered, row_block, col_block, block_width):
    left_block = lax.dynamic_slice_in_dim(gathered, row_block * block_width, block_width, 3)
    right_block = lax.dynamic_slice_in_dim(gathered, col_block * block_width, block_width, 3)
    channel_count = gathered.shape[0]
    depth = 2 * gathered.shape[2]
    left_real = left_block.reshape(channel_count, depth, block_width)
    left_imag = jnp.concatenate([left_block[:, 1], -left_block[:, 0]], axis=1)
    left_both = jnp.concatenate([left_real, left_imag], axis=2)
    right_both = right_block.reshape(channel_count, depth, block_width)
    return jnp.einsum(
        "cki,ckj->cij",
        left_both,
        right_both,
        precision=lax.Precision.HIGHEST,
        preferred_element_type=jnp.float32,
    )


def own_slots(tile_slot, tile_blocks, slot_count):
    first_slot = lax.axis_index("tile") * slot_count
    row_blocks = []
    col_blocks = []
    present = []
    for slot_index in range(slot_count):
        matches = (tile_slot == first_slot + slot_index).astype(jnp.int32)
        row_blocks.append(jnp.sum(matches * tile_blocks[:, 0]))
        col_blocks.append(jnp.sum(matches * tile_blocks[:, 1]))
        present.append(jnp.sum(matches))
    return row_blocks, col_blocks, present


def generic_body(voltage, fir_taps, tile_slot, tile_blocks):
    spectra = transform(filter_frames(voltage, fir_taps))
    tile_count = tile_blocks.shape[0]
    tile_size = lax.axis_size("tile")
    slot_count = (tile_count + tile_size - 1) // tile_size
    turned = lax.all_to_all(spectra, "chan", split_axis=0, concat_axis=3, tiled=True)
    spectra_total = turned.shape[2] * tile_size
    row_blocks, col_blocks, present = own_slots(tile_slot, tile_blocks, slot_count)
    portion = lax.all_gather(turned, "tile", axis=2, tiled=True)
    summed = jnp.stack(
        [
            tile_product(portion, row_blocks[slot_index], col_blocks[slot_index], BLOCK)
            for slot_index in range(slot_count)
        ]
    )
    weights = jnp.stack(present).astype(F32)[:, None, None, None] / spectra_total
    return (summed * weights).reshape(slot_count, turned.shape[0], 2, BLOCK, BLOCK)


def fourier_table(points, owners, scale):
    phase = np.outer(np.arange(points), np.arange(points)) % points
    angle = phase * (2.0 * math.pi / points)
    cosine = np.cos(angle) * scale
    sine = np.sin(angle) * scale
    both = np.stack([np.concatenate([cosine, sine], 1), np.concatenate([-sine, cosine], 1)], 0)
    both = both.reshape(2, owners, points // owners, 2 * points).transpose(1, 0, 2, 3)
    return both.reshape(owners, -1, 2 * points).astype(np.float32)


def twiddle_table(length):
    angle = np.outer(np.arange(1, RADIX), np.arange(length // RADIX)) * (2.0 * math.pi / length)
    return np.stack([np.cos(angle), np.sin(angle)], 1).reshape(-1, length // RADIX).astype(np.float32)


def filter_kernel(frames, voltage_ref, next_ref, taps_ref, twiddle_ref, *refs):
    out_refs = refs[-2 * RADIX :]
    tap_count, length = taps_ref.shape
    held = voltage_ref.shape[1]
    points = length // RADIX

    def quarter(part, frame, index):
        lanes = slice(index * points, (index + 1) * points)
        total = None
        for tap in range(tap_count):
            at = frame + tap
            source = voltage_ref[part, at, :, lanes] if at < held else next_ref[part, at - held, :, lanes]
            term = source * taps_ref[pl.ds(tap, 1), lanes]
            total = term if total is None else total + term
        return total

    for frame in range(frames):
        real = [quarter(0, frame, index) for index in range(RADIX)]
        imag = [quarter(1, frame, index) for index in range(RADIX)]
        even_real, odd_real = real[0] + real[2], real[1] + real[3]
        even_imag, odd_imag = imag[0] + imag[2], imag[1] + imag[3]
        left_real, right_real = real[0] - real[2], real[1] - real[3]
        left_imag, right_imag = imag[0] - imag[2], imag[1] - imag[3]
        residues = [
            (even_real + odd_real, even_imag + odd_imag),
            (left_real + right_imag, left_imag - right_real),
            (even_real - odd_real, even_imag - odd_imag),
            (left_real - right_imag, left_imag + right_real),
        ]
        for index, (re, im) in enumerate(residues):
            if index:
                cosine = twiddle_ref[pl.ds(2 * index - 2, 1), :]
                sine = twiddle_ref[pl.ds(2 * index - 1, 1), :]
                re, im = re * cosine + im * sine, im * cosine - re * sine
            for part, value in enumerate((re, im)):
                high, low = split(value)
                lanes = slice(part * points, (part + 1) * points)
                out_refs[2 * index][frame, :, lanes] = high
                out_refs[2 * index + 1][frame, :, lanes] = low


def filtered_samples(voltage, following, fir_taps, late, earlier, after):
    _, frames, inputs, length = voltage.shape
    width = 16
    depth = 2 * length // RADIX
    twiddles = jnp.asarray(twiddle_table(length))
    out = jax.ShapeDtypeStruct((frames, inputs, depth), BF16)
    if earlier:
        count, held, place = late, late, frames // late - 1
    else:
        count, held, place = frames - late, frames, 0
    others = list(earlier) + list(after)
    return pl.pallas_call(
        functools.partial(filter_kernel, count),
        grid=(inputs // width,),
        in_specs=[
            pl.BlockSpec((2, held, width, length), lambda i: (0, place, i, 0)),
            pl.BlockSpec((2, following.shape[1], width, length), lambda i: (0, 0, i, 0)),
            pl.BlockSpec(fir_taps.shape, lambda i: (0, 0)),
            pl.BlockSpec(twiddles.shape, lambda i: (0, 0)),
        ]
        + [pl.BlockSpec(memory_space=pl.ANY)] * len(others),
        out_specs=[pl.BlockSpec((count, width, depth), lambda i: (place, i, 0))] * (2 * RADIX),
        out_shape=[out] * (2 * RADIX),
        input_output_aliases={4 + index: index for index in range(len(earlier))},
        compiler_params=params(),
        cost_estimate=pl.CostEstimate(
            flops=16 * voltage.size * count // frames,
            bytes_accessed=8 * voltage.size * count // frames,
            transcendentals=0,
        ),
        name="filter",
    )(voltage, following, fir_taps, twiddles, *others)


def dot_rows(left, right):
    return lax.dot_general(left, right, (((1,), (1,)), ((), ())), preferred_element_type=F32)


def transform_kernel(groups, pieces, table_ref, xh_ref, xl_ref, *refs):
    out_refs, (th_ref, tl_ref) = refs[-2 - len(groups) * pieces : -2], refs[-2:]
    height = table_ref.shape[1]
    masks = [mask for group in groups for mask in group]

    @pl.when(pl.program_id(0) == 0)
    def _():
        me = lax.axis_index("chan")
        for index, mask in enumerate(masks):
            rows = slice(index * height, (index + 1) * height)
            th_ref[rows], tl_ref[rows] = split(table_ref[me ^ mask])

    high = xh_ref[...]
    result = dot_rows(th_ref[...], high) + dot_rows(th_ref[...], xl_ref[...])
    result = result + dot_rows(tl_ref[...], high)
    count = height // 2
    size = count // pieces
    places = [(which, at) for which, group in enumerate(groups) for at in range(len(group))]
    for index, (which, at) in enumerate(places):
        for part in range(2):
            for piece in range(pieces):
                first = index * height + part * count + piece * size
                for column in range(result.shape[1] // BLOCK):
                    out_refs[which * pieces + piece][at, part, column] = result[
                        first : first + size, column * BLOCK : (column + 1) * BLOCK
                    ]


def transformed(groups, pieces, table, samples, after, first, last, work):
    depth = samples[0].shape[1]
    owners, height, _ = table.shape
    size = height // 2 // pieces
    step = STEP
    rows = (last - first) * step
    row_spec = pl.BlockSpec((step, depth), lambda i: (first + i, 0))
    total = sum(map(len, groups)) * height
    counts = [len(group) for group in groups for _ in range(pieces)]
    return pl.pallas_call(
        functools.partial(transform_kernel, groups, pieces),
        grid=(rows // step,),
        in_specs=[pl.BlockSpec(table.shape, lambda i: (0, 0, 0)), row_spec, row_spec]
        + [pl.BlockSpec(memory_space=pl.ANY)] * len(after),
        out_specs=[
            pl.BlockSpec((count, 2, step // BLOCK, size, BLOCK), lambda i: (0, 0, i, 0, 0))
            for count in counts
        ],
        out_shape=[
            jax.ShapeDtypeStruct((count, 2, rows // BLOCK, size, BLOCK), F32) for count in counts
        ],
        scratch_shapes=[pltpu.VMEM((total, depth), BF16)] * 2,
        compiler_params=params(),
        cost_estimate=pl.CostEstimate(
            flops=work or 3 * 2 * total * depth * rows,
            bytes_accessed=4 * depth * rows + 4 * table.size + 4 * total * rows,
            transcendentals=0,
        ),
        name="transform",
    )(table, *samples, *after)


def merge_kernel(count, groups, piece, *refs):
    near_refs, far_refs, out_refs = refs[: len(groups)], refs[len(groups) : 2 * len(groups)], refs[-count:]
    total = sum(groups)
    odd = lax.axis_index("chan") % 2 == 1
    lower = lax.broadcasted_iota(jnp.int32, (total, BLOCK), 1) < BLOCK // 2
    for unit, out_ref in enumerate(out_refs):
        for channel in range(piece):
            for part in range(2):

                def rows_of(segment_refs):
                    rows = [
                        ref[pl.ds((unit * 2 + part) * held * piece + channel, held, stride=piece), :]
                        for ref, held in zip(segment_refs, groups)
                    ]
                    return rows[0] if len(rows) == 1 else jnp.concatenate(rows, axis=0)

                near, far = rows_of(near_refs), rows_of(far_refs)
                first = jnp.where(odd, far, near)
                second = jnp.where(odd, near, far)
                at = part * 2 * total
                out_ref[channel, at : at + total] = jnp.where(
                    lower, first, pltpu.roll(second, BLOCK // 2, 1)
                )
                out_ref[channel, at + total : at + 2 * total] = jnp.where(
                    lower, pltpu.roll(first, BLOCK // 2, 1), second
                )


def merged(near, far, after):
    count, _, _, piece, lanes = near[0].shape
    groups = [value.shape[2] for value in near]
    size = sum(value.size for value in near)
    return pl.pallas_call(
        functools.partial(merge_kernel, count, groups, piece),
        in_specs=[pl.BlockSpec(memory_space=pltpu.VMEM)] * (2 * len(near))
        + [pl.BlockSpec(memory_space=pl.ANY)] * len(after),
        out_specs=[pl.BlockSpec(memory_space=pltpu.VMEM)] * count,
        out_shape=[jax.ShapeDtypeStruct((piece, 4 * sum(groups), lanes), F32)] * count,
        compiler_params=params(),
        cost_estimate=pl.CostEstimate(flops=4 * size, bytes_accessed=16 * size, transcendentals=0),
        name="merge",
    )(*[value.reshape(-1, lanes) for value in list(near) + list(far)], *after)


def pack_kernel(counts, *refs):
    sources = iter(refs)
    for count, out_ref in zip(counts, refs[-len(counts) :]):
        for index in range(count):
            out_ref[index] = next(sources)[...]


def packed(batches, after, work=0):
    counts = [len(batch) for batch in batches]
    values = [value for batch in batches for value in batch]
    width = 8

    def spec(shape):
        lead = shape[:-3]
        return pl.BlockSpec(
            lead + (min(width, shape[-3]),) + shape[-2:], lambda i: (0,) * len(lead) + (i, 0, 0)
        )

    shapes = [(len(batch),) + batch[0].shape for batch in batches]
    return pl.pallas_call(
        functools.partial(pack_kernel, counts),
        grid=(values[0].shape[-3] // min(width, values[0].shape[-3]),),
        in_specs=[spec(value.shape) for value in values]
        + [pl.BlockSpec(memory_space=pl.ANY)] * len(after),
        out_specs=[spec(shape) for shape in shapes],
        out_shape=[jax.ShapeDtypeStruct(shape, F32) for shape in shapes],
        compiler_params=params(),
        cost_estimate=pl.CostEstimate(
            flops=work,
            bytes_accessed=8 * sum(value.size for value in values),
            transcendentals=0,
        ),
        name="pack",
    )(*values, *after)


def dot_columns(left, right):
    return lax.dot_general(left, right, (((0,), (0,)), ((), ())), preferred_element_type=F32)


def correlate_kernel(slots, tiles, order, slot_ref, blocks_ref, *refs):
    unit_refs = []
    for ref in refs[:-5]:
        if len(ref.shape) == 4:
            unit_refs.append(ref)
        elif len(ref.shape) == 5:
            unit_refs += [ref.at[0], ref.at[1]]
    near_refs = unit_refs[tiles:]
    out_ref, done_ref, high_ref, low_ref, place_ref = refs[-5:]
    done_ref[...] = jnp.zeros(done_ref.shape, F32)
    far, width, depth, _ = unit_refs[0].shape
    blocks = far + 1
    rows = depth // 2
    half = tiles * rows

    @pl.when(pl.program_id(0) == 0)
    def _():
        first_slot = lax.axis_index("tile") * slots
        for slot in range(slots):
            row = jnp.int32(0)
            col = jnp.int32(0)
            present = jnp.int32(0)
            for tile in range(slot_ref.shape[0]):
                match = (slot_ref[tile] == first_slot + slot).astype(jnp.int32)
                row = row + match * blocks_ref[2 * tile]
                col = col + match * blocks_ref[2 * tile + 1]
                present = present + match
            place_ref[3 * slot] = row
            place_ref[3 * slot + 1] = col
            place_ref[3 * slot + 2] = present

    own = lax.axis_index("chan") // 2
    for channel in range(width):
        for mask in range(blocks):
            block = own ^ order[mask]
            for part in range(2):
                joined = jnp.concatenate(
                    [
                        (unit_refs[tile][mask, channel, part * rows : (part + 1) * rows])
                        if mask < far
                        else near_refs[tile][0, channel, part * rows : (part + 1) * rows]
                        for tile in range(tiles)
                    ],
                    axis=0,
                )
                high, low = split(joined)
                high_ref[channel, block, part * half : (part + 1) * half] = high
                low_ref[channel, block, part * half : (part + 1) * half] = low
        for slot in range(slots):
            row = place_ref[3 * slot]
            col = place_ref[3 * slot + 1]
            weight = place_ref[3 * slot + 2].astype(F32)
            row_high = high_ref[channel, row]
            row_low = low_ref[channel, row]
            col_high = high_ref[channel, col]
            col_low = low_ref[channel, col]
            turned_high = jnp.concatenate([-col_high[half:], col_high[:half]], axis=0)
            turned_low = jnp.concatenate([-col_low[half:], col_low[:half]], axis=0)
            right_high = jnp.concatenate([col_high, turned_high], axis=1)
            right_low = jnp.concatenate([col_low, turned_low], axis=1)
            value = dot_columns(
                jnp.concatenate([row_high, row_low], axis=0),
                jnp.concatenate([right_high, right_high], axis=0),
            ) + dot_columns(row_high, right_low)
            value = value * weight
            out_ref[slot, channel, 0] = value[:, :BLOCK]
            out_ref[slot, channel, 1] = value[:, BLOCK:]


def correlated(order, tile_slot, tile_blocks, units, before, visibility, residue, first, total, slots, at):
    tiles = sum(1 if unit.ndim == 4 else unit.shape[0] for unit in units)
    blocks = len(order)
    piece, depth, lanes = units[0].shape[-3:]
    width = 4
    out = jax.ShapeDtypeStruct((slots, total, RADIX, 2, BLOCK, BLOCK), F32)
    operands = [tile_slot, tile_blocks.reshape(-1)] + units + before

    def spec(unit, held, at):
        lead = unit.shape[:-4]
        return pl.BlockSpec(
            lead + (held, width, depth, lanes), lambda i, *_: (0,) * len(lead) + (at, i, 0, 0)
        )

    in_specs = [spec(unit, blocks - 1, 0) for unit in units]
    in_specs += [spec(unit, 1, at % unit.shape[-4]) for unit in before]
    aliases = {}
    if visibility is not None:
        operands.append(visibility)
        in_specs.append(pl.BlockSpec(memory_space=pl.ANY))
        aliases = {len(operands) - 1: 0}
    return pl.pallas_call(
        functools.partial(correlate_kernel, slots, tiles, order),
        grid_spec=pltpu.PrefetchScalarGridSpec(
            num_scalar_prefetch=2,
            grid=(piece // width,),
            in_specs=in_specs,
            out_specs=[
                pl.BlockSpec(
                    (slots, width, None, 2, BLOCK, BLOCK), lambda i, *_: (0, first // width + i, residue, 0, 0, 0)
                ),
                pl.BlockSpec((8, BLOCK), lambda i, *_: (0, 0)),
            ],
            scratch_shapes=[pltpu.VMEM((width, blocks, tiles * depth, lanes), BF16)] * 2
            + [pltpu.SMEM((3 * slots,), jnp.int32)],
        ),
        out_shape=[out, jax.ShapeDtypeStruct((8, BLOCK), F32)],
        input_output_aliases=aliases,
        compiler_params=params(),
        cost_estimate=pl.CostEstimate(
            flops=3 * 2 * slots * piece * tiles * depth * BLOCK * 2 * BLOCK,
            bytes_accessed=4 * piece * lanes * (tiles * blocks * depth + slots * 2 * BLOCK),
            transcendentals=0,
        ),
        name="correlate",
    )(*operands)


def body(voltage, fir_taps, tile_slot, tile_blocks):
    _, frames, inputs, length = voltage.shape
    tap_count = fir_taps.shape[0]
    owners = lax.axis_size("chan")
    tiles = lax.axis_size("tile")
    channels = length // owners
    blocks = owners // 2
    slots = -(-tile_blocks.shape[0] // tiles)
    scale = 1.0 / math.sqrt(length * frames * tiles)
    table = jnp.asarray(fourier_table(length // RADIX, owners, scale))

    order = list(range(2, blocks)) + [1, 0]
    groups = [tuple(2 * block + x for block in order) for x in range(2)]
    halves = 2
    size = channels // RADIX // halves
    count = RADIX * halves
    near = [[] for _ in range(count)]
    share = [[] for _ in range(count)]
    away = [None] * count
    units = [None] * count
    paired = [None] * count

    steps = frames * inputs // STEP
    late = STEP // inputs
    following = shifted(voltage[:, : tap_count - 1], "tile", -1)
    early = filtered_samples(voltage, voltage[:, : tap_count - 1], fir_taps, late, [], [])

    def spectra(samples, residue, after, first, last, work=0):
        rows = [value.reshape(frames * inputs, -1) for value in samples[2 * residue : 2 * residue + 2]]
        values = transformed(groups, halves, table, rows, after, first, last, work)
        for half in range(halves):
            near[residue * halves + half].append(values[half])
            share[residue * halves + half].append(values[halves + half])

    spectra(early, 0, [], 0, steps - 1)
    samples = filtered_samples(voltage, following, fir_taps, late, early, [near[0][0]])
    spectra(samples, 0, [], steps - 1, steps)
    spectra(samples, 1, [], 0, steps)

    def leave(piece):
        values = share[piece]
        if 0 < piece < 5:
            after = [away[piece - 1][-1]]
            values = [packed([[value]], after)[0].reshape(value.shape) for value in values]
        away[piece] = [swapped(value, "chan", 1) for value in values]

    def merge(piece, after):
        units[piece] = merged(near[piece], away[piece], after)

    def along(piece):
        return [
            swapped(unit, "chan", 2 * block) if block else unit
            for block, unit in zip(order, units[piece])
        ]

    leave(0)
    merge(0, near[halves][:1])
    turned = along(0)
    for residue in range(2, RADIX):
        spectra(samples, residue, units[0][:1], 0, steps, LONG)
    leave(1)
    merge(1, [])
    leave(2)

    def products(piece, arrays, before, visibility):
        return correlated(
            order, tile_slot, tile_blocks, arrays, before, visibility,
            piece // halves, piece % halves * size, channels // RADIX, slots, blocks - 1 if piece == 0 else -1,
        )

    before = None
    visibility = None
    finished = []
    pair = None
    for piece in range(count):
        if piece:
            after = [pair[1]]
            for later in range(piece + 1, min(piece + 3, count)):
                if units[later] is None:
                    merge(later, [])
                after.append(units[later][0])
        else:
            after = [units[1][0], away[2][0]] + [near[residue * halves][0] for residue in range(2, RADIX)]
        after += finished[piece - 2 : piece - 1] if piece >= 2 else []
        following = list(units[piece + 1][-1:]) if piece + 1 < count else []
        (own,) = packed([turned[: None if piece == 0 else -1] + following], after, LONG)
        if piece + 1 < count:
            turned = along(piece + 1)
        across = swapped(own, "tile", 2)
        if piece + 3 < count:
            leave(piece + 3)
        if pair:
            (both,) = packed([pair], [own] + (away[piece + 3][-1:] if piece + 3 < count else []))
            arrays = pair + [swapped(both, "tile", 1)]
            visibility, token = products(piece - 1, arrays, before or arrays, visibility)
            finished.append(token)
            before = arrays
        pair = [own, across]
    (last,) = packed([[across]], finished[-1:])
    arrays = pair + [swapped(own, "tile", 1), swapped(last[0], "tile", 1)]
    visibility, _ = products(count - 1, arrays, before, visibility)
    return visibility.reshape(slots, channels, 2, BLOCK, BLOCK)


def solution(mesh):
    in_specs = (P(None, "tile", "chan", None), P(), P(), P())
    out_specs = P("tile", "chan", None, None, None)
    owners, tiles = mesh.shape["chan"], mesh.shape["tile"]

    def run(voltage, fir_taps, tile_slot, tile_blocks):
        paired = 2 * voltage.shape[2] == BLOCK * owners and tiles == 4
        chosen = body if paired else generic_body
        return jax.shard_map(
            chosen, mesh=mesh, in_specs=in_specs, out_specs=out_specs, check_vma=False
        )(voltage, fir_taps, tile_slot, tile_blocks)

    return run
```
